32 devices in a mesh: dp: 16 (over z, x, core), seq: 2 (over y).
Axes of the slice: x: 2, y: 2, z: 4, core: 2. Of those that a mesh axis runs over, the one named last changes fastest.
Arguments:
- inputs: bfloat16 [16, 258, 1152], P('dp', 'seq'), may hold values from -6 to 6
- skips: bfloat16 [16, 258, 1152], P('dp', None, 'seq'), may hold values from -6 to 6
- cotangent: bfloat16 [16, 258, 1152], P('dp', 'seq'), may hold values from -6 to 6
- bins: int32 [16], P('dp'), may hold values from 0 to 31
- bin_weights: float32 [32], replicated, may hold values from 0.3 to 3
- skip_w: bfloat16 [2304, 1152], P('dp'), may hold values from -0.125 to 0.125
- skip_b: bfloat16 [1152], P('dp'), may hold values from -1 to 1
- ln1_g: bfloat16 [1152], P('dp'), may hold values from 0.5 to 1.5
- ln1_b: bfloat16 [1152], P('dp'), may hold values from -1 to 1
- qkv_w: bfloat16 [1152, 3456], P('dp'), may hold values from -0.25 to 0.25
- proj_w: bfloat16 [1152, 1152], P('dp'), may hold values from -0.75 to 0.75
- proj_b: bfloat16 [1152], P('dp'), may hold values from -1 to 1
- ln2_g: bfloat16 [1152], P('dp'), may hold values from 0.5 to 1.5
- ln2_b: bfloat16 [1152], P('dp'), may hold values from -1 to 1
- fc1_w: bfloat16 [1152, 4608], P('dp'), may hold values from -0.1875 to 0.1875
- fc1_b: bfloat16 [4608], P('dp'), may hold values from -1 to 1
- fc2_w: bfloat16 [4608, 1152], P('dp'), may hold values from -0.125 to 0.125
- fc2_b: bfloat16 [1152], P('dp'), may hold values from -1 to 1
Outputs:
- output: bfloat16 [16, 258, 1152], P('dp', 'seq')
- d_inputs: bfloat16 [16, 258, 1152], P('dp', 'seq')
- d_skips: bfloat16 [16, 258, 1152], P('dp', None, 'seq')
- d_skip_w: float32 [2304, 1152], P('dp')
- d_skip_b: float32 [1152], P('dp')
- d_ln1_g: float32 [1152], P('dp')
- d_ln1_b: float32 [1152], P('dp')
- d_qkv_w: float32 [1152, 3456], P('dp')
- d_proj_w: float32 [1152, 1152], P('dp')
- d_proj_b: float32 [1152], P('dp')
- d_ln2_g: float32 [1152], P('dp')
- d_ln2_b: float32 [1152], P('dp')
- d_fc1_w: float32 [1152, 4608], P('dp')
- d_fc1_b: float32 [4608], P('dp')
- d_fc2_w: float32 [4608, 1152], P('dp')
- d_fc2_b: float32 [1152], P('dp')
The draws below stay inside these ranges and needn't reach their ends.
All inputs are finite; a program needn't handle non-finite values.
Results may differ from the reference program's by a relative error of at most 0.018.
Values may be sent and summed in bfloat16 or wider, within the bound.
No kernel may reach another device: no remote copies, remote signals or barrier semaphores. Data moves between devices by JAX's collectives and lax.ppermute only.
A program may use at most 256 MiB of HBM per device.

```python
import math
import jax
import jax.numpy as jnp
from jax import lax

D = 1152
HEADS = 16
HEAD_DIM = 72
FF = 4608
LEN = 258
BINS = 32
ITEMS = 16


def touch_ends(values, rng, low, top_value):
    index_at = [jax.random.randint(jax.random.fold_in(rng, axis), (), 0, length) for axis, length in enumerate(values.shape)]
    longest = values.shape.index(max(values.shape))
    beside = index_at[:longest] + [(index_at[longest] + 1) % values.shape[longest]] + index_at[longest + 1:]
    return values.at[tuple(index_at)].set(low).at[tuple(beside)].set(top_value)


def block_levels(rng, extent, cuts, low, top_value):
    def one(axis_at, blocks):
        draws = jax.random.uniform(jax.random.fold_in(jax.random.fold_in(rng, 6), axis_at), (blocks,), jnp.float32, low / len(cuts), top_value / len(cuts))
        return jnp.repeat(jnp.exp(draws), extent[axis_at] // blocks).reshape((-1,) + (1,) * (len(extent) - axis_at - 1))

    loudness = one(*cuts[0])
    for cut in cuts[1:]:
        loudness = loudness * one(*cut)
    return loudness


def bell_draw(own_key, dims, scale, most, cuts=(), kind=jnp.bfloat16):
    values = scale * jax.random.normal(own_key, dims, jnp.float32)
    if cuts:
        values = values * block_levels(own_key, dims, cuts, -0.22, 0.18)
    return jnp.clip(values, -most, most).astype(kind)


def setup_inputs(seed: int = 0) -> dict:
    streams_of = jax.random.split(jax.random.key(seed), 19)
    return {
        "inputs": bell_draw(streams_of[0], (ITEMS, LEN, D), 1.0, 6.0, ((0, 16), (1, 2))),
        "skips": bell_draw(streams_of[1], (ITEMS, LEN, D), 1.0, 6.0, ((0, 16), (2, 2))),
        "cotangent": bell_draw(streams_of[2], (ITEMS, LEN, D), 1.0, 6.0, ((0, 16), (1, 2))),
        "bins": touch_ends(jax.random.randint(streams_of[3], (ITEMS,), 0, BINS), jax.random.fold_in(streams_of[3], 1), 0, BINS - 1).astype(jnp.int32),
        "bin_weights": jnp.clip(jnp.exp(jax.random.uniform(streams_of[4], (BINS,), jnp.float32, math.log(0.3), math.log(3.0))), 0.3, 3.0),
        "skip_w": bell_draw(streams_of[5], (2 * D, D), (2 * D) ** -0.5, 0.125, ((0, 16),)),
        "skip_b": bell_draw(streams_of[6], (D,), 0.2, 1.0, ((0, 16),)),
        "ln1_g": jnp.clip(1.0 + 0.1 * jax.random.normal(streams_of[7], (D,), jnp.float32), 0.5, 1.5).astype(jnp.bfloat16),
        "ln1_b": bell_draw(streams_of[8], (D,), 0.2, 1.0, ((0, 16),)),
        "qkv_w": bell_draw(streams_of[9], (D, 3 * D), (D // 2) ** -0.5, 0.25, ((0, 16),)),
        "proj_w": bell_draw(streams_of[10], (D, D), (D // 16) ** -0.5, 0.75, ((0, 16),)),
        "proj_b": bell_draw(streams_of[11], (D,), 0.2, 1.0, ((0, 16),)),
        "ln2_g": jnp.clip(1.0 + 0.1 * jax.random.normal(streams_of[12], (D,), jnp.float32), 0.5, 1.5).astype(jnp.bfloat16),
        "ln2_b": bell_draw(streams_of[13], (D,), 0.2, 1.0, ((0, 16),)),
        "fc1_w": bell_draw(streams_of[14], (D, FF), D ** -0.5, 0.1875, ((0, 16),)),
        "fc1_b": bell_draw(streams_of[15], (FF,), 0.2, 1.0, ((0, 16),)),
        "fc2_w": bell_draw(streams_of[16], (FF, D), (FF // 2) ** -0.5, 0.125, ((0, 16),)),
        "fc2_b": bell_draw(streams_of[17], (D,), 0.2, 1.0, ((0, 16),)),
    }


@jax.custom_vjp
def low(v):
    return lax.optimization_barrier(v.astype(jnp.bfloat16)).astype(jnp.float32)

@jax.custom_vjp
def low_back(v):
    return v

def low_keep(v):
    return (low(v), None)

def low_pass(kept, grad):
    return (grad,)

def back_keep(v):
    return (v, None)

def back_low(kept, grad):
    return (low(grad),)
low.defvjp(low_keep, low_pass)
low_back.defvjp(back_keep, back_low)

def hi_dot(left, right):
    return jnp.dot(left, right, precision=lax.Precision.HIGHEST)

def layer_norm(values, gain, shift):
    center = values - lax.optimization_barrier(jnp.mean(values, axis=-1, keepdims=True))
    spread = lax.optimization_barrier(jnp.mean(center * center, axis=-1, keepdims=True))
    return center * lax.rsqrt(spread + 1e-05) * gain + shift

def forward(params, inputs, skips):
    skip_w, skip_b, ln1_g, ln1_b, qkv_w, proj_w, proj_b, ln2_g, ln2_b, fc1_w, fc1_b, fc2_w, fc2_b = params
    group, length, width = inputs.shape
    rows = jnp.concatenate((inputs, skips), axis=2).reshape(group * length, 2 * width)
    hidden = low_back(hi_dot(rows, skip_w) + skip_b)
    normed = low(layer_norm(hidden, ln1_g, ln1_b))
    joined = hi_dot(normed, qkv_w)
    query = low(low_back(joined[:, :width])).reshape(group, length, HEADS, HEAD_DIM)
    keys = low(low_back(joined[:, width:2 * width])).reshape(group, length, HEADS, HEAD_DIM)
    values = low(low_back(joined[:, 2 * width:])).reshape(group, length, HEADS, HEAD_DIM)
    scores = jnp.einsum('gqhd,gkhd->ghqk', query, keys, precision=lax.Precision.HIGHEST)
    scores = low_back(scores * HEAD_DIM ** (-0.5))
    top = lax.optimization_barrier(jnp.max(scores, axis=-1, keepdims=True))
    expo = jnp.exp(scores - top)
    probs = low(expo / lax.optimization_barrier(jnp.sum(expo, axis=-1, keepdims=True)))
    mixed = jnp.einsum('ghqk,gkhd->gqhd', probs, values, precision=lax.Precision.HIGHEST)
    mixed = low(low_back(mixed.reshape(group * length, width)))
    branch = low_back(hi_dot(mixed, proj_w) + proj_b)
    middle = hidden + branch
    second = low(layer_norm(middle, ln2_g, ln2_b))
    upper = low_back(hi_dot(second, fc1_w) + fc1_b)
    active = low(jax.nn.gelu(upper, approximate=False))
    mlp_out = low_back(hi_dot(active, fc2_w) + fc2_b)
    return (middle + mlp_out).reshape(group, length, width)

def reference(inputs, skips, cotangent, bins, bin_weights, skip_w, skip_b, ln1_g, ln1_b, qkv_w, proj_w, proj_b, ln2_g, ln2_b, fc1_w, fc1_b, fc2_w, fc2_b):
    params = tuple((item.astype(jnp.float32) for item in (skip_w, skip_b, ln1_g, ln1_b, qkv_w, proj_w, proj_b, ln2_g, ln2_b, fc1_w, fc1_b, fc2_w, fc2_b)))
    group = max((step for step in range(1, 17) if ITEMS % step == 0))
    count = ITEMS // group
    item_weight = bin_weights.astype(jnp.float32)[bins]
    xs = inputs.astype(jnp.float32).reshape(count, group, LEN, D)
    ss = skips.astype(jnp.float32).reshape(count, group, LEN, D)
    cs = cotangent.astype(jnp.float32).reshape(count, group, LEN, D)
    ws = item_weight.reshape(count, group)

    def one_group(total, pieces):
        x_part, s_part, c_part, w_part = pieces
        result, pull = jax.vjp(forward, params, x_part, s_part)
        grads, d_x, d_s = pull(c_part * w_part[:, None, None])
        total = jax.tree.map(jnp.add, total, grads)
        return (total, (result.astype(jnp.bfloat16), d_x.astype(jnp.bfloat16), d_s.astype(jnp.bfloat16)))
    zeros = tuple((jnp.zeros_like(item) for item in params))
    total, (outs, d_xs, d_ss) = lax.scan(one_group, zeros, (xs, ss, cs, ws))
    return (outs.reshape(ITEMS, LEN, D), d_xs.reshape(ITEMS, LEN, D), d_ss.reshape(ITEMS, LEN, D), total[0], total[1], total[2], total[3], total[4], total[5], total[6], total[7], total[8], total[9], total[10], total[11], total[12])
```

```python
import functools

import jax
import jax.numpy as jnp
from jax import lax
from jax.experimental import pallas as pl
from jax.experimental.pallas import tpu as pltpu
from jax.sharding import Mesh, PartitionSpec as P

HEADS = 16
HEAD_DIM = 72
EPS = 1e-05
F32 = jnp.float32
BF16 = jnp.bfloat16
TEAM = ("near", "core", "seq")
FLIP2 = [(0, 1), (1, 0)]
FLIP4 = [(0, 3), (1, 2), (2, 1), (3, 0)]
VMEM = 56 * 1024 * 1024


def params():
    return pltpu.CompilerParams(vmem_limit_bytes=VMEM)


def nn(a, b):
    return lax.dot_general(a, b, (((1,), (0,)), ((), ())), preferred_element_type=F32)


def nt(a, b):
    return lax.dot_general(a, b, (((1,), (1,)), ((), ())), preferred_element_type=F32)


def tn(a, b):
    return lax.dot_general(a, b, (((0,), (0,)), ((), ())), preferred_element_type=F32)


def norm_forward(total, g, b):
    center = total - jnp.mean(total, axis=-1, keepdims=True)
    spread = jnp.mean(center * center, axis=-1, keepdims=True)
    return center * lax.rsqrt(spread + EPS) * g + b


def norm_kernel(base, a, b, c, d, bias, gain, shift, total_ref, normed_ref):
    total = a[...] + b[...].astype(F32) + c[...].astype(F32) + d[...].astype(F32) + bias[...]
    if base is not None:
        total = total + base[...]
    total_ref[...] = total
    normed_ref[...] = norm_forward(total, gain[...], shift[...]).astype(BF16)


def norm_call(base, parts, bias, gain, shift):
    shape = parts[0].shape
    body = norm_kernel if base is not None else functools.partial(norm_kernel, None)
    ops = (() if base is None else (base,)) + tuple(parts) + (bias, gain, shift)
    return pl.pallas_call(
        body,
        out_shape=(jax.ShapeDtypeStruct(shape, F32), jax.ShapeDtypeStruct(shape, BF16)),
        compiler_params=params(),
        name="norm",
    )(*ops)


def norm_back_kernel(a, b, c, d, total, gain, resid, factor, wide_ref, low_ref, sums_ref):
    grad = a[...] + b[...].astype(F32) + c[...].astype(F32) + d[...].astype(F32)
    center = total[...] - jnp.mean(total[...], axis=-1, keepdims=True)
    spread = jnp.mean(center * center, axis=-1, keepdims=True)
    scale = lax.rsqrt(spread + EPS)
    unit = center * scale
    inner = grad * gain[...]
    back = inner - jnp.mean(inner, axis=-1, keepdims=True)
    back = (back - unit * jnp.mean(inner * unit, axis=-1, keepdims=True)) * scale
    passed = resid[...].astype(F32)
    if factor is not None:
        passed = passed * factor[...]
    wide = passed + back
    low = wide.astype(BF16)
    if wide_ref is not None:
        wide_ref[...] = wide
    low_ref[...] = low
    sums_ref[0:1, :] = jnp.sum(grad * unit, axis=0, keepdims=True)
    sums_ref[1:2, :] = jnp.sum(grad, axis=0, keepdims=True)
    sums_ref[2:3, :] = jnp.sum(low.astype(F32), axis=0, keepdims=True)


def norm_back_first(a, b, c, d, total, gain, resid, factor, wide_ref, low_ref, sums_ref):
    norm_back_kernel(a, b, c, d, total, gain, resid, factor, wide_ref, low_ref, sums_ref)


def norm_back_last(a, b, c, d, total, gain, resid, low_ref, sums_ref):
    norm_back_kernel(a, b, c, d, total, gain, resid, None, None, low_ref, sums_ref)


def norm_back_call(parts, total, gain, resid, factor):
    shape = total.shape
    low = jax.ShapeDtypeStruct(shape, BF16)
    sums = jax.ShapeDtypeStruct((3, shape[1]), F32)
    if factor is None:
        return pl.pallas_call(
            norm_back_last, out_shape=(low, sums), compiler_params=params(), name="norm_back"
        )(*parts, total, gain, resid)
    return pl.pallas_call(
        norm_back_first,
        out_shape=(jax.ShapeDtypeStruct(shape, F32), low, sums),
        compiler_params=params(),
        name="norm_back",
    )(*parts, total, gain, resid, factor)


def key_bias(rows, part):
    place = lax.broadcasted_iota(jnp.int32, (2 * rows, 1), 0)
    place = jnp.where(place >= rows, place - rows, place)
    return jnp.where(place < part, 0.0, -1e30).astype(F32)


def head_masks(width):
    lane = lax.broadcasted_iota(jnp.int32, (1, width), 1)
    return [
        jnp.where((lane >= i * HEAD_DIM) & (lane < (i + 1) * HEAD_DIM), 1.0, 0.0).astype(BF16)
        for i in range(width // HEAD_DIM)
    ]


def probs_of(k, q, bias):
    scores = nt(k, q) * (HEAD_DIM**-0.5) + bias
    expo = jnp.exp(scores - jnp.max(scores, axis=0, keepdims=True))
    return expo / jnp.sum(expo, axis=0, keepdims=True)


def attend_kernel(part, x_ref, qkv_ref, proj_ref, joined_ref, mixed_ref, out_ref):
    joined = nn(x_ref[0], qkv_ref[...]).astype(BF16)
    joined_ref[0] = joined
    width = joined.shape[1] // 3
    q, k, v = (joined[:, i * width : (i + 1) * width] for i in range(3))
    bias = key_bias(joined.shape[0] // 2, part)
    mixed = None
    for mask in head_masks(width):
        probs = probs_of(k, q * mask, bias).astype(BF16)
        term = tn(probs, v * mask)
        mixed = term if mixed is None else mixed + term
    mixed = mixed.astype(BF16)
    mixed_ref[0] = mixed
    out_ref[0] = nn(mixed, proj_ref[...]).astype(out_ref.dtype)


def attend_call(part, x, w_qkv, w_proj, kind):
    items, rows, width = x.shape
    whole = lambda w: pl.BlockSpec(w.shape, lambda i: (0, 0))
    slab = lambda n: pl.BlockSpec((1, rows, n), lambda i: (i, 0, 0))
    inner = w_proj.shape[0]
    return pl.pallas_call(
        functools.partial(attend_kernel, part),
        grid=(items,),
        in_specs=[slab(width), whole(w_qkv), whole(w_proj)],
        out_specs=[slab(3 * inner), slab(inner), slab(width)],
        out_shape=(
            jax.ShapeDtypeStruct((items, rows, 3 * inner), BF16),
            jax.ShapeDtypeStruct((items, rows, inner), BF16),
            jax.ShapeDtypeStruct((items, rows, width), kind),
        ),
        compiler_params=params(),
        name="attend",
    )(x, w_qkv, w_proj)


def attend_back_kernel(part, d_ref, joined_ref, qkv_ref, proj_ref, grads_ref, out_ref):
    d_mixed = nt(d_ref[0], proj_ref[...]).astype(BF16)
    joined = joined_ref[0]
    width = joined.shape[1] // 3
    q, k, v = (joined[:, i * width : (i + 1) * width] for i in range(3))
    bias = key_bias(joined.shape[0] // 2, part)
    d_q = d_k = d_v = 0.0
    for mask in head_masks(width):
        probs = probs_of(k, q * mask, bias)
        d_one = d_mixed * mask
        d_v = d_v + nn(probs.astype(BF16), d_one)
        d_probs = nt(v, d_one)
        inner = jnp.sum(d_probs * probs, axis=0, keepdims=True)
        d_scores = (probs * (d_probs - inner)).astype(BF16)
        d_k = d_k + nn(d_scores, q * mask)
        d_q = d_q + tn(d_scores, k * mask)
    factor = HEAD_DIM**-0.5
    grads = jnp.concatenate((d_q * factor, d_k * factor, d_v), axis=1).astype(BF16)
    grads_ref[0] = grads
    out_ref[0] = nt(grads, qkv_ref[...]).astype(out_ref.dtype)


def attend_back_call(part, d, joined, w_qkv, w_proj, kind):
    items, rows, width = d.shape
    whole = lambda w: pl.BlockSpec(w.shape, lambda i: (0, 0))
    slab = lambda n: pl.BlockSpec((1, rows, n), lambda i: (i, 0, 0))
    return pl.pallas_call(
        functools.partial(attend_back_kernel, part),
        grid=(items,),
        in_specs=[slab(width), slab(joined.shape[2]), whole(w_qkv), whole(w_proj)],
        out_specs=[slab(joined.shape[2]), slab(width)],
        out_shape=(
            jax.ShapeDtypeStruct(joined.shape, BF16),
            jax.ShapeDtypeStruct((items, rows, width), kind),
        ),
        compiler_params=params(),
        name="attend_back",
    )(d, joined, w_qkv, w_proj)


def mlp_kernel(x_ref, d_ref, up_ref, bias_ref, down_ref, act_ref, grad_ref, sum_ref, out_ref, back_ref):
    upper = nn(x_ref[0], up_ref[...]) + bias_ref[...]
    bell = 0.5 * (1.0 + lax.erf(upper * (0.5**0.5)))
    active = (upper * bell).astype(BF16)
    slope = bell + upper * jnp.exp(-0.5 * upper * upper) * 0.3989422804014327
    d_upper = (slope * nt(d_ref[0], down_ref[...])).astype(BF16)
    act_ref[0] = active
    grad_ref[0] = d_upper
    sum_ref[0] = jnp.sum(d_upper.astype(F32), axis=0, keepdims=True)
    back_ref[0] = nt(d_upper, up_ref[...]).astype(back_ref.dtype)
    out_ref[0] = nn(active, down_ref[...]).astype(out_ref.dtype)


def mlp_call(x, d, w_up, b_up, w_down, kind):
    items, rows, width = x.shape
    inner = w_up.shape[1]
    whole = lambda w: pl.BlockSpec(w.shape, lambda i: (0, 0))
    slab = lambda n: pl.BlockSpec((1, rows, n), lambda i: (i, 0, 0))
    return pl.pallas_call(
        mlp_kernel,
        grid=(items,),
        in_specs=[slab(width), slab(width), whole(w_up), whole(b_up), whole(w_down)],
        out_specs=[
            slab(inner),
            slab(inner),
            pl.BlockSpec((1, 1, inner), lambda i: (i, 0, 0)),
            slab(width),
            slab(width),
        ],
        out_shape=(
            jax.ShapeDtypeStruct((items, rows, inner), BF16),
            jax.ShapeDtypeStruct((items, rows, inner), BF16),
            jax.ShapeDtypeStruct((items, 1, inner), F32),
            jax.ShapeDtypeStruct((items, rows, width), kind),
            jax.ShapeDtypeStruct((items, rows, width), kind),
        ),
        compiler_params=params(),
        name="mlp",
    )(x, d, w_up, b_up, w_down)


def swap(v, *axes):
    return lax.ppermute(v, axes if len(axes) > 1 else axes[0], FLIP4 if len(axes) > 1 else FLIP2)


def spread_blocks(own):
    rows, width = own.shape
    quad = jnp.stack(
        (own, swap(own, "seq"), swap(own, "near"), swap(own, "near", "seq"))
    ).reshape(2, 2 * rows, width)
    return quad, swap(quad, "core")


def collect_blocks(mine, theirs, rows):
    width = mine.shape[-1]
    got = swap(theirs, "core")
    total = (mine.astype(F32) + got.astype(F32)).reshape(2, 2, rows, width)
    low = total.astype(BF16)
    return (
        total[0, 0],
        swap(low[0, 1], "seq"),
        swap(low[1, 0], "near"),
        swap(low[1, 1], "near", "seq"),
    )


def relative(blocks, far_first):
    for axis, name in enumerate(TEAM):
        at = {"near": 1, "core": 0, "seq": 2}[name] if far_first else axis
        here = lax.axis_index(name)
        blocks = jnp.where(here == 1, jnp.flip(blocks, axis=at), blocks)
    return blocks


def pad_rows(v, rows, axis):
    pads = [(0, 0)] * v.ndim
    pads[axis] = (0, rows - v.shape[axis])
    return jnp.pad(v, pads)


def gather_far(v):
    return lax.all_gather(v, "far", axis=0, tiled=False)


def pick(v, at, axis):
    return lax.dynamic_index_in_dim(v, at, axis, keepdims=False)


def body(
    inputs,
    skips,
    cotangent,
    bins,
    bin_weights,
    skip_w,
    skip_b,
    ln1_g,
    ln1_b,
    qkv_w,
    proj_w,
    proj_b,
    ln2_g,
    ln2_b,
    fc1_w,
    fc1_b,
    fc2_w,
    fc2_b,
    *,
    far,
):
    _, part, width = inputs.shape
    rows = -(-part // 8) * 8
    team = 8
    dp = far * 4
    hidden_all = fc1_w.shape[1]
    seq = lax.axis_index("seq")
    lo = lax.axis_index("near") * 2 + lax.axis_index("core")
    per = HEADS // team

    deep = width // dp
    k = skip_w.shape[0] // 2
    f = fc2_w.shape[0] // 2
    w_skip = gather_far(pick(skip_w.reshape(2, k, width), seq, 0)).reshape(far * k, width)
    w_down = gather_far(pick(fc2_w.reshape(2, f, width), seq, 0)).reshape(far * f, width)
    qkv_part = pick(qkv_w.reshape(deep, 3, 2, per, 4, HEAD_DIM), seq, 2)
    qkv_part = qkv_part.transpose(3, 0, 1, 2, 4).reshape(4, deep, 3 * per * HEAD_DIM)
    up_part = pick(fc1_w.reshape(deep, far, 4, 2, f), seq, 3)
    up_part = up_part.transpose(2, 0, 1, 3).reshape(4, deep, far * f)
    columns = jnp.concatenate((qkv_part, up_part), axis=2)
    columns = lax.all_to_all(columns, ("near", "core"), split_axis=0, concat_axis=0, tiled=True)
    columns = gather_far(columns).reshape(width, columns.shape[2])
    inner = per * HEAD_DIM
    w_qkv, w_up = columns[:, : 3 * inner], columns[:, 3 * inner :]
    one_head = dp == HEADS
    if one_head:
        w_proj = pick(gather_far(proj_w).reshape(2, per * HEAD_DIM, width), seq, 0)
    else:
        w_proj = lax.all_gather(proj_w, ("far", "near", "core"), axis=0, tiled=True)
        w_proj = pick(w_proj.reshape(2, per, 4, HEAD_DIM, width), seq, 0)
        w_proj = pick(w_proj, lo, 1).reshape(inner, width)
    small = jnp.concatenate((skip_b, ln1_g, ln1_b, proj_b, ln2_g, ln2_b, fc2_b, fc1_b))
    small = lax.all_gather(small, ("far", "near", "core"), axis=0, tiled=False).astype(F32)
    vectors = small[:, : 7 * deep].reshape(dp, 7, deep).transpose(1, 0, 2).reshape(7, 1, width)
    b_skip, g_one, s_one, b_proj, g_two, s_two, b_down = (vectors[i] for i in range(7))
    b_up = small[:, 7 * deep :].reshape(far, 4, 2, f)
    b_up = pick(pick(b_up, lo, 1), seq, 1).reshape(1, far * f)

    picks = bins[:, None] == jnp.arange(bin_weights.shape[0], dtype=jnp.int32)[None, :]
    item_weight = jnp.sum(jnp.where(picks, bin_weights[None, :], 0.0), axis=1)
    factor = jnp.broadcast_to(item_weight.reshape(1, 1), (1, width))
    cot = pad_rows(cotangent[0], rows, 0)
    d_own = (cot.astype(F32) * factor).astype(BF16)
    d_mlp = spread_blocks(d_own)

    half = far // 2
    quarter = far // 4
    x_in = pad_rows(inputs[0], rows, 0).reshape(rows, half, team, k)
    x_in = x_in.transpose(2, 0, 1, 3).reshape(team, rows, half * k)
    x_sk = pad_rows(skips[0].reshape(2, part, -1), rows, 1).reshape(2, rows, quarter, team, k)
    x_sk = x_sk.transpose(3, 1, 0, 2, 4).reshape(team, rows, 2 * quarter * k)
    sent = jnp.concatenate((x_in, x_sk), axis=2)
    got = lax.all_to_all(sent, TEAM, split_axis=0, concat_axis=0, tiled=True)
    got = got.reshape(4, 2, rows, far * k)
    got_sk = got[..., half * k :].reshape(4, 2, rows, 2, quarter * k).transpose(0, 3, 2, 1, 4)
    x_all = jnp.concatenate((got[..., : half * k], got_sk.reshape(4, 2, rows, half * k)), axis=3)
    x_all = x_all.reshape(2, 2, 2, rows, far * k).transpose(1, 0, 2, 3, 4)
    x_all = relative(x_all, True).reshape(2, 4 * rows, far * k)
    theirs = nn(x_all[1], w_skip).astype(BF16).reshape(2, 2 * rows, width)
    mine = nn(x_all[0], w_skip).reshape(2, 2 * rows, width)
    hidden, normed = norm_call(None, collect_blocks(mine, theirs, rows), b_skip, g_one, s_one)

    n1 = spread_blocks(normed)
    joined1, mixed1, theirs = attend_call(part, n1[1], w_qkv, w_proj, BF16)
    joined0, mixed0, mine = attend_call(part, n1[0], w_qkv, w_proj, F32)
    middle, second = norm_call(hidden, collect_blocks(mine, theirs, rows), b_proj, g_two, s_two)

    n2 = spread_blocks(second)
    act1, du1, s1, out1, back1 = mlp_call(n2[1], d_mlp[1], w_up, b_up, w_down, BF16)
    act0, du0, s0, out0, back0 = mlp_call(n2[0], d_mlp[0], w_up, b_up, w_down, F32)
    back = collect_blocks(back0, back1, rows)
    d_middle, d_branch, sums_two = norm_back_call(back, middle, g_two, cot, factor)
    out = collect_blocks(out0, out1, rows)
    output = middle + b_down + out[0]
    for term in out[1:]:
        output = output + term.astype(F32)
    output = output.astype(BF16)[:part].reshape(1, part, width)

    da = spread_blocks(d_branch)
    dj1, theirs = attend_back_call(part, da[1], joined1, w_qkv, w_proj, BF16)
    dj0, mine = attend_back_call(part, da[0], joined0, w_qkv, w_proj, F32)
    back = collect_blocks(mine, theirs, rows)
    d_hidden, sums_one = norm_back_call(back, hidden, g_one, d_middle, None)
    dh = spread_blocks(d_hidden)

    flat = lambda v: v.reshape(-1, v.shape[-1])
    dx1 = nt(flat(dh[1]), w_skip).astype(BF16)
    dx0 = nt(flat(dh[0]), w_skip).astype(BF16)
    dx = jnp.stack((dx0, dx1)).reshape(2, 2, 2, rows, far * k)
    dx = relative(dx, True).transpose(1, 0, 2, 3, 4).reshape(4, 2, rows, far * k)
    dx_sk = dx[..., half * k :].reshape(4, 2, rows, 2, quarter * k).transpose(0, 3, 2, 1, 4)
    sent = jnp.concatenate((dx[..., : half * k], dx_sk.reshape(4, 2, rows, half * k)), axis=3)
    got = lax.all_to_all(
        sent.reshape(team, rows, far * k), TEAM, split_axis=0, concat_axis=0, tiled=True
    )
    d_inputs = got[..., : half * k].reshape(team, rows, half, k).transpose(1, 2, 0, 3)
    d_inputs = d_inputs.reshape(rows, width)[:part].reshape(1, part, width)
    d_skips = got[..., half * k :].reshape(team, rows, 2, quarter, k).transpose(2, 1, 3, 0, 4)
    d_skips = d_skips.reshape(2, rows, width // 2)[:, :part].reshape(1, 2 * part, width // 2)

    def product(left, right):
        return (tn(flat(left[0]), flat(right[0])) + tn(flat(left[1]), flat(right[1]))).astype(BF16)

    g_down = product((act0, act1), d_mlp)
    g_up = product(n2, (du0, du1))
    g_proj = product((mixed0, mixed1), da)
    g_qkv = product(n1, (dj0, dj1))
    g_skip = product((x_all[0], x_all[1]), dh)

    def scatter(v):
        return lax.psum_scatter(v, "far", scatter_dimension=0, tiled=True)

    def both(v):
        return lax.all_gather(v, "seq", axis=0, tiled=False)

    d_fc2_w = both(scatter(g_down)).reshape(2 * f, width).astype(F32)
    d_skip_w = both(scatter(g_skip)).reshape(2 * k, width).astype(F32)
    g_up = scatter(g_up).reshape(4, deep, far * f)
    g_up = both(lax.all_to_all(g_up, ("near", "core"), split_axis=0, concat_axis=0, tiled=True))
    d_fc1_w = g_up.reshape(2, 4, deep, far, f).transpose(2, 3, 1, 0, 4)
    d_fc1_w = d_fc1_w.reshape(deep, hidden_all).astype(F32)
    g_qkv = scatter(g_qkv).reshape(4, deep, 3 * inner)
    g_qkv = both(lax.all_to_all(g_qkv, ("near", "core"), split_axis=0, concat_axis=0, tiled=True))
    d_qkv_w = g_qkv.reshape(2, 4, deep, 3, per, HEAD_DIM).transpose(2, 3, 0, 4, 1, 5)
    d_qkv_w = d_qkv_w.reshape(deep, 3 * width).astype(F32)
    if one_head:
        zero = jnp.zeros_like(g_proj)
        wide = jnp.concatenate(
            (jnp.where(seq == 0, g_proj, zero), jnp.where(seq == 1, g_proj, zero)), axis=0
        )
        low = scatter(wide)
    else:
        wide = jnp.zeros((2, per, 4, HEAD_DIM, width), BF16)
        wide = lax.dynamic_update_slice(
            wide, g_proj.reshape(1, per, 1, HEAD_DIM, width), (seq, 0, lo, 0, 0)
        )
        low = lax.psum_scatter(
            wide.reshape(width, width), ("far", "near", "core"), scatter_dimension=0, tiled=True
        )
    d_proj_w = low.astype(F32) + swap(low, "seq").astype(F32)

    d_down_b = jnp.sum(d_own.astype(F32), axis=0)
    d_up_b = jnp.zeros((far, 4, 2, f), F32)
    d_up_b = lax.dynamic_update_slice(
        d_up_b, (jnp.sum(s0, axis=0) + jnp.sum(s1, axis=0)).reshape(far, 1, 1, f), (0, lo, seq, 0)
    )
    here = jnp.concatenate(
        (
            sums_one[2].reshape(dp, deep),
            sums_one[0].reshape(dp, deep),
            sums_one[1].reshape(dp, deep),
            sums_two[2].reshape(dp, deep),
            sums_two[0].reshape(dp, deep),
            sums_two[1].reshape(dp, deep),
            d_down_b.reshape(dp, deep),
            d_up_b.reshape(dp, 2 * f),
        ),
        axis=1,
    )
    here = lax.psum(here, ("far", "near", "core", "seq"))
    here = pick(here, lax.axis_index("far") * 4 + lo, 0)
    vec = [here[i * deep : (i + 1) * deep] for i in range(7)]

    return (
        output,
        d_inputs,
        d_skips,
        d_skip_w,
        vec[0],
        vec[1],
        vec[2],
        d_qkv_w,
        d_proj_w,
        vec[3],
        vec[4],
        vec[5],
        d_fc1_w,
        here[7 * deep :],
        d_fc2_w,
        vec[6],
    )


def solution(mesh):
    dp, seq = mesh.shape["dp"], mesh.shape["seq"]
    far = dp // 4
    fine = Mesh(mesh.devices.reshape(far, 2, 2, seq), ("far", "near", "core", "seq"))
    items = ("far", "near", "core")
    tokens = P(items, "seq", None)
    features = P(items, None, "seq")
    matrix = P(items, None)
    vector = P(items)
    in_specs = (
        tokens,
        features,
        tokens,
        vector,
        P(),
        matrix,
        vector,
        vector,
        vector,
        matrix,
        matrix,
        vector,
        vector,
        vector,
        matrix,
        vector,
        matrix,
        vector,
    )
    out_specs = (
        tokens,
        tokens,
        features,
        matrix,
        vector,
        vector,
        vector,
        matrix,
        matrix,
        vector,
        vector,
        vector,
        matrix,
        vector,
        matrix,
        vector,
    )
    return jax.shard_map(
        functools.partial(body, far=far),
        mesh=fine,
        in_specs=in_specs,
        out_specs=out_specs,
        check_vma=False,
    )
```

```python
import functools

import jax
import jax.numpy as jnp
from jax import lax
from jax.experimental import pallas as pl
from jax.experimental.pallas import tpu as pltpu
from jax.sharding import Mesh, PartitionSpec as P

HEADS = 16
HEAD_DIM = 72
EPS = 1e-05
F32 = jnp.float32
BF16 = jnp.bfloat16
TEAM = ("near", "core", "seq")
LITTLE, WINDOW, FIRST = 5, 20, 100
FLIP2 = [(0, 1), (1, 0)]
FLIP4 = [(0, 3), (1, 2), (2, 1), (3, 0)]


def nn(a, b):
    return lax.dot_general(a, b, (((1,), (0,)), ((), ())), preferred_element_type=F32)


def nt(a, b):
    return lax.dot_general(a, b, (((1,), (1,)), ((), ())), preferred_element_type=F32)


def tn(a, b):
    return lax.dot_general(a, b, (((0,), (0,)), ((), ())), preferred_element_type=F32)


def shape(dims, kind):
    return jax.ShapeDtypeStruct(tuple(dims), kind)


class Line:
    def __init__(self):
        self.word = None

    def __call__(self, kernel, outs, *ops, scratch=(), limit=12, name=None, scalars=(), cost=0.1):
        single = not isinstance(outs, tuple)
        outs = (outs,) if single else outs
        spec = pl.BlockSpec(memory_space=pltpu.VMEM)
        n, m = len(ops) + len(scalars), len(outs)
        late = () if self.word is None else (self.word,)

        def call(*refs):
            ins, rest = refs[:n], refs[n + len(late) :]
            rest[m][...] = jnp.zeros_like(rest[m])
            kernel(*ins, *rest[:m], *rest[m + 1 :])

        *results, self.word = pl.pallas_call(
            call,
            out_shape=outs + (jax.ShapeDtypeStruct((8, 128), F32),),
            in_specs=[spec] * len(ops)
            + [pl.BlockSpec(memory_space=pltpu.SMEM)] * len(scalars)
            + [pl.BlockSpec(memory_space=pl.ANY)] * len(late),
            out_specs=(spec,) * (m + 1),
            scratch_shapes=list(scratch),
            cost_estimate=pl.CostEstimate(flops=int(cost * 1e9), bytes_accessed=1000, transcendentals=0),
            compiler_params=pltpu.CompilerParams(vmem_limit_bytes=limit * 1024 * 1024),
            name=name,
        )(*ops, *scalars, *late)
        return results[0] if single else tuple(results)


def pack_kernel(half, quarter, k, x_ref, s_ref, out_ref, wide, tall):
    part = x_ref.shape[0]
    x = x_ref[...].astype(F32)
    wide[0 : 2 * part, :] = s_ref[...].astype(F32)
    first, second = wide[0:part, :], wide[part : 2 * part, :]
    tall[part:, :] = jnp.zeros((tall.shape[0] - part, tall.shape[1]), F32)
    for r in range(8):
        pieces = [
            src[:, (j * 8 + r) * k : (j * 8 + r + 1) * k]
            for src, n in ((x, half), (first, quarter), (second, quarter))
            for j in range(n)
        ]
        tall[0:part, :] = jnp.concatenate(pieces, axis=1)
        out_ref[r] = tall[...].astype(BF16)


def pack_call(run, x, s, rows, half, quarter, k):
    deep = 2 * half * k
    return run(
        functools.partial(pack_kernel, half, quarter, k),
        shape((8, rows, deep), BF16),
        x,
        s,
        scratch=[pltpu.VMEM((s.shape[0], s.shape[1]), F32), pltpu.VMEM((rows, deep), F32)],
        name="pack",
        cost=FIRST,
    )


def skip_half_kernel(w_ref, *refs):
    *small, out_ref = refs
    k = w_ref.shape[0] // 2
    w = w_ref[...].astype(F32)
    w = jnp.where(lax.axis_index("seq") == 0, w[:k], w[k:])
    line = [ref[...].astype(F32) for ref in small]
    line.append(jnp.zeros((1, w.shape[1] - sum(v.shape[1] for v in line)), F32))
    line = jnp.concatenate(line, axis=1)
    line = jnp.where(lax.broadcasted_iota(jnp.int32, (8, 1), 0) == 0, line, 0.0)
    out_ref[...] = jnp.concatenate((w, line), axis=0).astype(BF16)


def lo_index():
    return lax.axis_index("near") * 2 + lax.axis_index("core")


def choose(at, values):
    out = values[0]
    for i in range(1, len(values)):
        out = jnp.where(at == i, values[i], out)
    return out


def pack_columns_kernel(far, per, joint, f, qkv_ref, up_ref, *outs):
    seq = lax.axis_index("seq")
    lo = lo_index()
    w, up = qkv_ref[...].astype(F32), up_ref[...].astype(F32)
    deep, width = w.shape[0], w.shape[1] // 3
    spare = jnp.zeros((deep, joint - 3 * per * HEAD_DIM), F32)
    blocks = []
    for j in range(4):
        both = []
        for s in range(2):
            heads = [
                w[:, at : at + HEAD_DIM]
                for b in range(3)
                for i in range(per)
                for at in (b * width + ((s * per + i) * 4 + j) * HEAD_DIM,)
            ]
            hidden = [up[:, at : at + f] for z in range(far) for at in (((z * 4 + j) * 2 + s) * f,)]
            both.append(jnp.concatenate(heads + [spare] + hidden, axis=1))
        blocks.append(jnp.where(seq == 0, both[0], both[1]))
    for j, out in enumerate(outs):
        out[...] = choose(lax.bitwise_xor(lo, j), blocks).astype(BF16)


def order_columns_kernel(joint, own, a, b, c, down_ref, proj_ref, qkv_ref, rest_ref):
    lo = lo_index()
    got = [ref[...].astype(F32) for ref in (own, a, b, c)]
    deep = got[0].shape[0]
    blocks = [choose(lax.bitwise_xor(lo, j), got) for j in range(4)]
    third = proj_ref.shape[1] // 3
    for j in range(4):
        qkv_ref[j, :, :joint] = blocks[j][:, :joint].astype(BF16)
        if j < 3:
            qkv_ref[j, :, joint:] = proj_ref[:, j * third : (j + 1) * third]
        else:
            qkv_ref[j, :, joint:] = jnp.zeros((deep, third), BF16)
    down = down_ref[...].astype(F32)
    down = jnp.where(lax.axis_index("seq") == 0, down[: 2 * deep], down[2 * deep :])
    for i in range(2):
        up = jnp.concatenate((blocks[i][:, joint:], blocks[2 + i][:, joint:]), axis=1)
        rest_ref[i] = up.astype(BF16)
        rest_ref[2 + i] = down[i * deep : (i + 1) * deep].astype(BF16)


def split_first_kernel(got_ref, qkv_ref, proj_ref):
    joint = qkv_ref.shape[2]
    third = got_ref.shape[2] - joint
    for g in range(got_ref.shape[0]):
        qkv_ref[g] = got_ref[g, :, :joint]
        if g % 4 < 3:
            proj_ref[g // 4, :, (g % 4) * third : (g % 4 + 1) * third] = got_ref[g, :, joint:]


def split_kernel(far, got_ref, up_ref, down_ref):
    for z in range(far):
        for i in range(2):
            pair = got_ref[4 * z + i].astype(F32)
            n = pair.shape[1] // 2
            up_ref[4 * z + i] = pair[:, :n].astype(BF16)
            up_ref[4 * z + 2 + i] = pair[:, n:].astype(BF16)
            down_ref[2 * z + i] = got_ref[4 * z + 2 + i]


def order_skip_kernel(deep, lo_f, *refs):
    *blocks, w_ref, vec_ref, up_ref = refs
    n = len(blocks)
    k = w_ref.shape[1]
    far, lo, seq = lax.axis_index("far"), lo_index(), lax.axis_index("seq")
    got = [ref[...].astype(F32) for ref in blocks]
    for j, v in enumerate(got):
        w_ref[lax.rem(far - j + n, n)] = v[:k].astype(BF16)
    lines = [choose(lax.rem(far - z + n, n), [v[k : k + 1] for v in got]) for z in range(n)]
    up_ref[...] = jnp.concatenate(
        [jnp.where(seq == 0, v[:, :lo_f], v[:, lo_f : 2 * lo_f]) for v in lines], axis=1
    )
    pieces = []
    for v in lines:
        tall = [v[:, 2 * lo_f + i * deep : 2 * lo_f + (i + 1) * deep] for i in range(7)]
        tall = jnp.concatenate([jnp.zeros_like(tall[0])] + tall, axis=0)
        pieces += [jnp.where((lo == j) & (seq == 0), tall, 0.0) for j in range(4)]
    vec_ref[...] = jnp.concatenate(pieces, axis=1)


def unpack_kernel(half, quarter, k, got_ref, x_ref, s_ref, wide):
    part = x_ref.shape[0]
    got = [got_ref[r, 0:part, :].astype(F32) for r in range(8)]
    x_ref[...] = jnp.concatenate(
        [got[r][:, j * k : (j + 1) * k] for j in range(half) for r in range(8)], axis=1
    ).astype(BF16)
    for t in range(2):
        base = half + t * quarter
        wide[t * part : (t + 1) * part, :] = jnp.concatenate(
            [got[r][:, (base + j) * k : (base + j + 1) * k] for j in range(quarter) for r in range(8)],
            axis=1,
        )
    s_ref[...] = wide[...].astype(BF16)


def unpack_call(run, got, part, half, quarter, k):
    width = 8 * half * k
    return run(
        functools.partial(unpack_kernel, half, quarter, k),
        (shape((part, width), BF16), shape((2 * part, width // 2), BF16)),
        got,
        scratch=[pltpu.VMEM((2 * part, width // 2), F32)],
        name="unpack",
    )


def halves(h, q, a, b):
    zero = jnp.concatenate((a[:, :h], a[:, h : h + q], b[:, h : h + q]), axis=1)
    one = jnp.concatenate((b[:, :h], a[:, h + q :], b[:, h + q :]), axis=1)
    return zero, one


def skip_kernel(side, part, h, q, got_ref, w_ref, vec_ref, x_ref, out_ref):
    near, core, seq = (lax.axis_index(name) for name in TEAM)
    real = lax.broadcasted_iota(jnp.int32, (got_ref.shape[1], 1), 0) < part
    for fn in range(2):
        base = lax.bitwise_xor(near, fn) * 4 + lax.bitwise_xor(core, side) * 2
        zero, one = halves(h, q, got_ref[base].astype(F32), got_ref[base + 1].astype(F32))
        mine = jnp.where(seq == 0, zero, one)
        other = jnp.where(seq == 0, one, zero)
        for i, x in enumerate((mine, other)):
            x = jnp.where(real, x, 0.0).astype(BF16)
            x_ref[2 * fn + i] = x
            out = nn(x, w_ref[...])
            base = out.shape[0] - 8
            out = jnp.concatenate((out[:base], out[base:] + vec_ref[...]), axis=0)
            out_ref[2 * fn + i] = out.astype(out_ref.dtype)


def skip_call(run, side, part, h, q, got, w, vec, kind):
    _, rows, deep = got.shape
    return run(
        functools.partial(skip_kernel, side, part, h, q),
        (shape((4, rows, deep), BF16), shape((4, rows, w.shape[1]), kind)),
        got,
        w,
        vec,
        name="skip",
    )


def turn_kernel(x0_ref, x1_ref, out_ref):
    for i, ref in enumerate((x0_ref, x1_ref)):
        for j in range(4):
            out_ref[4 * i + j] = ref[j].astype(F32).T.astype(BF16)


def skip_back_kernel(h, q, d0_ref, d1_ref, w_ref, out_ref):
    near, core, seq = (lax.axis_index(name) for name in TEAM)
    for side, d_ref in enumerate((d0_ref, d1_ref)):
        for fn in range(2):
            base = lax.bitwise_xor(near, fn) * 4 + lax.bitwise_xor(core, side) * 2
            mine = nt(d_ref[2 * fn], w_ref[...])
            other = nt(d_ref[2 * fn + 1], w_ref[...])
            zero = jnp.where(seq == 0, mine, other)
            one = jnp.where(seq == 0, other, mine)
            out_ref[base] = jnp.concatenate(
                (zero[:, :h], zero[:, h : h + q], one[:, h : h + q]), axis=1
            ).astype(BF16)
            out_ref[base + 1] = jnp.concatenate(
                (one[:, :h], zero[:, h + q :], one[:, h + q :]), axis=1
            ).astype(BF16)


def skip_back_call(run, h, q, dh, w):
    rows = dh[0].shape[1]
    return run(
        functools.partial(skip_back_kernel, h, q),
        shape((8, rows, w.shape[0]), BF16),
        dh[0],
        dh[1],
        w,
        name="skip_back",
    )


def merge_kernel(mine_ref, got_ref, *outs):
    for i, out in enumerate(outs):
        out[...] = (mine_ref[i + 1] + got_ref[i + 1].astype(F32)).astype(BF16)


def stack_kernel(a, b, c, d, out_ref):
    for i, ref in enumerate((a, b, c, d)):
        out_ref[i] = ref[...]


def arrived(mine_ref, got_ref, others):
    total = mine_ref[0] + got_ref[0].astype(F32)
    for ref in others:
        total = total + ref[...].astype(F32)
    return total


def normalized(total, gain, shift):
    center = total - jnp.mean(total, axis=-1, keepdims=True)
    spread = jnp.mean(center * center, axis=-1, keepdims=True)
    return (center * lax.rsqrt(spread + EPS) * gain + shift).astype(BF16)


def norm_first_kernel(mine, got, b, c, d, total_ref, normed_ref, vec_ref):
    total = arrived(mine, got, (b, c, d))
    vec_ref[...] = total[total.shape[0] - 8 :]
    bias, gain, shift = (vec_ref[i : i + 1, :] for i in (1, 2, 3))
    total = total + bias
    total_ref[...] = total
    normed_ref[...] = normalized(total, gain, shift)


def norm_second_kernel(base, mine, got, b, c, d, vec_ref, total_ref, normed_ref):
    bias, gain, shift = (vec_ref[i : i + 1, :] for i in (4, 5, 6))
    total = arrived(mine, got, (b, c, d)) + bias + base[...]
    total_ref[...] = total
    normed_ref[...] = normalized(total, gain, shift)


def norm_back_kernel(place, part, mine, got, b, c, d, total_ref, vec_ref, resid, wide_ref, low_ref):
    grad = arrived(mine, got, (b, c, d))
    gain = vec_ref[place : place + 1, :]
    center = total_ref[...] - jnp.mean(total_ref[...], axis=-1, keepdims=True)
    spread = jnp.mean(center * center, axis=-1, keepdims=True)
    scale = lax.rsqrt(spread + EPS)
    unit = center * scale
    inner = grad * gain
    back = inner - jnp.mean(inner, axis=-1, keepdims=True)
    back = (back - unit * jnp.mean(inner * unit, axis=-1, keepdims=True)) * scale
    wide = resid[...] + back
    if wide_ref is not None:
        wide_ref[...] = wide
    d_gain = jnp.sum(grad * unit, axis=0, keepdims=True)
    d_shift = jnp.sum(grad, axis=0, keepdims=True)
    row = lax.broadcasted_iota(jnp.int32, (wide.shape[0], 1), 0)
    wide = jnp.where(row < part, wide, 0.0)
    for i, v in enumerate((d_gain, d_shift)):
        high = v.astype(BF16).astype(F32)
        wide = jnp.where(row == part + 2 * i, high, wide)
        wide = jnp.where(row == part + 2 * i + 1, v - high, wide)
    low_ref[...] = wide.astype(BF16)


def norm_back_last(place, part, mine, got, b, c, d, total, vec, resid, low_ref):
    norm_back_kernel(place, part, mine, got, b, c, d, total, vec, resid, None, low_ref)


def norm_back_call(run, place, part, parts, total, vec, resid, both):
    low = shape(total.shape, BF16)
    body = functools.partial(norm_back_kernel if both else norm_back_last, place, part)
    outs = (shape(total.shape, F32), low) if both else low
    return run(body, outs, *parts, total, vec, resid, name="norm_back")


def cot_kernel(cot_ref, bins_ref, weights_ref, wide_ref, low_ref):
    part = cot_ref.shape[0]
    wide_ref[...] = jnp.zeros_like(wide_ref)
    wide_ref[0:part, :] = cot_ref[...].astype(F32) * weights_ref[bins_ref[0]]
    low_ref[...] = wide_ref[...].astype(BF16)


def token_place(rows):
    place = lax.broadcasted_iota(jnp.int32, (2 * rows, 1), 0)
    return jnp.where(place >= rows, place - rows, place)


def head_masks(width):
    lane = lax.broadcasted_iota(jnp.int32, (1, width), 1)
    return [
        jnp.where((lane >= i * HEAD_DIM) & (lane < (i + 1) * HEAD_DIM), 1.0, 0.0).astype(BF16)
        for i in range(width // HEAD_DIM)
    ]


def probs_of(k, q, bias):
    scores = nt(k, q) * (HEAD_DIM**-0.5) + bias
    expo = jnp.exp(scores - jnp.max(scores, axis=0, keepdims=True))
    return expo * (1.0 / jnp.sum(expo, axis=0, keepdims=True))


def split3(v, width):
    return (v[:, i * width : (i + 1) * width] for i in range(3))


def attend_kernel(part, x_ref, qkv_ref, proj_ref, joined_ref, mixed_ref, out_ref):
    rows = out_ref.shape[1]
    seq = lax.axis_index("seq") if proj_ref.shape[0] > 1 else 0
    real = token_place(rows) < part
    bias = jnp.where(real, 0.0, -1e30).astype(F32)
    for item in range(x_ref.shape[0]):
        joined = nn(x_ref[item], qkv_ref[...]).astype(BF16)
        joined_ref[item] = joined
        q, k, v = split3(joined, mixed_ref.shape[2])
        mixed = None
        for mask in head_masks(q.shape[1]):
            probs = probs_of(k, q * mask, bias).astype(BF16)
            term = tn(probs, v * mask)
            mixed = term if mixed is None else mixed + term
        mixed = jnp.where(real, mixed, 0.0).astype(BF16)
        mixed_ref[item] = mixed
        out = nn(mixed, proj_ref[seq])
        out_ref[2 * item] = out[:rows].astype(out_ref.dtype)
        out_ref[2 * item + 1] = out[rows:].astype(out_ref.dtype)


def attend_call(run, part, x, w_qkv, w_proj, kind):
    items, rows, width = x.shape
    inner = w_proj.shape[1]
    return run(
        functools.partial(attend_kernel, part),
        (
            shape((items, rows, w_qkv.shape[1]), BF16),
            shape((items, rows, inner), BF16),
            shape((2 * items, rows // 2, width), kind),
        ),
        x,
        w_qkv,
        w_proj,
        name="attend",
        cost=LITTLE,
    )


def attend_back_kernel(part, d_ref, joined_ref, qkv_ref, proj_ref, grads_ref, out_ref):
    rows = out_ref.shape[1]
    real = token_place(rows) < part
    bias = jnp.where(real, 0.0, -1e30).astype(F32)
    factor = HEAD_DIM**-0.5
    seq = lax.axis_index("seq") if proj_ref.shape[0] > 1 else 0
    for item in range(d_ref.shape[0]):
        d_mixed = nt(d_ref[item], proj_ref[seq])
        d_mixed = jnp.where(real, d_mixed, 0.0).astype(BF16)
        q, k, v = split3(joined_ref[item], proj_ref.shape[1])
        d_q = d_k = d_v = 0.0
        for mask in head_masks(q.shape[1]):
            probs = probs_of(k, q * mask, bias)
            d_one = d_mixed * mask
            d_v = d_v + nn(probs.astype(BF16), d_one)
            d_probs = nt(v, d_one)
            inner = jnp.sum(d_probs * probs, axis=0, keepdims=True)
            d_scores = (probs * (d_probs - inner)).astype(BF16)
            d_k = d_k + nn(d_scores, q * mask)
            d_q = d_q + tn(d_scores, k * mask)
        spare = jnp.zeros((2 * rows, grads_ref.shape[2] - 3 * d_v.shape[1]), F32)
        grads = jnp.concatenate((d_q * factor, d_k * factor, d_v, spare), axis=1).astype(BF16)
        grads_ref[item] = grads
        out = nt(grads, qkv_ref[...])
        out_ref[2 * item] = out[:rows].astype(out_ref.dtype)
        out_ref[2 * item + 1] = out[rows:].astype(out_ref.dtype)


def attend_back_call(run, part, d, joined, w_qkv, w_proj, kind):
    items, rows, width = d.shape
    return run(
        functools.partial(attend_back_kernel, part),
        (shape(joined.shape, BF16), shape((2 * items, rows // 2, width), kind)),
        d,
        joined,
        w_qkv,
        w_proj,
        name="attend_back",
        cost=3,
    )


def mlp_kernel(x_ref, d_ref, up_ref, bias_ref, down_ref, act_ref, grad_ref, sum_ref, out_ref):
    rows = out_ref.shape[1]
    total = 0.0
    for item in range(x_ref.shape[0]):
        upper = nn(x_ref[item], up_ref[...]) + bias_ref[...]
        bell = 0.5 * (1.0 + lax.erf(upper * (0.5**0.5)))
        act_ref[item] = (upper * bell).astype(BF16)
        slope = bell + upper * jnp.exp(-0.5 * upper * upper) * 0.3989422804014327
        d_upper = (slope * nt(d_ref[item], down_ref[...])).astype(BF16)
        grad_ref[item] = d_upper
        total = total + jnp.sum(d_upper.astype(F32), axis=0, keepdims=True)
        out = nt(d_upper, up_ref[...])
        out_ref[2 * item] = out[:rows].astype(out_ref.dtype)
        out_ref[2 * item + 1] = out[rows:].astype(out_ref.dtype)
    sum_ref[...] = total


def mlp_call(run, x, d, w_up, b_up, w_down, kind):
    items, rows, width = x.shape
    inner = w_up.shape[1]
    return run(
        mlp_kernel,
        (
            shape((items, rows, inner), BF16),
            shape((items, rows, inner), BF16),
            shape((1, inner), F32),
            shape((2 * items, rows // 2, width), kind),
        ),
        x,
        d,
        w_up,
        b_up,
        w_down,
        name="mlp",
    )


def down_kernel(act_ref, w_ref, out_ref):
    rows = out_ref.shape[1]
    for item in range(act_ref.shape[0]):
        out = nn(act_ref[item], w_ref[...])
        out_ref[2 * item] = out[:rows].astype(out_ref.dtype)
        out_ref[2 * item + 1] = out[rows:].astype(out_ref.dtype)


def down_call(run, act, w, kind):
    items, rows, _ = act.shape
    dims = (2 * items, rows // 2, w.shape[1])
    return run(down_kernel, shape(dims, kind), act, w, name="down", cost=WINDOW)


def output_kernel(place, base, mine, got, b, c, d, vec_ref, out_ref):
    total = base[...] + arrived(mine, got, (b, c, d)) + vec_ref[place : place + 1, :]
    out_ref[...] = total[: out_ref.shape[0]].astype(BF16)


def product_kernel(*refs):
    *sides, out_ref = refs
    total = 0.0
    n = len(sides) // 2
    for left, right in zip(sides[:n], sides[n:]):
        for item in range(left.shape[0]):
            total = total + tn(left[item], right[item])
    out_ref[...] = total.astype(BF16)


def product_call(run, left, right, name):
    dims = (left[0].shape[-1], right[0].shape[-1])
    return run(product_kernel, shape(dims, BF16), *left, *right, name=name)


def product_two_kernel(far, n20, n21, du0, du1, act0, act1, dm0, dm1, out_ref):
    def product(pairs):
        total = 0.0
        for left, right in pairs:
            for item in range(2):
                total = total + tn(left[item], right[item])
        return total

    deep = out_ref.shape[2]
    down = product(((act0, dm0), (act1, dm1)))
    for z in range(far):
        for i in range(2):
            at = (2 * z + i) * deep
            out_ref[z, 2 + i] = down[at : at + deep].astype(BF16)
    up = product(((n20, du0), (n21, du1)))
    for z in range(far):
        for i in range(2):
            at = (4 * z + i) * deep
            pair = (up[at : at + deep], up[at + 2 * deep : at + 3 * deep])
            out_ref[z, i] = jnp.concatenate(pair, axis=1).astype(BF16)


def product_attend_kernel(far, n10, n11, dj0, dj1, a0, a1, d0, d1, out_ref):
    def product(pairs):
        total = 0.0
        for left, right in pairs:
            for item in range(2):
                total = total + tn(left[item], right[item])
        return total

    deep, joint = out_ref.shape[2], dj0.shape[2]
    third = out_ref.shape[3] - joint
    qkv = product(((n10, dj0), (n11, dj1)))
    for z in range(far):
        for j in range(4):
            at = (4 * z + j) * deep
            out_ref[z, j, :, :joint] = qkv[at : at + deep].astype(BF16)
    proj = product(((a0, d0), (a1, d1)))
    seq = lax.axis_index("seq")
    for z in range(far):
        at = z % 2 * deep
        rows = jnp.where(seq == z // 2, proj[at : at + deep], 0.0).astype(BF16)
        for j in range(4):
            cut = rows[:, j * third : (j + 1) * third] if j < 3 else jnp.zeros((deep, third), BF16)
            out_ref[z, j, :, joint:] = cut


def double_up_kernel(got_ref, up_ref, down_ref):
    n = up_ref.shape[2]
    for j in range(4):
        v = got_ref[j % 2].astype(F32)[:, (j // 2) * n : (j // 2 + 1) * n].astype(BF16)
        up_ref[2 * j] = v
        up_ref[2 * j + 1] = v
    for i in range(2):
        down_ref[i] = got_ref[2 + i]


def double_qkv_kernel(got_ref, qkv_ref, proj_ref):
    joint = qkv_ref.shape[2]
    third = got_ref.shape[2] - joint
    for j in range(4):
        v = got_ref[j, :, :joint]
        qkv_ref[2 * j] = v
        qkv_ref[2 * j + 1] = v
        if j < 3:
            proj_ref[:, j * third : (j + 1) * third] = got_ref[j, :, joint:]


def pair_sum_kernel(a_ref, b_ref, out_ref):
    out_ref[...] = a_ref[...].astype(F32) + b_ref[...].astype(F32)


def sums_kernel(part, rows, da0, da1, dm0, dm1, out_ref):
    lines = block_sums(part, rows, (da0, da1), True) + block_sums(part, rows, (dm0, dm1), False)
    out_ref[...] = jnp.concatenate(lines + [jnp.zeros((4, da0.shape[-1]), F32)], axis=0)


def block_sums(part, rows, refs, extra):
    place = token_place(rows)
    sums = [0.0, 0.0, 0.0]
    for ref in refs:
        for item in range(2):
            v = ref[item].astype(F32)
            sums[0] = sums[0] + jnp.sum(jnp.where(place < part, v, 0.0), axis=0, keepdims=True)
            if extra:
                for i in range(2):
                    at = (place == part + 2 * i) | (place == part + 2 * i + 1)
                    sums[1 + i] = sums[1 + i] + jnp.sum(jnp.where(at, v, 0.0), axis=0, keepdims=True)
    return sums if extra else sums[:1]


def vector_kernel(far, deep, part, rows, xt_ref, dh0, dh1, sums_ref, s0, s1, out_ref):
    lo = lax.axis_index("near") * 2 + lax.axis_index("core")
    width = dh0.shape[-1]
    total = 0.0
    for side, ref in enumerate((dh0, dh1)):
        for item in range(2):
            d = ref[item]
            for i in range(2):
                total = total + nn(xt_ref[4 * side + 2 * item + i], d[i * rows : (i + 1) * rows])
    k = total.shape[0] // far
    lines = block_sums(part, rows, (dh0, dh1), True)
    stacked = jnp.concatenate(lines + [sums_ref[i : i + 1, :] for i in range(5)], axis=0)
    up = s0[...] + s1[...]
    f = up.shape[1] // far
    spare = jnp.zeros((8, width - 2 * f), F32)
    row = lax.broadcasted_iota(jnp.int32, (8, 1), 0)
    for z in range(far):
        cut = 0.0
        for j in range(4):
            at = (z * 4 + j) * deep
            cut = cut + jnp.where(lo == j, stacked[:, at : at + deep], 0.0)
        low = jnp.concatenate((cut, jnp.zeros((8, 2 * f - deep), F32)), axis=1)
        tall = jnp.concatenate((up[:, z * f : (z + 1) * f], jnp.zeros((1, f), F32)), axis=1)
        low = jnp.where(row == 7, tall, low)
        low = jnp.concatenate((low, spare), axis=1)
        out_ref[z] = jnp.concatenate((total[z * k : (z + 1) * k], low), axis=0).astype(BF16)


def two_halves_kernel(mine_ref, other_ref, out_ref):
    seq = lax.axis_index("seq")
    k = mine_ref.shape[1]
    for i in range(2):
        mine, other = mine_ref[i].astype(F32), other_ref[i].astype(F32)
        out_ref[i * k : (i + 1) * k, :] = jnp.where(seq == 0, mine, other)
        out_ref[(2 + i) * k : (3 + i) * k, :] = jnp.where(seq == 0, other, mine)


def last_kernel(k, deep, f, mine_ref, other_ref, out_ref, vec_ref, up_ref):
    seq = lax.axis_index("seq")
    mine, other = mine_ref[...].astype(F32), other_ref[...].astype(F32)
    zero = jnp.where(seq == 0, mine, other)
    one = jnp.where(seq == 0, other, mine)
    out_ref[0:k, :] = zero[:k]
    out_ref[k : 2 * k, :] = one[:k]
    vec_ref[...] = mine[k : k + 8, :deep]
    up_ref[...] = jnp.concatenate((zero[k + 7 : k + 8, :f], one[k + 7 : k + 8, :f]), axis=1)


def columns_kernel(order, got_ref, out_ref):
    got = [got_ref[i].astype(F32) for i in range(8)]
    out_ref[...] = jnp.concatenate([got[2 * lo + s][:, at : at + n] for s, lo, at, n in order], axis=1)


def columns_call(run, order, got, name):
    wide = sum(n for *_, n in order)
    return run(functools.partial(columns_kernel, order), shape((got.shape[1], wide), F32), got, name=name)


def swap(v, *axes):
    return lax.ppermute(v, axes if len(axes) > 1 else axes[0], FLIP4 if len(axes) > 1 else FLIP2)


def send_own(own):
    return own, swap(own, "seq"), swap(own, "near"), swap(own, "near", "seq")


def spread_blocks(run, parts):
    rows, width = parts[0].shape
    quad = run(stack_kernel, shape((4, rows, width), BF16), *parts, name="stack")
    other = swap(quad, "core")
    return quad.reshape(2, 2 * rows, width), other.reshape(2, 2 * rows, width)


def collect_blocks(run, mine, got):
    one = shape(mine.shape[1:], BF16)
    b, c, d = run(merge_kernel, (one, one, one), mine, got, name="merge")
    return mine, got, swap(b, "seq"), swap(c, "near"), swap(d, "near", "seq")


def from_far(v, far):
    return [v] + [lax.ppermute(v, "far", [(i, (i + j) % far) for i in range(far)]) for j in range(1, far)]


def to_far(blocks, far):
    return [blocks[0]] + [
        lax.ppermute(blocks[j], "far", [(i, (i + j) % far) for i in range(far)]) for j in range(1, far)
    ]


def gather_far(v):
    return lax.all_gather(v, "far", axis=0, tiled=False)


def pick(v, at, axis):
    return lax.dynamic_index_in_dim(v, at, axis, keepdims=False)


def body(
    inputs,
    skips,
    cotangent,
    bins,
    bin_weights,
    skip_w,
    skip_b,
    ln1_g,
    ln1_b,
    qkv_w,
    proj_w,
    proj_b,
    ln2_g,
    ln2_b,
    fc1_w,
    fc1_b,
    fc2_w,
    fc2_b,
    *,
    far,
):
    _, part, width = inputs.shape
    rows = -(-part // 8) * 8
    dp = far * 4
    seq = lax.axis_index("seq")
    lo = lax.axis_index("near") * 2 + lax.axis_index("core")
    per = HEADS // 8
    inner = per * HEAD_DIM
    joint = -(-3 * inner // 128) * 128
    deep = width // dp
    k = skip_w.shape[0] // 2
    f = fc2_w.shape[0] // 2
    half, quarter = far // 2, far // 4
    spread = far * k
    one_head = dp == HEADS

    run = Line()

    sent = pack_call(run, inputs[0], skips[0], rows, half, quarter, k)
    got = lax.all_to_all(sent, TEAM, split_axis=0, concat_axis=0, tiled=True)
    small = tuple(v.reshape(1, -1) for v in (fc1_b, skip_b, ln1_g, ln1_b, proj_b, ln2_g, ln2_b, fc2_b))
    skip_half = run(
        skip_half_kernel, shape((k + 8, width), BF16), skip_w, *small, name="skip_half", cost=FIRST
    )
    skip_blocks = from_far(skip_half, far)
    columns = run(
        functools.partial(pack_columns_kernel, far, per, joint, f),
        (shape((deep, joint + far * f), BF16),) * 4,
        qkv_w,
        fc1_w,
        name="pack_columns",
        cost=FIRST,
    )
    columns = (columns[0], swap(columns[1], "core"), swap(columns[2], "near"), swap(columns[3], "near", "core"))
    w_skip, vec, b_up = run(
        functools.partial(order_skip_kernel, deep, f),
        (shape((far, k, width), BF16), shape((8, width), F32), shape((1, far * f), F32)),
        *skip_blocks,
        name="order_skip",
    )
    w_skip = w_skip.reshape(spread, width)
    qkv_part, rest = run(
        functools.partial(order_columns_kernel, joint),
        (shape((4, deep, joint + width // 3), BF16), shape((4, deep, width), BF16)),
        *columns,
        fc2_w,
        proj_w,
        name="order_columns",
    )
    first = gather_far(qkv_part).reshape(dp, deep, joint + width // 3)
    rest = gather_far(rest).reshape(4 * far, deep, width)
    x1, theirs = skip_call(run, 1, part, half * k, quarter * k, got, w_skip, vec, BF16)
    pair = swap(theirs, "core")
    x0, mine = skip_call(run, 0, part, half * k, quarter * k, got, w_skip, vec, F32)
    come = collect_blocks(run, mine, pair)
    x_turned = run(turn_kernel, shape((8, spread, rows), BF16), x0, x1, name="turn")
    d_wide, d_own = run(
        cot_kernel,
        (shape((rows, width), F32), shape((rows, width), BF16)),
        cotangent[0],
        name="cot",
        scalars=(bins, bin_weights),
    )
    hidden, normed, vec = run(
        norm_first_kernel,
        (shape((rows, width), F32), shape((rows, width), BF16), shape((8, width), F32)),
        *come,
        name="norm",
    )

    parts = send_own(normed)
    n1 = spread_blocks(run, parts)
    w_qkv, w_proj = run(
        split_first_kernel,
        (shape((dp, deep, joint), BF16), shape((far, deep, width), BF16)),
        first,
        name="split_first",
    )
    w_qkv = w_qkv.reshape(width, joint)
    if one_head:
        w_proj = w_proj.reshape(2, inner, width)
    else:
        w_proj = lax.all_gather(proj_w, ("far", "near", "core"), axis=0, tiled=True)
        w_proj = pick(w_proj.reshape(2, per, 4, HEAD_DIM, width), seq, 0)
        w_proj = pick(w_proj, lo, 1).reshape(1, inner, width)
    joined1, mixed1, theirs = attend_call(run, part, n1[1], w_qkv, w_proj, BF16)
    pair = swap(theirs, "core")
    d_parts = send_own(d_own)
    joined0, mixed0, mine = attend_call(run, part, n1[0], w_qkv, w_proj, F32)
    come = collect_blocks(run, mine, pair)
    d_mlp = spread_blocks(run, d_parts)
    middle, second = run(
        norm_second_kernel,
        (shape((rows, width), F32), shape((rows, width), BF16)),
        hidden,
        *come,
        vec,
        name="norm",
    )

    parts = send_own(second)
    n2 = spread_blocks(run, parts)
    w_up, w_down = run(
        functools.partial(split_kernel, far),
        (shape((4 * far, deep, far * f), BF16), shape((2 * far, deep, width), BF16)),
        rest,
        name="split",
    )
    w_up, w_down = w_up.reshape(width, far * f), w_down.reshape(far * f, width)
    act1, du1, s1, theirs = mlp_call(run, n2[1], d_mlp[1], w_up, b_up, w_down, BF16)
    pair = swap(theirs, "core")
    act0, du0, s0, mine = mlp_call(run, n2[0], d_mlp[0], w_up, b_up, w_down, F32)
    come = collect_blocks(run, mine, pair)

    def scatter(v):
        return lax.psum_scatter(v, "far", scatter_dimension=0, tiled=True)

    def to_team(v):
        return lax.all_to_all(v, TEAM, split_axis=0, concat_axis=0, tiled=True)

    g_rest = run(
        functools.partial(product_two_kernel, far),
        shape((far, 4, deep, width), BF16),
        *n2,
        du0,
        du1,
        act0,
        act1,
        *d_mlp,
        name="grad_mlp",
        cost=WINDOW,
    )
    g_rest = scatter(g_rest.reshape(4 * far, deep, width))
    d_middle, d_branch = norm_back_call(run, 5, part, come, middle, vec, d_wide, True)

    parts = send_own(d_branch)
    out_pair = swap(down_call(run, act1, w_down, BF16), "core")
    out_mine = down_call(run, act0, w_down, F32)
    da = spread_blocks(run, parts)
    out_come = collect_blocks(run, out_mine, out_pair)
    dj1, theirs = attend_back_call(run, part, da[1], joined1, w_qkv, w_proj, BF16)
    pair = swap(theirs, "core")
    dj0, mine = attend_back_call(run, part, da[0], joined0, w_qkv, w_proj, F32)
    output = run(
        functools.partial(output_kernel, 7), shape((part, width), BF16), middle, *out_come, vec, name="output"
    )
    come = collect_blocks(run, mine, pair)
    if one_head:
        g_first = run(
            functools.partial(product_attend_kernel, far),
            shape((far, 4, deep, joint + width // 3), BF16),
            *n1,
            dj0,
            dj1,
            mixed0,
            mixed1,
            *da,
            name="grad_attend",
            cost=WINDOW,
        )
        g_first = scatter(g_first.reshape(4 * far, deep, -1))
    else:
        g_qkv = scatter(product_call(run, n1, (dj0, dj1), "grad_qkv")).reshape(4, deep, joint)
        g_first = jnp.pad(g_qkv, ((0, 0), (0, 0), (0, width // 3)))
        g_proj = product_call(run, (mixed0, mixed1), da, "grad_proj")
        spot = jnp.zeros((2, per, 4, HEAD_DIM, width), BF16)
        spot = lax.dynamic_update_slice(
            spot, g_proj.reshape(1, per, 1, HEAD_DIM, width), (seq, 0, lo, 0, 0)
        )
        low_own = lax.psum_scatter(
            spot.reshape(width, width), ("far", "near", "core"), scatter_dimension=0, tiled=True
        )
    g_up, g_down = run(
        double_up_kernel,
        (shape((8, deep, far * f), BF16), shape((2, deep, width), BF16)),
        g_rest,
        name="double_up",
        cost=WINDOW,
    )
    g_up = to_team(g_up)
    down_other = swap(g_down, "seq")
    d_hidden = norm_back_call(run, 2, part, come, hidden, vec, d_middle, False)

    parts = send_own(d_hidden)
    early = run(
        functools.partial(sums_kernel, part, rows), shape((8, width), F32), *da, *d_mlp, name="sums", cost=WINDOW
    )
    dh = spread_blocks(run, parts)
    g_skip = run(
        functools.partial(vector_kernel, far, deep, part, rows),
        shape((far, k + 8, width), BF16),
        x_turned,
        *dh,
        early,
        s0,
        s1,
        name="grad_skip",
    )
    g_skip = scatter(g_skip.reshape(far * (k + 8), width))
    blocks = tuple(v.reshape(4, rows, width) for v in dh)
    sent = skip_back_call(run, half * k, quarter * k, blocks, w_skip)
    got = lax.all_to_all(sent, TEAM, split_axis=0, concat_axis=0, tiled=True)
    order = [(s, j, z * f, f) for z in range(far) for j in range(4) for s in range(2)]
    d_fc1_w = columns_call(run, order, g_up, "whole_up")
    d_fc2_w = run(two_halves_kernel, shape((2 * f, width), F32), g_down, down_other, name="whole_down")
    g_qkv, low = run(
        double_qkv_kernel,
        (shape((8, deep, joint), BF16), shape((deep, width), BF16)),
        g_first,
        name="double_qkv",
    )
    g_qkv = to_team(g_qkv)
    if not one_head:
        low = low_own
    low_other = swap(low, "seq")

    d_inputs, d_skips = unpack_call(run, got, part, half, quarter, k)
    order = [
        (s, j, (b * per + i) * HEAD_DIM, HEAD_DIM)
        for b in range(3)
        for s in range(2)
        for i in range(per)
        for j in range(4)
    ]
    d_qkv_w = columns_call(run, order, g_qkv, "whole_qkv")
    d_proj_w = run(pair_sum_kernel, shape(low.shape, F32), low, low_other, name="whole_proj")
    d_skip_w, vectors, d_up_b = run(
        functools.partial(last_kernel, k, deep, f),
        (shape((2 * k, width), F32), shape((8, deep), F32), shape((1, 2 * f), F32)),
        g_skip,
        swap(g_skip, "seq"),
        name="whole_skip",
    )
    return (
        output.reshape(1, part, width),
        d_inputs.reshape(1, part, width),
        d_skips.reshape(1, 2 * part, width // 2),
        d_skip_w,
        vectors[0],
        vectors[1],
        vectors[2],
        d_qkv_w,
        d_proj_w,
        vectors[3],
        vectors[4],
        vectors[5],
        d_fc1_w,
        d_up_b.reshape(2 * f),
        d_fc2_w,
        vectors[6],
    )


def solution(mesh):
    dp, seq = mesh.shape["dp"], mesh.shape["seq"]
    far = dp // 4
    fine = Mesh(mesh.devices.reshape(far, 2, 2, seq), ("far", "near", "core", "seq"))
    items = ("far", "near", "core")
    tokens = P(items, "seq", None)
    features = P(items, None, "seq")
    matrix = P(items, None)
    vector = P(items)
    in_specs = (
        tokens,
        features,
        tokens,
        vector,
        P(),
        matrix,
        vector,
        vector,
        vector,
        matrix,
        matrix,
        vector,
        vector,
        vector,
        matrix,
        vector,
        matrix,
        vector,
    )
    out_specs = (
        tokens,
        tokens,
        features,
        matrix,
        vector,
        vector,
        vector,
        matrix,
        matrix,
        vector,
        vector,
        vector,
        matrix,
        vector,
        matrix,
        vector,
    )
    return jax.shard_map(
        functools.partial(body, far=far),
        mesh=fine,
        in_specs=in_specs,
        out_specs=out_specs,
        check_vma=False,
    )
```

```python
import functools

import jax
import jax.numpy as jnp
from jax import lax
from jax.experimental import pallas as pl
from jax.experimental.pallas import tpu as pltpu
from jax.sharding import Mesh, PartitionSpec as P

HEADS = 16
HEAD_DIM = 72
EPS = 1e-05
F32 = jnp.float32
BF16 = jnp.bfloat16
TEAM = ("near", "core", "seq")
WEIGHTS = {"turn": 6, "attend": 5, "grad_mlp": 12, "grad_attend": 12, "down": 20, "sums": 12, "double_up": 20, "skip_half": 8, "pack": 4, "pack_columns": 50, "whole_down": 6, "attend_back1": 3, "norm_back2": 2, "output": 2, "order_skip": 0.5, "merge3": 3, "grad_skip": 0.1, "unpack": 20, "stack4": 0.1, "stack5": 4, "mlp2": 3, "order_columns": 12, "norm_back1": 12, "merge5": 8, "mlp1": 1, "down_part": 0.1}
FLIP2 = [(0, 1), (1, 0)]
FLIP4 = [(0, 3), (1, 2), (2, 1), (3, 0)]


def nn(a, b):
    return lax.dot_general(a, b, (((1,), (0,)), ((), ())), preferred_element_type=F32)


def nt(a, b):
    return lax.dot_general(a, b, (((1,), (1,)), ((), ())), preferred_element_type=F32)


def tn(a, b):
    return lax.dot_general(a, b, (((0,), (0,)), ((), ())), preferred_element_type=F32)


def shape(dims, kind):
    return jax.ShapeDtypeStruct(tuple(dims), kind)


class Line:
    def __init__(self):
        self.word = None
        self.calls = {}

    def __call__(self, kernel, outs, *ops, scratch=(), limit=12, name=None, scalars=()):
        single = not isinstance(outs, tuple)
        outs = (outs,) if single else outs
        spec = pl.BlockSpec(memory_space=pltpu.VMEM)
        n, m = len(ops) + len(scalars), len(outs)
        late = () if self.word is None else (self.word,)
        count = self.calls[name] = self.calls.get(name, 0) + 1
        weight = WEIGHTS.get(f"{name}{count}", WEIGHTS.get(name, 0.1))

        def call(*refs):
            ins, rest = refs[:n], refs[n + len(late) :]
            rest[m][...] = jnp.zeros_like(rest[m])
            kernel(*ins, *rest[:m], *rest[m + 1 :])

        *results, self.word = pl.pallas_call(
            call,
            out_shape=outs + (jax.ShapeDtypeStruct((8, 128), F32),),
            in_specs=[spec] * len(ops)
            + [pl.BlockSpec(memory_space=pltpu.SMEM)] * len(scalars)
            + [pl.BlockSpec(memory_space=pl.ANY)] * len(late),
            out_specs=(spec,) * (m + 1),
            scratch_shapes=list(scratch),
            cost_estimate=pl.CostEstimate(flops=int(weight * 1e9), bytes_accessed=1000, transcendentals=0),
            compiler_params=pltpu.CompilerParams(vmem_limit_bytes=limit * 1024 * 1024),
            name=name,
        )(*ops, *scalars, *late)
        return results[0] if single else tuple(results)


def pack_kernel(half, quarter, k, x_ref, s_ref, out_ref, wide, tall):
    part = x_ref.shape[0]
    x = x_ref[...].astype(F32)
    wide[0 : 2 * part, :] = s_ref[...].astype(F32)
    first, second = wide[0:part, :], wide[part : 2 * part, :]
    tall[part:, :] = jnp.zeros((tall.shape[0] - part, tall.shape[1]), F32)
    for r in range(8):
        pieces = [
            src[:, (j * 8 + r) * k : (j * 8 + r + 1) * k]
            for src, n in ((x, half), (first, quarter), (second, quarter))
            for j in range(n)
        ]
        tall[0:part, :] = jnp.concatenate(pieces, axis=1)
        out_ref[r] = tall[...].astype(BF16)


def pack_call(run, x, s, rows, half, quarter, k):
    deep = 2 * half * k
    return run(
        functools.partial(pack_kernel, half, quarter, k),
        shape((8, rows, deep), BF16),
        x,
        s,
        scratch=[pltpu.VMEM((s.shape[0], s.shape[1]), F32), pltpu.VMEM((rows, deep), F32)],
        name="pack",
    )


def skip_half_kernel(w_ref, *refs):
    *small, out_ref = refs
    k = w_ref.shape[0] // 2
    w = w_ref[...].astype(F32)
    w = jnp.where(lax.axis_index("seq") == 0, w[:k], w[k:])
    line = [ref[...].astype(F32) for ref in small]
    line.append(jnp.zeros((1, w.shape[1] - sum(v.shape[1] for v in line)), F32))
    line = jnp.concatenate(line, axis=1)
    line = jnp.where(lax.broadcasted_iota(jnp.int32, (8, 1), 0) == 0, line, 0.0)
    out_ref[...] = jnp.concatenate((w, line), axis=0).astype(BF16)


def lo_index():
    return lax.axis_index("near") * 2 + lax.axis_index("core")


def choose(at, values):
    out = values[0]
    for i in range(1, len(values)):
        out = jnp.where(at == i, values[i], out)
    return out


def pack_columns_kernel(far, per, joint, f, qkv_ref, up_ref, *outs):
    seq = lax.axis_index("seq")
    lo = lo_index()
    w, up = qkv_ref[...].astype(F32), up_ref[...].astype(F32)
    deep, width = w.shape[0], w.shape[1] // 3
    spare = jnp.zeros((deep, joint - 3 * per * HEAD_DIM), F32)
    blocks = []
    for j in range(4):
        both = []
        for s in range(2):
            heads = [
                w[:, at : at + HEAD_DIM]
                for b in range(3)
                for i in range(per)
                for at in (b * width + ((s * per + i) * 4 + j) * HEAD_DIM,)
            ]
            hidden = [up[:, at : at + f] for z in range(far) for at in (((z * 4 + j) * 2 + s) * f,)]
            both.append(jnp.concatenate(heads + [spare] + hidden, axis=1))
        blocks.append(jnp.where(seq == 0, both[0], both[1]))
    for j, out in enumerate(outs):
        out[...] = choose(lax.bitwise_xor(lo, j), blocks).astype(BF16)


def order_columns_kernel(joint, own, a, b, c, down_ref, proj_ref, qkv_ref, rest_ref):
    lo = lo_index()
    got = [ref[...].astype(F32) for ref in (own, a, b, c)]
    deep = got[0].shape[0]
    blocks = [choose(lax.bitwise_xor(lo, j), got) for j in range(4)]
    third = proj_ref.shape[1] // 3
    for j in range(4):
        qkv_ref[j, :, :joint] = blocks[j][:, :joint].astype(BF16)
        if j < 3:
            qkv_ref[j, :, joint:] = proj_ref[:, j * third : (j + 1) * third]
        else:
            qkv_ref[j, :, joint:] = jnp.zeros((deep, third), BF16)
    down = down_ref[...].astype(F32)
    down = jnp.where(lax.axis_index("seq") == 0, down[: 2 * deep], down[2 * deep :])
    for i in range(2):
        up = jnp.concatenate((blocks[i][:, joint:], blocks[2 + i][:, joint:]), axis=1)
        rest_ref[i] = up.astype(BF16)
        rest_ref[2 + i] = down[i * deep : (i + 1) * deep].astype(BF16)


def split_first_kernel(got_ref, qkv_ref, proj_ref):
    joint = qkv_ref.shape[2]
    third = got_ref.shape[2] - joint
    for g in range(got_ref.shape[0]):
        qkv_ref[g] = got_ref[g, :, :joint]
        if g % 4 < 3:
            proj_ref[g // 4, :, (g % 4) * third : (g % 4 + 1) * third] = got_ref[g, :, joint:]


def split_kernel(far, got_ref, up_ref, down_ref):
    for z in range(far):
        for i in range(2):
            pair = got_ref[4 * z + i].astype(F32)
            n = pair.shape[1] // 2
            up_ref[4 * z + i] = pair[:, :n].astype(BF16)
            up_ref[4 * z + 2 + i] = pair[:, n:].astype(BF16)
            down_ref[2 * z + i] = got_ref[4 * z + 2 + i]


def order_skip_kernel(deep, lo_f, *refs):
    *blocks, w_ref, vec_ref, up_ref = refs
    n = len(blocks)
    k = w_ref.shape[1]
    far, lo, seq = lax.axis_index("far"), lo_index(), lax.axis_index("seq")
    got = [ref[...].astype(F32) for ref in blocks]
    for j, v in enumerate(got):
        w_ref[lax.rem(far - j + n, n)] = v[:k].astype(BF16)
    lines = [choose(lax.rem(far - z + n, n), [v[k : k + 1] for v in got]) for z in range(n)]
    up_ref[...] = jnp.concatenate(
        [jnp.where(seq == 0, v[:, :lo_f], v[:, lo_f : 2 * lo_f]) for v in lines], axis=1
    )
    pieces = []
    for v in lines:
        tall = [v[:, 2 * lo_f + i * deep : 2 * lo_f + (i + 1) * deep] for i in range(7)]
        tall = jnp.concatenate([jnp.zeros_like(tall[0])] + tall, axis=0)
        pieces += [jnp.where((lo == j) & (seq == 0), tall, 0.0) for j in range(4)]
    vec_ref[...] = jnp.concatenate(pieces, axis=1)


def unpack_kernel(half, quarter, k, got_ref, x_ref, s_ref, wide):
    part = x_ref.shape[0]
    got = [got_ref[r, 0:part, :].astype(F32) for r in range(8)]
    x_ref[...] = jnp.concatenate(
        [got[r][:, j * k : (j + 1) * k] for j in range(half) for r in range(8)], axis=1
    ).astype(BF16)
    for t in range(2):
        base = half + t * quarter
        wide[t * part : (t + 1) * part, :] = jnp.concatenate(
            [got[r][:, (base + j) * k : (base + j + 1) * k] for j in range(quarter) for r in range(8)],
            axis=1,
        )
    s_ref[...] = wide[...].astype(BF16)


def unpack_call(run, got, part, half, quarter, k):
    width = 8 * half * k
    return run(
        functools.partial(unpack_kernel, half, quarter, k),
        (shape((part, width), BF16), shape((2 * part, width // 2), BF16)),
        got,
        scratch=[pltpu.VMEM((2 * part, width // 2), F32)],
        name="unpack",
    )


def halves(h, q, a, b):
    zero = jnp.concatenate((a[:, :h], a[:, h : h + q], b[:, h : h + q]), axis=1)
    one = jnp.concatenate((b[:, :h], a[:, h + q :], b[:, h + q :]), axis=1)
    return zero, one


def skip_kernel(side, part, h, q, got_ref, w_ref, vec_ref, x_ref, out_ref):
    near, core, seq = (lax.axis_index(name) for name in TEAM)
    real = lax.broadcasted_iota(jnp.int32, (got_ref.shape[1], 1), 0) < part
    for fn in range(2):
        base = lax.bitwise_xor(near, fn) * 4 + lax.bitwise_xor(core, side) * 2
        zero, one = halves(h, q, got_ref[base].astype(F32), got_ref[base + 1].astype(F32))
        mine = jnp.where(seq == 0, zero, one)
        other = jnp.where(seq == 0, one, zero)
        for i, x in enumerate((mine, other)):
            x = jnp.where(real, x, 0.0).astype(BF16)
            x_ref[2 * fn + i] = x
            out = nn(x, w_ref[...])
            base = out.shape[0] - 8
            out = jnp.concatenate((out[:base], out[base:] + vec_ref[...]), axis=0)
            out_ref[2 * fn + i] = out.astype(out_ref.dtype)


def skip_call(run, side, part, h, q, got, w, vec, kind):
    _, rows, deep = got.shape
    return run(
        functools.partial(skip_kernel, side, part, h, q),
        (shape((4, rows, deep), BF16), shape((4, rows, w.shape[1]), kind)),
        got,
        w,
        vec,
        name="skip",
    )


def turn_kernel(x0_ref, x1_ref, out_ref):
    for i, ref in enumerate((x0_ref, x1_ref)):
        for j in range(4):
            out_ref[4 * i + j] = ref[j].astype(F32).T.astype(BF16)


def skip_back_kernel(h, q, d0_ref, d1_ref, w_ref, out_ref):
    near, core, seq = (lax.axis_index(name) for name in TEAM)
    for side, d_ref in enumerate((d0_ref, d1_ref)):
        for fn in range(2):
            base = lax.bitwise_xor(near, fn) * 4 + lax.bitwise_xor(core, side) * 2
            mine = nt(d_ref[2 * fn], w_ref[...])
            other = nt(d_ref[2 * fn + 1], w_ref[...])
            zero = jnp.where(seq == 0, mine, other)
            one = jnp.where(seq == 0, other, mine)
            out_ref[base] = jnp.concatenate(
                (zero[:, :h], zero[:, h : h + q], one[:, h : h + q]), axis=1
            ).astype(BF16)
            out_ref[base + 1] = jnp.concatenate(
                (one[:, :h], zero[:, h + q :], one[:, h + q :]), axis=1
            ).astype(BF16)


def skip_back_call(run, h, q, dh, w):
    rows = dh[0].shape[1]
    return run(
        functools.partial(skip_back_kernel, h, q),
        shape((8, rows, w.shape[0]), BF16),
        dh[0],
        dh[1],
        w,
        name="skip_back",
    )


def merge_kernel(mine_ref, got_ref, own_ref, *outs):
    own_ref[...] = mine_ref[0] + got_ref[0].astype(F32)
    for i, out in enumerate(outs):
        out[...] = (mine_ref[i + 1] + got_ref[i + 1].astype(F32)).astype(BF16)


def stack_kernel(a, b, c, d, out_ref):
    for i, ref in enumerate((a, b, c, d)):
        out_ref[i] = ref[...]


def arrived(own_ref, others):
    total = own_ref[...]
    for ref in others:
        total = total + ref[...].astype(F32)
    return total


def normalized(total, gain, shift):
    center = total - jnp.mean(total, axis=-1, keepdims=True)
    spread = jnp.mean(center * center, axis=-1, keepdims=True)
    return (center * lax.rsqrt(spread + EPS) * gain + shift).astype(BF16)


def norm_first_kernel(own, b, c, d, total_ref, normed_ref, vec_ref):
    total = arrived(own, (b, c, d))
    vec_ref[...] = total[total.shape[0] - 8 :]
    bias, gain, shift = (vec_ref[i : i + 1, :] for i in (1, 2, 3))
    total = total + bias
    total_ref[...] = total
    normed_ref[...] = normalized(total, gain, shift)


def norm_second_kernel(base, own, b, c, d, vec_ref, total_ref, normed_ref):
    bias, gain, shift = (vec_ref[i : i + 1, :] for i in (4, 5, 6))
    total = arrived(own, (b, c, d)) + bias + base[...]
    total_ref[...] = total
    normed_ref[...] = normalized(total, gain, shift)


def norm_back_kernel(place, part, own, b, c, d, total_ref, vec_ref, resid, wide_ref, low_ref):
    grad = arrived(own, (b, c, d))
    gain = vec_ref[place : place + 1, :]
    center = total_ref[...] - jnp.mean(total_ref[...], axis=-1, keepdims=True)
    spread = jnp.mean(center * center, axis=-1, keepdims=True)
    scale = lax.rsqrt(spread + EPS)
    unit = center * scale
    inner = grad * gain
    back = inner - jnp.mean(inner, axis=-1, keepdims=True)
    back = (back - unit * jnp.mean(inner * unit, axis=-1, keepdims=True)) * scale
    wide = resid[...] + back
    if wide_ref is not None:
        wide_ref[...] = wide
    d_gain = jnp.sum(grad * unit, axis=0, keepdims=True)
    d_shift = jnp.sum(grad, axis=0, keepdims=True)
    row = lax.broadcasted_iota(jnp.int32, (wide.shape[0], 1), 0)
    wide = jnp.where(row < part, wide, 0.0)
    for i, v in enumerate((d_gain, d_shift)):
        high = v.astype(BF16).astype(F32)
        wide = jnp.where(row == part + 2 * i, high, wide)
        wide = jnp.where(row == part + 2 * i + 1, v - high, wide)
    low_ref[...] = wide.astype(BF16)


def norm_back_last(place, part, own, b, c, d, total, vec, resid, low_ref):
    norm_back_kernel(place, part, own, b, c, d, total, vec, resid, None, low_ref)


def norm_back_call(run, place, part, parts, total, vec, resid, both):
    low = shape(total.shape, BF16)
    body = functools.partial(norm_back_kernel if both else norm_back_last, place, part)
    outs = (shape(total.shape, F32), low) if both else low
    return run(body, outs, *parts, total, vec, resid, name="norm_back")


def cot_kernel(cot_ref, bins_ref, weights_ref, wide_ref, low_ref):
    part = cot_ref.shape[0]
    wide_ref[...] = jnp.zeros_like(wide_ref)
    wide_ref[0:part, :] = cot_ref[...].astype(F32) * weights_ref[bins_ref[0]]
    low_ref[...] = wide_ref[...].astype(BF16)


def token_place(rows):
    place = lax.broadcasted_iota(jnp.int32, (2 * rows, 1), 0)
    return jnp.where(place >= rows, place - rows, place)


def head_masks(width):
    lane = lax.broadcasted_iota(jnp.int32, (1, width), 1)
    return [
        jnp.where((lane >= i * HEAD_DIM) & (lane < (i + 1) * HEAD_DIM), 1.0, 0.0).astype(BF16)
        for i in range(width // HEAD_DIM)
    ]


def probs_of(k, q, bias):
    scores = nt(k, q) * (HEAD_DIM**-0.5) + bias
    expo = jnp.exp(scores - jnp.max(scores, axis=0, keepdims=True))
    return expo * (1.0 / jnp.sum(expo, axis=0, keepdims=True))


def split3(v, width):
    return (v[:, i * width : (i + 1) * width] for i in range(3))


def attend_kernel(part, x_ref, qkv_ref, proj_ref, joined_ref, mixed_ref, out_ref):
    rows = out_ref.shape[1]
    seq = lax.axis_index("seq") if proj_ref.shape[0] > 1 else 0
    real = token_place(rows) < part
    bias = jnp.where(real, 0.0, -1e30).astype(F32)

    @pl.loop(0, x_ref.shape[0])
    def _(item):
        joined = nn(x_ref[item], qkv_ref[...]).astype(BF16)
        joined_ref[item] = joined
        q, k, v = split3(joined, mixed_ref.shape[2])
        mixed = None
        for mask in head_masks(q.shape[1]):
            probs = probs_of(k, q * mask, bias).astype(BF16)
            term = tn(probs, v * mask)
            mixed = term if mixed is None else mixed + term
        mixed = jnp.where(real, mixed, 0.0).astype(BF16)
        mixed_ref[item] = mixed
        out = nn(mixed, proj_ref[seq])
        out_ref[2 * item] = out[:rows].astype(out_ref.dtype)
        out_ref[2 * item + 1] = out[rows:].astype(out_ref.dtype)


def attend_call(run, part, x, w_qkv, w_proj, kind):
    items, rows, width = x.shape
    inner = w_proj.shape[1]
    return run(
        functools.partial(attend_kernel, part),
        (
            shape((items, rows, w_qkv.shape[1]), BF16),
            shape((items, rows, inner), BF16),
            shape((2 * items, rows // 2, width), kind),
        ),
        x,
        w_qkv,
        w_proj,
        name="attend",
    )


def attend_back_kernel(part, d_ref, joined_ref, qkv_ref, proj_ref, grads_ref, out_ref):
    rows = out_ref.shape[1]
    real = token_place(rows) < part
    bias = jnp.where(real, 0.0, -1e30).astype(F32)
    factor = HEAD_DIM**-0.5
    seq = lax.axis_index("seq") if proj_ref.shape[0] > 1 else 0

    @pl.loop(0, d_ref.shape[0])
    def _(item):
        d_mixed = nt(d_ref[item], proj_ref[seq])
        d_mixed = jnp.where(real, d_mixed, 0.0).astype(BF16)
        q, k, v = split3(joined_ref[item], proj_ref.shape[1])
        d_q = d_k = d_v = 0.0
        for mask in head_masks(q.shape[1]):
            probs = probs_of(k, q * mask, bias)
            d_one = d_mixed * mask
            d_v = d_v + nn(probs.astype(BF16), d_one)
            d_probs = nt(v, d_one)
            inner = jnp.sum(d_probs * probs, axis=0, keepdims=True)
            d_scores = (probs * (d_probs - inner)).astype(BF16)
            d_k = d_k + nn(d_scores, q * mask)
            d_q = d_q + tn(d_scores, k * mask)
        spare = jnp.zeros((2 * rows, grads_ref.shape[2] - 3 * d_v.shape[1]), F32)
        grads = jnp.concatenate((d_q * factor, d_k * factor, d_v, spare), axis=1).astype(BF16)
        grads_ref[item] = grads
        out = nt(grads, qkv_ref[...])
        out_ref[2 * item] = out[:rows].astype(out_ref.dtype)
        out_ref[2 * item + 1] = out[rows:].astype(out_ref.dtype)


def attend_back_call(run, part, d, joined, w_qkv, w_proj, kind):
    items, rows, width = d.shape
    return run(
        functools.partial(attend_back_kernel, part),
        (shape(joined.shape, BF16), shape((2 * items, rows // 2, width), kind)),
        d,
        joined,
        w_qkv,
        w_proj,
        name="attend_back",
    )


def mlp_kernel(x_ref, d_ref, up_ref, bias_ref, down_ref, act_ref, grad_ref, sum_ref, out_ref):
    rows = out_ref.shape[1]
    sum_ref[...] = jnp.zeros_like(sum_ref)

    @pl.loop(0, x_ref.shape[0])
    def _(item):
        upper = nn(x_ref[item], up_ref[...]) + bias_ref[...]
        bell = 0.5 * (1.0 + lax.erf(upper * (0.5**0.5)))
        act_ref[item] = (upper * bell).astype(BF16)
        slope = bell + upper * jnp.exp(-0.5 * upper * upper) * 0.3989422804014327
        d_upper = (slope * nt(d_ref[item], down_ref[...])).astype(BF16)
        grad_ref[item] = d_upper
        sum_ref[...] += jnp.sum(d_upper.astype(F32), axis=0, keepdims=True)
        out = nt(d_upper, up_ref[...])
        out_ref[2 * item] = out[:rows].astype(out_ref.dtype)
        out_ref[2 * item + 1] = out[rows:].astype(out_ref.dtype)


def mlp_call(run, x, d, w_up, b_up, w_down, kind):
    items, rows, width = x.shape
    inner = w_up.shape[1]
    return run(
        mlp_kernel,
        (
            shape((items, rows, inner), BF16),
            shape((items, rows, inner), BF16),
            shape((1, inner), F32),
            shape((2 * items, rows // 2, width), kind),
        ),
        x,
        d,
        w_up,
        b_up,
        w_down,
        name="mlp",
    )


def down_kernel(act_ref, w_ref, out_ref):
    rows = out_ref.shape[1]

    @pl.loop(0, act_ref.shape[0])
    def _(item):
        out = nn(act_ref[item], w_ref[...])
        out_ref[2 * item] = out[:rows].astype(out_ref.dtype)
        out_ref[2 * item + 1] = out[rows:].astype(out_ref.dtype)


def down_call(run, act, w, kind):
    items, rows, _ = act.shape
    dims = (2 * items, rows // 2, w.shape[1])
    return run(down_kernel, shape(dims, kind), act, w, name="down")


def output_kernel(place, base, own, b, c, d, vec_ref, out_ref):
    total = base[...] + arrived(own, (b, c, d)) + vec_ref[place : place + 1, :]
    out_ref[...] = total[: out_ref.shape[0]].astype(BF16)


def product_kernel(*refs):
    *sides, out_ref = refs
    total = 0.0
    n = len(sides) // 2
    for left, right in zip(sides[:n], sides[n:]):
        for item in range(left.shape[0]):
            total = total + tn(left[item], right[item])
    out_ref[...] = total.astype(BF16)


def product_call(run, left, right, name):
    dims = (left[0].shape[-1], right[0].shape[-1])
    return run(product_kernel, shape(dims, BF16), *left, *right, name=name)


def product_two_kernel(far, n20, n21, du0, du1, act0, act1, dm0, dm1, out_ref):
    def product(pairs):
        total = 0.0
        for left, right in pairs:
            for item in range(2):
                total = total + tn(left[item], right[item])
        return total

    deep = out_ref.shape[2]
    down = product(((act0, dm0), (act1, dm1)))
    for z in range(far):
        for i in range(2):
            at = (2 * z + i) * deep
            out_ref[z, 2 + i] = down[at : at + deep].astype(BF16)
    up = product(((n20, du0), (n21, du1)))
    for z in range(far):
        for i in range(2):
            at = (4 * z + i) * deep
            pair = (up[at : at + deep], up[at + 2 * deep : at + 3 * deep])
            out_ref[z, i] = jnp.concatenate(pair, axis=1).astype(BF16)


def product_attend_kernel(far, n10, n11, dj0, dj1, a0, a1, d0, d1, out_ref):
    def product(pairs):
        total = 0.0
        for left, right in pairs:
            for item in range(2):
                total = total + tn(left[item], right[item])
        return total

    deep, joint = out_ref.shape[2], dj0.shape[2]
    third = out_ref.shape[3] - joint
    qkv = product(((n10, dj0), (n11, dj1)))
    for z in range(far):
        for j in range(4):
            at = (4 * z + j) * deep
            out_ref[z, j, :, :joint] = qkv[at : at + deep].astype(BF16)
    proj = product(((a0, d0), (a1, d1)))
    seq = lax.axis_index("seq")
    for z in range(far):
        at = z % 2 * deep
        rows = jnp.where(seq == z // 2, proj[at : at + deep], 0.0).astype(BF16)
        for j in range(4):
            cut = rows[:, j * third : (j + 1) * third] if j < 3 else jnp.zeros((deep, third), BF16)
            out_ref[z, j, :, joint:] = cut


def double_up_kernel(got_ref, up_ref, down_ref):
    n = up_ref.shape[2]
    for j in range(4):
        v = got_ref[j % 2].astype(F32)[:, (j // 2) * n : (j // 2 + 1) * n].astype(BF16)
        up_ref[2 * j] = v
        up_ref[2 * j + 1] = v
    for i in range(2):
        down_ref[i] = got_ref[2 + i]


def double_qkv_kernel(got_ref, qkv_ref, proj_ref):
    joint = qkv_ref.shape[2]
    third = got_ref.shape[2] - joint
    for j in range(4):
        v = got_ref[j, :, :joint]
        qkv_ref[2 * j] = v
        qkv_ref[2 * j + 1] = v
        if j < 3:
            proj_ref[:, j * third : (j + 1) * third] = got_ref[j, :, joint:]


def pair_sum_kernel(a_ref, b_ref, out_ref):
    out_ref[...] = a_ref[...].astype(F32) + b_ref[...].astype(F32)


def sums_kernel(part, rows, da0, da1, dm0, dm1, out_ref):
    lines = block_sums(part, rows, (da0, da1), True) + block_sums(part, rows, (dm0, dm1), False)
    out_ref[...] = jnp.concatenate(lines + [jnp.zeros((4, da0.shape[-1]), F32)], axis=0)


def block_sums(part, rows, refs, extra):
    place = token_place(rows)
    sums = [0.0, 0.0, 0.0]
    for ref in refs:
        for item in range(2):
            v = ref[item].astype(F32)
            sums[0] = sums[0] + jnp.sum(jnp.where(place < part, v, 0.0), axis=0, keepdims=True)
            if extra:
                for i in range(2):
                    at = (place == part + 2 * i) | (place == part + 2 * i + 1)
                    sums[1 + i] = sums[1 + i] + jnp.sum(jnp.where(at, v, 0.0), axis=0, keepdims=True)
    return sums if extra else sums[:1]


def vector_kernel(far, deep, part, rows, xt_ref, dh0, dh1, sums_ref, s0, s1, out_ref):
    lo = lax.axis_index("near") * 2 + lax.axis_index("core")
    width = dh0.shape[-1]
    total = 0.0
    for side, ref in enumerate((dh0, dh1)):
        for item in range(2):
            d = ref[item]
            for i in range(2):
                total = total + nn(xt_ref[4 * side + 2 * item + i], d[i * rows : (i + 1) * rows])
    k = total.shape[0] // far
    lines = block_sums(part, rows, (dh0, dh1), True)
    stacked = jnp.concatenate(lines + [sums_ref[i : i + 1, :] for i in range(5)], axis=0)
    up = s0[...] + s1[...]
    f = up.shape[1] // far
    spare = jnp.zeros((8, width - 2 * f), F32)
    row = lax.broadcasted_iota(jnp.int32, (8, 1), 0)
    for z in range(far):
        cut = 0.0
        for j in range(4):
            at = (z * 4 + j) * deep
            cut = cut + jnp.where(lo == j, stacked[:, at : at + deep], 0.0)
        low = jnp.concatenate((cut, jnp.zeros((8, 2 * f - deep), F32)), axis=1)
        tall = jnp.concatenate((up[:, z * f : (z + 1) * f], jnp.zeros((1, f), F32)), axis=1)
        low = jnp.where(row == 7, tall, low)
        low = jnp.concatenate((low, spare), axis=1)
        out_ref[z] = jnp.concatenate((total[z * k : (z + 1) * k], low), axis=0).astype(BF16)


def two_halves_kernel(mine_ref, other_ref, out_ref):
    seq = lax.axis_index("seq")
    k = mine_ref.shape[1]
    for i in range(2):
        mine, other = mine_ref[i].astype(F32), other_ref[i].astype(F32)
        out_ref[i * k : (i + 1) * k, :] = jnp.where(seq == 0, mine, other)
        out_ref[(2 + i) * k : (3 + i) * k, :] = jnp.where(seq == 0, other, mine)


def last_kernel(k, deep, f, mine_ref, other_ref, out_ref, vec_ref, up_ref):
    seq = lax.axis_index("seq")
    mine, other = mine_ref[...].astype(F32), other_ref[...].astype(F32)
    zero = jnp.where(seq == 0, mine, other)
    one = jnp.where(seq == 0, other, mine)
    out_ref[0:k, :] = zero[:k]
    out_ref[k : 2 * k, :] = one[:k]
    vec_ref[...] = mine[k : k + 8, :deep]
    up_ref[...] = jnp.concatenate((zero[k + 7 : k + 8, :f], one[k + 7 : k + 8, :f]), axis=1)


def columns_kernel(order, got_ref, out_ref):
    got = [got_ref[i].astype(F32) for i in range(8)]
    out_ref[...] = jnp.concatenate([got[2 * lo + s][:, at : at + n] for s, lo, at, n in order], axis=1)


def columns_call(run, order, got, name):
    wide = sum(n for *_, n in order)
    return run(functools.partial(columns_kernel, order), shape((got.shape[1], wide), F32), got, name=name)


def swap(v, *axes):
    return lax.ppermute(v, axes if len(axes) > 1 else axes[0], FLIP4 if len(axes) > 1 else FLIP2)


def send_own(own):
    return own, swap(own, "seq"), swap(own, "near"), swap(own, "near", "seq")


def spread_blocks(run, parts):
    rows, width = parts[0].shape
    quad = run(stack_kernel, shape((4, rows, width), BF16), *parts, name="stack")
    other = swap(quad, "core")
    return quad.reshape(2, 2 * rows, width), other.reshape(2, 2 * rows, width)


def collect_blocks(run, mine, got):
    dims = mine.shape[1:]
    outs = (shape(dims, F32),) + (shape(dims, BF16),) * 3
    own, b, c, d = run(merge_kernel, outs, mine, got, name="merge")
    return own, swap(b, "seq"), swap(c, "near"), swap(d, "near", "seq")


def from_far(v, far):
    return [v] + [lax.ppermute(v, "far", [(i, (i + j) % far) for i in range(far)]) for j in range(1, far)]


def to_far(blocks, far):
    return [blocks[0]] + [
        lax.ppermute(blocks[j], "far", [(i, (i + j) % far) for i in range(far)]) for j in range(1, far)
    ]


def gather_far(v):
    return lax.all_gather(v, "far", axis=0, tiled=False)


def pick(v, at, axis):
    return lax.dynamic_index_in_dim(v, at, axis, keepdims=False)


def body(
    inputs,
    skips,
    cotangent,
    bins,
    bin_weights,
    skip_w,
    skip_b,
    ln1_g,
    ln1_b,
    qkv_w,
    proj_w,
    proj_b,
    ln2_g,
    ln2_b,
    fc1_w,
    fc1_b,
    fc2_w,
    fc2_b,
    *,
    far,
):
    _, part, width = inputs.shape
    rows = -(-part // 8) * 8
    dp = far * 4
    seq = lax.axis_index("seq")
    lo = lax.axis_index("near") * 2 + lax.axis_index("core")
    per = HEADS // 8
    inner = per * HEAD_DIM
    joint = -(-3 * inner // 128) * 128
    deep = width // dp
    k = skip_w.shape[0] // 2
    f = fc2_w.shape[0] // 2
    half, quarter = far // 2, far // 4
    spread = far * k
    one_head = dp == HEADS

    run = Line()

    sent = pack_call(run, inputs[0], skips[0], rows, half, quarter, k)
    got = lax.all_to_all(sent, TEAM, split_axis=0, concat_axis=0, tiled=True)
    small = tuple(v.reshape(1, -1) for v in (fc1_b, skip_b, ln1_g, ln1_b, proj_b, ln2_g, ln2_b, fc2_b))
    skip_half = run(
        skip_half_kernel, shape((k + 8, width), BF16), skip_w, *small, name="skip_half"
    )
    skip_blocks = from_far(skip_half, far)
    columns = run(
        functools.partial(pack_columns_kernel, far, per, joint, f),
        (shape((deep, joint + far * f), BF16),) * 4,
        qkv_w,
        fc1_w,
        name="pack_columns",
    )
    columns = (columns[0], swap(columns[1], "core"), swap(columns[2], "near"), swap(columns[3], "near", "core"))
    qkv_part, rest = run(
        functools.partial(order_columns_kernel, joint),
        (shape((4, deep, joint + width // 3), BF16), shape((4, deep, width), BF16)),
        *columns,
        fc2_w,
        proj_w,
        name="order_columns",
    )
    first = gather_far(qkv_part).reshape(dp, deep, joint + width // 3)
    rest = gather_far(rest).reshape(4 * far, deep, width)
    w_skip, vec, b_up = run(
        functools.partial(order_skip_kernel, deep, f),
        (shape((far, k, width), BF16), shape((8, width), F32), shape((1, far * f), F32)),
        *skip_blocks,
        name="order_skip",
    )
    w_skip = w_skip.reshape(spread, width)

    x1, theirs = skip_call(run, 1, part, half * k, quarter * k, got, w_skip, vec, BF16)
    pair = swap(theirs, "core")
    x0, mine = skip_call(run, 0, part, half * k, quarter * k, got, w_skip, vec, F32)
    come = collect_blocks(run, mine, pair)
    x_turned = run(turn_kernel, shape((8, spread, rows), BF16), x0, x1, name="turn")
    d_wide, d_own = run(
        cot_kernel,
        (shape((rows, width), F32), shape((rows, width), BF16)),
        cotangent[0],
        name="cot",
        scalars=(bins, bin_weights),
    )
    hidden, normed, vec = run(
        norm_first_kernel,
        (shape((rows, width), F32), shape((rows, width), BF16), shape((8, width), F32)),
        *come,
        name="norm",
    )

    parts = send_own(normed)
    n1 = spread_blocks(run, parts)
    w_qkv, w_proj = run(
        split_first_kernel,
        (shape((dp, deep, joint), BF16), shape((far, deep, width), BF16)),
        first,
        name="split_first",
    )
    w_qkv = w_qkv.reshape(width, joint)
    if one_head:
        w_proj = w_proj.reshape(2, inner, width)
    else:
        w_proj = lax.all_gather(proj_w, ("far", "near", "core"), axis=0, tiled=True)
        w_proj = pick(w_proj.reshape(2, per, 4, HEAD_DIM, width), seq, 0)
        w_proj = pick(w_proj, lo, 1).reshape(1, inner, width)
    joined1, mixed1, theirs = attend_call(run, part, n1[1], w_qkv, w_proj, BF16)
    pair = swap(theirs, "core")
    d_parts = send_own(d_own)
    joined0, mixed0, mine = attend_call(run, part, n1[0], w_qkv, w_proj, F32)
    come = collect_blocks(run, mine, pair)
    d_mlp = spread_blocks(run, d_parts)
    middle, second = run(
        norm_second_kernel,
        (shape((rows, width), F32), shape((rows, width), BF16)),
        hidden,
        *come,
        vec,
        name="norm",
    )

    parts = send_own(second)
    n2 = spread_blocks(run, parts)
    w_up, w_down = run(
        functools.partial(split_kernel, far),
        (shape((4 * far, deep, far * f), BF16), shape((2 * far, deep, width), BF16)),
        rest,
        name="split",
    )
    w_up, w_down = w_up.reshape(width, far * f), w_down.reshape(far * f, width)
    act1, du1, s1, theirs = mlp_call(run, n2[1], d_mlp[1], w_up, b_up, w_down, BF16)
    pair = swap(theirs, "core")
    act0, du0, s0, mine = mlp_call(run, n2[0], d_mlp[0], w_up, b_up, w_down, F32)
    come = collect_blocks(run, mine, pair)

    def scatter(v):
        return lax.psum_scatter(v, "far", scatter_dimension=0, tiled=True)

    def to_team(v):
        return lax.all_to_all(v, TEAM, split_axis=0, concat_axis=0, tiled=True)

    g_rest = run(
        functools.partial(product_two_kernel, far),
        shape((far, 4, deep, width), BF16),
        *n2,
        du0,
        du1,
        act0,
        act1,
        *d_mlp,
        name="grad_mlp",
    )
    g_rest = scatter(g_rest.reshape(4 * far, deep, width))
    d_middle, d_branch = norm_back_call(run, 5, part, come, middle, vec, d_wide, True)

    parts = send_own(d_branch)
    out_pair = swap(down_call(run, act1, w_down, BF16), "core")
    out_mine = down_call(run, act0, w_down, F32)
    da = spread_blocks(run, parts)
    out_come = collect_blocks(run, out_mine, out_pair)
    dj1, theirs = attend_back_call(run, part, da[1], joined1, w_qkv, w_proj, BF16)
    pair = swap(theirs, "core")
    dj0, mine = attend_back_call(run, part, da[0], joined0, w_qkv, w_proj, F32)
    come = collect_blocks(run, mine, pair)
    output = run(
        functools.partial(output_kernel, 7), shape((part, width), BF16), middle, *out_come, vec, name="output"
    )
    if one_head:
        g_first = run(
            functools.partial(product_attend_kernel, far),
            shape((far, 4, deep, joint + width // 3), BF16),
            *n1,
            dj0,
            dj1,
            mixed0,
            mixed1,
            *da,
            name="grad_attend",
        )
        g_first = scatter(g_first.reshape(4 * far, deep, -1))
    else:
        g_qkv = scatter(product_call(run, n1, (dj0, dj1), "grad_qkv")).reshape(4, deep, joint)
        g_first = jnp.pad(g_qkv, ((0, 0), (0, 0), (0, width // 3)))
        g_proj = product_call(run, (mixed0, mixed1), da, "grad_proj")
        spot = jnp.zeros((2, per, 4, HEAD_DIM, width), BF16)
        spot = lax.dynamic_update_slice(
            spot, g_proj.reshape(1, per, 1, HEAD_DIM, width), (seq, 0, lo, 0, 0)
        )
        low_own = lax.psum_scatter(
            spot.reshape(width, width), ("far", "near", "core"), scatter_dimension=0, tiled=True
        )
    g_up, g_down = run(
        double_up_kernel,
        (shape((8, deep, far * f), BF16), shape((2, deep, width), BF16)),
        g_rest,
        name="double_up",
    )
    g_up = to_team(g_up)
    down_other = swap(g_down, "seq")
    d_hidden = norm_back_call(run, 2, part, come, hidden, vec, d_middle, False)

    parts = send_own(d_hidden)
    early = run(
        functools.partial(sums_kernel, part, rows), shape((8, width), F32), *da, *d_mlp, name="sums"
    )
    dh = spread_blocks(run, parts)
    g_skip = run(
        functools.partial(vector_kernel, far, deep, part, rows),
        shape((far, k + 8, width), BF16),
        x_turned,
        *dh,
        early,
        s0,
        s1,
        name="grad_skip",
    )
    g_skip = scatter(g_skip.reshape(far * (k + 8), width))
    blocks = tuple(v.reshape(4, rows, width) for v in dh)
    sent = skip_back_call(run, half * k, quarter * k, blocks, w_skip)
    got = lax.all_to_all(sent, TEAM, split_axis=0, concat_axis=0, tiled=True)
    g_qkv, low = run(
        double_qkv_kernel,
        (shape((8, deep, joint), BF16), shape((deep, width), BF16)),
        g_first,
        name="double_qkv",
    )
    g_qkv = to_team(g_qkv)
    if not one_head:
        low = low_own
    low_other = swap(low, "seq")

    order = [(s, j, z * f, f) for z in range(far) for j in range(4) for s in range(2)]
    d_fc1_w = columns_call(run, order, g_up, "whole_up")
    d_inputs, d_skips = unpack_call(run, got, part, half, quarter, k)
    order = [
        (s, j, (b * per + i) * HEAD_DIM, HEAD_DIM)
        for b in range(3)
        for s in range(2)
        for i in range(per)
        for j in range(4)
    ]
    d_qkv_w = columns_call(run, order, g_qkv, "whole_qkv")
    d_fc2_w = run(two_halves_kernel, shape((2 * f, width), F32), g_down, down_other, name="whole_down")
    d_proj_w = run(pair_sum_kernel, shape(low.shape, F32), low, low_other, name="whole_proj")
    d_skip_w, vectors, d_up_b = run(
        functools.partial(last_kernel, k, deep, f),
        (shape((2 * k, width), F32), shape((8, deep), F32), shape((1, 2 * f), F32)),
        g_skip,
        swap(g_skip, "seq"),
        name="whole_skip",
    )
    return (
        output.reshape(1, part, width),
        d_inputs.reshape(1, part, width),
        d_skips.reshape(1, 2 * part, width // 2),
        d_skip_w,
        vectors[0],
        vectors[1],
        vectors[2],
        d_qkv_w,
        d_proj_w,
        vectors[3],
        vectors[4],
        vectors[5],
        d_fc1_w,
        d_up_b.reshape(2 * f),
        d_fc2_w,
        vectors[6],
    )


def solution(mesh):
    dp, seq = mesh.shape["dp"], mesh.shape["seq"]
    far = dp // 4
    fine = Mesh(mesh.devices.reshape(far, 2, 2, seq), ("far", "near", "core", "seq"))
    items = ("far", "near", "core")
    tokens = P(items, "seq", None)
    features = P(items, None, "seq")
    matrix = P(items, None)
    vector = P(items)
    in_specs = (
        tokens,
        features,
        tokens,
        vector,
        P(),
        matrix,
        vector,
        vector,
        vector,
        matrix,
        matrix,
        vector,
        vector,
        vector,
        matrix,
        vector,
        matrix,
        vector,
    )
    out_specs = (
        tokens,
        tokens,
        features,
        matrix,
        vector,
        vector,
        vector,
        matrix,
        matrix,
        vector,
        vector,
        vector,
        matrix,
        vector,
        matrix,
        vector,
    )
    return jax.shard_map(
        functools.partial(body, far=far),
        mesh=fine,
        in_specs=in_specs,
        out_specs=out_specs,
        check_vma=False,
    )
```

```python
import functools

import jax
import jax.numpy as jnp
from jax import lax
from jax.experimental import pallas as pl
from jax.experimental.pallas import tpu as pltpu
from jax.sharding import Mesh, PartitionSpec as P

HEADS = 16
HEAD_DIM = 72
EPS = 1e-05
F32 = jnp.float32
BF16 = jnp.bfloat16
TEAM = ("near", "core", "seq")
WEIGHTS = {"turn": 12, "attend": 12, "grad_mlp": 12, "grad_attend": 12, "down": 20, "sums": 12, "double_up": 20, "skip_half": 8, "pack": 4, "pack_columns": 50, "whole_down": 6, "attend_back1": 3, "norm_back2": 2, "output": 2, "order_skip": 0.5, "merge3": 3, "grad_skip": 0.1, "unpack": 20, "stack4": 0.1, "stack5": 4, "mlp2": 3, "order_columns": 12, "norm_back1": 12, "merge5": 8, "mlp1": 1, "down_part": 0.1}
FLIP2 = [(0, 1), (1, 0)]
FLIP4 = [(0, 3), (1, 2), (2, 1), (3, 0)]


def nn(a, b):
    return lax.dot_general(a, b, (((1,), (0,)), ((), ())), preferred_element_type=F32)


def nt(a, b):
    return lax.dot_general(a, b, (((1,), (1,)), ((), ())), preferred_element_type=F32)


def tn(a, b):
    return lax.dot_general(a, b, (((0,), (0,)), ((), ())), preferred_element_type=F32)


def shape(dims, kind):
    return jax.ShapeDtypeStruct(tuple(dims), kind)


class Line:
    def __init__(self):
        self.word = None
        self.calls = {}

    def __call__(self, kernel, outs, *ops, scratch=(), limit=12, name=None, scalars=()):
        single = not isinstance(outs, tuple)
        outs = (outs,) if single else outs
        spec = pl.BlockSpec(memory_space=pltpu.VMEM)
        n, m = len(ops) + len(scalars), len(outs)
        late = () if self.word is None else (self.word,)
        count = self.calls[name] = self.calls.get(name, 0) + 1
        weight = WEIGHTS.get(f"{name}{count}", WEIGHTS.get(name, 0.1))

        def call(*refs):
            ins, rest = refs[:n], refs[n + len(late) :]
            rest[m][...] = jnp.zeros_like(rest[m])
            kernel(*ins, *rest[:m], *rest[m + 1 :])

        *results, self.word = pl.pallas_call(
            call,
            out_shape=outs + (jax.ShapeDtypeStruct((8, 128), F32),),
            in_specs=[spec] * len(ops)
            + [pl.BlockSpec(memory_space=pltpu.SMEM)] * len(scalars)
            + [pl.BlockSpec(memory_space=pl.ANY)] * len(late),
            out_specs=(spec,) * (m + 1),
            scratch_shapes=list(scratch),
            cost_estimate=pl.CostEstimate(flops=int(weight * 1e9), bytes_accessed=1000, transcendentals=0),
            compiler_params=pltpu.CompilerParams(vmem_limit_bytes=limit * 1024 * 1024),
            name=name,
        )(*ops, *scalars, *late)
        return results[0] if single else tuple(results)


def pack_kernel(half, quarter, k, x_ref, s_ref, out_ref, wide, tall):
    part = x_ref.shape[0]
    x = x_ref[...].astype(F32)
    wide[0 : 2 * part, :] = s_ref[...].astype(F32)
    first, second = wide[0:part, :], wide[part : 2 * part, :]
    tall[part:, :] = jnp.zeros((tall.shape[0] - part, tall.shape[1]), F32)
    for r in range(8):
        pieces = [
            src[:, (j * 8 + r) * k : (j * 8 + r + 1) * k]
            for src, n in ((x, half), (first, quarter), (second, quarter))
            for j in range(n)
        ]
        tall[0:part, :] = jnp.concatenate(pieces, axis=1)
        out_ref[r] = tall[...].astype(BF16)


def pack_call(run, x, s, rows, half, quarter, k):
    deep = 2 * half * k
    return run(
        functools.partial(pack_kernel, half, quarter, k),
        shape((8, rows, deep), BF16),
        x,
        s,
        scratch=[pltpu.VMEM((s.shape[0], s.shape[1]), F32), pltpu.VMEM((rows, deep), F32)],
        name="pack",
    )


def skip_half_kernel(w_ref, *refs):
    *small, out_ref = refs
    k = w_ref.shape[0] // 2
    w = w_ref[...].astype(F32)
    w = jnp.where(lax.axis_index("seq") == 0, w[:k], w[k:])
    line = [ref[...].astype(F32) for ref in small]
    line.append(jnp.zeros((1, w.shape[1] - sum(v.shape[1] for v in line)), F32))
    line = jnp.concatenate(line, axis=1)
    line = jnp.where(lax.broadcasted_iota(jnp.int32, (8, 1), 0) == 0, line, 0.0)
    out_ref[...] = jnp.concatenate((w, line), axis=0).astype(BF16)


def lo_index():
    return lax.axis_index("near") * 2 + lax.axis_index("core")


def choose(at, values):
    out = values[0]
    for i in range(1, len(values)):
        out = jnp.where(at == i, values[i], out)
    return out


def pack_columns_kernel(far, per, joint, f, qkv_ref, up_ref, *outs):
    seq = lax.axis_index("seq")
    lo = lo_index()
    w, up = qkv_ref[...].astype(F32), up_ref[...].astype(F32)
    deep, width = w.shape[0], w.shape[1] // 3
    spare = jnp.zeros((deep, joint - 3 * per * HEAD_DIM), F32)
    blocks = []
    for j in range(4):
        both = []
        for s in range(2):
            heads = [
                w[:, at : at + HEAD_DIM]
                for b in range(3)
                for i in range(per)
                for at in (b * width + ((s * per + i) * 4 + j) * HEAD_DIM,)
            ]
            hidden = [up[:, at : at + f] for z in range(far) for at in (((z * 4 + j) * 2 + s) * f,)]
            both.append(jnp.concatenate(heads + [spare] + hidden, axis=1))
        blocks.append(jnp.where(seq == 0, both[0], both[1]))
    for j, out in enumerate(outs):
        out[...] = choose(lax.bitwise_xor(lo, j), blocks).astype(BF16)


def order_columns_kernel(joint, own, a, b, c, down_ref, proj_ref, qkv_ref, rest_ref):
    lo = lo_index()
    got = [ref[...].astype(F32) for ref in (own, a, b, c)]
    deep = got[0].shape[0]
    blocks = [choose(lax.bitwise_xor(lo, j), got) for j in range(4)]
    third = proj_ref.shape[1] // 3
    for j in range(4):
        qkv_ref[j, :, :joint] = blocks[j][:, :joint].astype(BF16)
        if j < 3:
            qkv_ref[j, :, joint:] = proj_ref[:, j * third : (j + 1) * third]
        else:
            qkv_ref[j, :, joint:] = jnp.zeros((deep, third), BF16)
    down = down_ref[...].astype(F32)
    down = jnp.where(lax.axis_index("seq") == 0, down[: 2 * deep], down[2 * deep :])
    for i in range(2):
        up = jnp.concatenate((blocks[i][:, joint:], blocks[2 + i][:, joint:]), axis=1)
        rest_ref[i] = up.astype(BF16)
        rest_ref[2 + i] = down[i * deep : (i + 1) * deep].astype(BF16)


def split_first_kernel(got_ref, qkv_ref, proj_ref):
    joint = qkv_ref.shape[2]
    third = got_ref.shape[2] - joint
    for g in range(got_ref.shape[0]):
        qkv_ref[g] = got_ref[g, :, :joint]
        if g % 4 < 3:
            proj_ref[g // 4, :, (g % 4) * third : (g % 4 + 1) * third] = got_ref[g, :, joint:]


def split_kernel(far, got_ref, up_ref, down_ref):
    for z in range(far):
        for i in range(2):
            pair = got_ref[4 * z + i].astype(F32)
            n = pair.shape[1] // 2
            up_ref[4 * z + i] = pair[:, :n].astype(BF16)
            up_ref[4 * z + 2 + i] = pair[:, n:].astype(BF16)
            down_ref[2 * z + i] = got_ref[4 * z + 2 + i]


def order_skip_kernel(deep, lo_f, *refs):
    *blocks, w_ref, vec_ref, up_ref = refs
    n = len(blocks)
    k = w_ref.shape[1]
    far, lo, seq = lax.axis_index("far"), lo_index(), lax.axis_index("seq")
    got = [ref[...].astype(F32) for ref in blocks]
    for j, v in enumerate(got):
        w_ref[lax.rem(far - j + n, n)] = v[:k].astype(BF16)
    lines = [choose(lax.rem(far - z + n, n), [v[k : k + 1] for v in got]) for z in range(n)]
    up_ref[...] = jnp.concatenate(
        [jnp.where(seq == 0, v[:, :lo_f], v[:, lo_f : 2 * lo_f]) for v in lines], axis=1
    )
    pieces = []
    for v in lines:
        tall = [v[:, 2 * lo_f + i * deep : 2 * lo_f + (i + 1) * deep] for i in range(7)]
        tall = jnp.concatenate([jnp.zeros_like(tall[0])] + tall, axis=0)
        pieces += [jnp.where((lo == j) & (seq == 0), tall, 0.0) for j in range(4)]
    vec_ref[...] = jnp.concatenate(pieces, axis=1)


def unpack_kernel(half, quarter, k, got_ref, x_ref, s_ref, wide):
    part = x_ref.shape[0]
    got = [got_ref[r, 0:part, :].astype(F32) for r in range(8)]
    x_ref[...] = jnp.concatenate(
        [got[r][:, j * k : (j + 1) * k] for j in range(half) for r in range(8)], axis=1
    ).astype(BF16)
    for t in range(2):
        base = half + t * quarter
        wide[t * part : (t + 1) * part, :] = jnp.concatenate(
            [got[r][:, (base + j) * k : (base + j + 1) * k] for j in range(quarter) for r in range(8)],
            axis=1,
        )
    s_ref[...] = wide[...].astype(BF16)


def unpack_call(run, got, part, half, quarter, k):
    width = 8 * half * k
    return run(
        functools.partial(unpack_kernel, half, quarter, k),
        (shape((part, width), BF16), shape((2 * part, width // 2), BF16)),
        got,
        scratch=[pltpu.VMEM((2 * part, width // 2), F32)],
        name="unpack",
    )


def halves(h, q, a, b):
    zero = jnp.concatenate((a[:, :h], a[:, h : h + q], b[:, h : h + q]), axis=1)
    one = jnp.concatenate((b[:, :h], a[:, h + q :], b[:, h + q :]), axis=1)
    return zero, one


def skip_kernel(side, part, h, q, got_ref, w_ref, vec_ref, x_ref, out_ref):
    near, core, seq = (lax.axis_index(name) for name in TEAM)
    real = lax.broadcasted_iota(jnp.int32, (got_ref.shape[1], 1), 0) < part
    for fn in range(2):
        base = lax.bitwise_xor(near, fn) * 4 + lax.bitwise_xor(core, side) * 2
        zero, one = halves(h, q, got_ref[base].astype(F32), got_ref[base + 1].astype(F32))
        mine = jnp.where(seq == 0, zero, one)
        other = jnp.where(seq == 0, one, zero)
        for i, x in enumerate((mine, other)):
            x = jnp.where(real, x, 0.0).astype(BF16)
            x_ref[2 * fn + i] = x
            out = nn(x, w_ref[...])
            base = out.shape[0] - 8
            out = jnp.concatenate((out[:base], out[base:] + vec_ref[...]), axis=0)
            out_ref[2 * fn + i] = out.astype(out_ref.dtype)


def skip_call(run, side, part, h, q, got, w, vec, kind):
    _, rows, deep = got.shape
    return run(
        functools.partial(skip_kernel, side, part, h, q),
        (shape((4, rows, deep), BF16), shape((4, rows, w.shape[1]), kind)),
        got,
        w,
        vec,
        name="skip",
    )


def turn_kernel(x0_ref, x1_ref, out_ref):
    for i, ref in enumerate((x0_ref, x1_ref)):
        for j in range(4):
            out_ref[4 * i + j] = ref[j].astype(F32).T.astype(BF16)


def skip_back_kernel(h, q, d0_ref, d1_ref, w_ref, out_ref):
    near, core, seq = (lax.axis_index(name) for name in TEAM)
    for side, d_ref in enumerate((d0_ref, d1_ref)):
        for fn in range(2):
            base = lax.bitwise_xor(near, fn) * 4 + lax.bitwise_xor(core, side) * 2
            mine = nt(d_ref[2 * fn], w_ref[...])
            other = nt(d_ref[2 * fn + 1], w_ref[...])
            zero = jnp.where(seq == 0, mine, other)
            one = jnp.where(seq == 0, other, mine)
            out_ref[base] = jnp.concatenate(
                (zero[:, :h], zero[:, h : h + q], one[:, h : h + q]), axis=1
            ).astype(BF16)
            out_ref[base + 1] = jnp.concatenate(
                (one[:, :h], zero[:, h + q :], one[:, h + q :]), axis=1
            ).astype(BF16)


def skip_back_call(run, h, q, dh, w):
    rows = dh[0].shape[1]
    return run(
        functools.partial(skip_back_kernel, h, q),
        shape((8, rows, w.shape[0]), BF16),
        dh[0],
        dh[1],
        w,
        name="skip_back",
    )


def merge_kernel(mine_ref, got_ref, own_ref, *outs):
    own_ref[...] = mine_ref[0] + got_ref[0].astype(F32)
    for i, out in enumerate(outs):
        out[...] = (mine_ref[i + 1] + got_ref[i + 1].astype(F32)).astype(BF16)


def stack_kernel(a, b, c, d, out_ref):
    for i, ref in enumerate((a, b, c, d)):
        out_ref[i] = ref[...]


def arrived(own_ref, others):
    total = own_ref[...]
    for ref in others:
        total = total + ref[...].astype(F32)
    return total


def normalized(total, gain, shift):
    center = total - jnp.mean(total, axis=-1, keepdims=True)
    spread = jnp.mean(center * center, axis=-1, keepdims=True)
    return (center * lax.rsqrt(spread + EPS) * gain + shift).astype(BF16)


def norm_first_kernel(own, b, c, d, total_ref, normed_ref, vec_ref):
    total = arrived(own, (b, c, d))
    vec_ref[...] = total[total.shape[0] - 8 :]
    bias, gain, shift = (vec_ref[i : i + 1, :] for i in (1, 2, 3))
    total = total + bias
    total_ref[...] = total
    normed_ref[...] = normalized(total, gain, shift)


def norm_second_kernel(base, own, b, c, d, vec_ref, total_ref, normed_ref):
    bias, gain, shift = (vec_ref[i : i + 1, :] for i in (4, 5, 6))
    total = arrived(own, (b, c, d)) + bias + base[...]
    total_ref[...] = total
    normed_ref[...] = normalized(total, gain, shift)


def norm_back_kernel(place, part, own, b, c, d, total_ref, vec_ref, resid, wide_ref, low_ref):
    grad = arrived(own, (b, c, d))
    gain = vec_ref[place : place + 1, :]
    center = total_ref[...] - jnp.mean(total_ref[...], axis=-1, keepdims=True)
    spread = jnp.mean(center * center, axis=-1, keepdims=True)
    scale = lax.rsqrt(spread + EPS)
    unit = center * scale
    inner = grad * gain
    back = inner - jnp.mean(inner, axis=-1, keepdims=True)
    back = (back - unit * jnp.mean(inner * unit, axis=-1, keepdims=True)) * scale
    wide = resid[...] + back
    if wide_ref is not None:
        wide_ref[...] = wide
    d_gain = jnp.sum(grad * unit, axis=0, keepdims=True)
    d_shift = jnp.sum(grad, axis=0, keepdims=True)
    row = lax.broadcasted_iota(jnp.int32, (wide.shape[0], 1), 0)
    wide = jnp.where(row < part, wide, 0.0)
    for i, v in enumerate((d_gain, d_shift)):
        high = v.astype(BF16).astype(F32)
        wide = jnp.where(row == part + 2 * i, high, wide)
        wide = jnp.where(row == part + 2 * i + 1, v - high, wide)
    low_ref[...] = wide.astype(BF16)


def norm_back_last(place, part, own, b, c, d, total, vec, resid, low_ref):
    norm_back_kernel(place, part, own, b, c, d, total, vec, resid, None, low_ref)


def norm_back_call(run, place, part, parts, total, vec, resid, both):
    low = shape(total.shape, BF16)
    body = functools.partial(norm_back_kernel if both else norm_back_last, place, part)
    outs = (shape(total.shape, F32), low) if both else low
    return run(body, outs, *parts, total, vec, resid, name="norm_back")


def cot_kernel(cot_ref, bins_ref, weights_ref, wide_ref, low_ref):
    part = cot_ref.shape[0]
    wide_ref[...] = jnp.zeros_like(wide_ref)
    wide_ref[0:part, :] = cot_ref[...].astype(F32) * weights_ref[bins_ref[0]]
    low_ref[...] = wide_ref[...].astype(BF16)


def token_place(rows):
    place = lax.broadcasted_iota(jnp.int32, (2 * rows, 1), 0)
    return jnp.where(place >= rows, place - rows, place)


def head_masks(width):
    lane = lax.broadcasted_iota(jnp.int32, (1, width), 1)
    return [
        jnp.where((lane >= i * HEAD_DIM) & (lane < (i + 1) * HEAD_DIM), 1.0, 0.0).astype(BF16)
        for i in range(width // HEAD_DIM)
    ]


def probs_of(k, q, bias):
    scores = nt(k, q) * (HEAD_DIM**-0.5) + bias
    expo = jnp.exp(scores - jnp.max(scores, axis=0, keepdims=True))
    return expo * (1.0 / jnp.sum(expo, axis=0, keepdims=True))


def split3(v, width):
    return (v[:, i * width : (i + 1) * width] for i in range(3))


def attend_kernel(part, x_ref, qkv_ref, proj_ref, joined_ref, mixed_ref, out_ref):
    rows = out_ref.shape[1]
    seq = lax.axis_index("seq") if proj_ref.shape[0] > 1 else 0
    real = token_place(rows) < part
    bias = jnp.where(real, 0.0, -1e30).astype(F32)

    @pl.loop(0, x_ref.shape[0])
    def _(item):
        joined = nn(x_ref[item], qkv_ref[...]).astype(BF16)
        joined_ref[item] = joined
        q, k, v = split3(joined, mixed_ref.shape[2])
        mixed = None
        for mask in head_masks(q.shape[1]):
            probs = probs_of(k, q * mask, bias).astype(BF16)
            term = tn(probs, v * mask)
            mixed = term if mixed is None else mixed + term
        mixed = jnp.where(real, mixed, 0.0).astype(BF16)
        mixed_ref[item] = mixed
        out = nn(mixed, proj_ref[seq])
        out_ref[2 * item] = out[:rows].astype(out_ref.dtype)
        out_ref[2 * item + 1] = out[rows:].astype(out_ref.dtype)


def attend_call(run, part, x, w_qkv, w_proj, kind):
    items, rows, width = x.shape
    inner = w_proj.shape[1]
    return run(
        functools.partial(attend_kernel, part),
        (
            shape((items, rows, w_qkv.shape[1]), BF16),
            shape((items, rows, inner), BF16),
            shape((2 * items, rows // 2, width), kind),
        ),
        x,
        w_qkv,
        w_proj,
        name="attend",
    )


def attend_back_kernel(part, d_ref, joined_ref, qkv_ref, proj_ref, grads_ref, out_ref):
    rows = out_ref.shape[1]
    real = token_place(rows) < part
    bias = jnp.where(real, 0.0, -1e30).astype(F32)
    factor = HEAD_DIM**-0.5
    seq = lax.axis_index("seq") if proj_ref.shape[0] > 1 else 0

    @pl.loop(0, d_ref.shape[0])
    def _(item):
        d_mixed = nt(d_ref[item], proj_ref[seq])
        d_mixed = jnp.where(real, d_mixed, 0.0).astype(BF16)
        q, k, v = split3(joined_ref[item], proj_ref.shape[1])
        d_q = d_k = d_v = 0.0
        for mask in head_masks(q.shape[1]):
            probs = probs_of(k, q * mask, bias)
            d_one = d_mixed * mask
            d_v = d_v + nn(probs.astype(BF16), d_one)
            d_probs = nt(v, d_one)
            inner = jnp.sum(d_probs * probs, axis=0, keepdims=True)
            d_scores = (probs * (d_probs - inner)).astype(BF16)
            d_k = d_k + nn(d_scores, q * mask)
            d_q = d_q + tn(d_scores, k * mask)
        spare = jnp.zeros((2 * rows, grads_ref.shape[2] - 3 * d_v.shape[1]), F32)
        grads = jnp.concatenate((d_q * factor, d_k * factor, d_v, spare), axis=1).astype(BF16)
        grads_ref[item] = grads
        out = nt(grads, qkv_ref[...])
        out_ref[2 * item] = out[:rows].astype(out_ref.dtype)
        out_ref[2 * item + 1] = out[rows:].astype(out_ref.dtype)


def attend_back_call(run, part, d, joined, w_qkv, w_proj, kind):
    items, rows, width = d.shape
    return run(
        functools.partial(attend_back_kernel, part),
        (shape(joined.shape, BF16), shape((2 * items, rows // 2, width), kind)),
        d,
        joined,
        w_qkv,
        w_proj,
        name="attend_back",
    )


def mlp_kernel(x_ref, d_ref, up_ref, bias_ref, down_ref, act_ref, grad_ref, sum_ref, out_ref):
    rows = out_ref.shape[1]
    sum_ref[...] = jnp.zeros_like(sum_ref)

    @pl.loop(0, x_ref.shape[0])
    def _(item):
        upper = nn(x_ref[item], up_ref[...]) + bias_ref[...]
        bell = 0.5 * (1.0 + lax.erf(upper * (0.5**0.5)))
        act_ref[item] = (upper * bell).astype(BF16)
        slope = bell + upper * jnp.exp(-0.5 * upper * upper) * 0.3989422804014327
        d_upper = (slope * nt(d_ref[item], down_ref[...])).astype(BF16)
        grad_ref[item] = d_upper
        sum_ref[...] += jnp.sum(d_upper.astype(F32), axis=0, keepdims=True)
        out = nt(d_upper, up_ref[...])
        out_ref[2 * item] = out[:rows].astype(out_ref.dtype)
        out_ref[2 * item + 1] = out[rows:].astype(out_ref.dtype)


def mlp_call(run, x, d, w_up, b_up, w_down, kind):
    items, rows, width = x.shape
    inner = w_up.shape[1]
    return run(
        mlp_kernel,
        (
            shape((items, rows, inner), BF16),
            shape((items, rows, inner), BF16),
            shape((1, inner), F32),
            shape((2 * items, rows // 2, width), kind),
        ),
        x,
        d,
        w_up,
        b_up,
        w_down,
        name="mlp",
    )


def down_kernel(act_ref, w_ref, out_ref):
    rows = out_ref.shape[1]

    @pl.loop(0, act_ref.shape[0])
    def _(item):
        out = nn(act_ref[item], w_ref[...])
        out_ref[2 * item] = out[:rows].astype(out_ref.dtype)
        out_ref[2 * item + 1] = out[rows:].astype(out_ref.dtype)


def down_call(run, act, w, kind):
    items, rows, _ = act.shape
    dims = (2 * items, rows // 2, w.shape[1])
    return run(down_kernel, shape(dims, kind), act, w, name="down")


def output_kernel(place, base, own, b, c, d, vec_ref, out_ref):
    total = base[...] + arrived(own, (b, c, d)) + vec_ref[place : place + 1, :]
    out_ref[...] = total[: out_ref.shape[0]].astype(BF16)


def product_kernel(*refs):
    *sides, out_ref = refs
    total = 0.0
    n = len(sides) // 2
    for left, right in zip(sides[:n], sides[n:]):
        for item in range(left.shape[0]):
            total = total + tn(left[item], right[item])
    out_ref[...] = total.astype(BF16)


def product_call(run, left, right, name):
    dims = (left[0].shape[-1], right[0].shape[-1])
    return run(product_kernel, shape(dims, BF16), *left, *right, name=name)


def product_two_kernel(far, n20, n21, du0, du1, act0, act1, dm0, dm1, out_ref):
    def product(pairs):
        total = 0.0
        for left, right in pairs:
            for item in range(2):
                total = total + tn(left[item], right[item])
        return total

    deep = out_ref.shape[2]
    down = product(((act0, dm0), (act1, dm1)))
    for z in range(far):
        for i in range(2):
            at = (2 * z + i) * deep
            out_ref[z, 2 + i] = down[at : at + deep].astype(BF16)
    up = product(((n20, du0), (n21, du1)))
    for z in range(far):
        for i in range(2):
            at = (4 * z + i) * deep
            pair = (up[at : at + deep], up[at + 2 * deep : at + 3 * deep])
            out_ref[z, i] = jnp.concatenate(pair, axis=1).astype(BF16)


def product_attend_kernel(far, n10, n11, dj0, dj1, a0, a1, d0, d1, out_ref):
    def product(pairs):
        total = 0.0
        for left, right in pairs:
            for item in range(2):
                total = total + tn(left[item], right[item])
        return total

    deep, joint = out_ref.shape[2], dj0.shape[2]
    third = out_ref.shape[3] - joint
    qkv = product(((n10, dj0), (n11, dj1)))
    for z in range(far):
        for j in range(4):
            at = (4 * z + j) * deep
            out_ref[z, j, :, :joint] = qkv[at : at + deep].astype(BF16)
    proj = product(((a0, d0), (a1, d1)))
    seq = lax.axis_index("seq")
    for z in range(far):
        at = z % 2 * deep
        rows = jnp.where(seq == z // 2, proj[at : at + deep], 0.0).astype(BF16)
        for j in range(4):
            cut = rows[:, j * third : (j + 1) * third] if j < 3 else jnp.zeros((deep, third), BF16)
            out_ref[z, j, :, joint:] = cut


def double_up_kernel(got_ref, up_ref, down_ref):
    n = up_ref.shape[2]
    for j in range(4):
        v = got_ref[j % 2].astype(F32)[:, (j // 2) * n : (j // 2 + 1) * n].astype(BF16)
        up_ref[2 * j] = v
        up_ref[2 * j + 1] = v
    for i in range(2):
        down_ref[i] = got_ref[2 + i]


def double_qkv_kernel(got_ref, qkv_ref, proj_ref):
    joint = qkv_ref.shape[2]
    third = got_ref.shape[2] - joint
    for j in range(4):
        v = got_ref[j, :, :joint]
        qkv_ref[2 * j] = v
        qkv_ref[2 * j + 1] = v
        if j < 3:
            proj_ref[:, j * third : (j + 1) * third] = got_ref[j, :, joint:]


def pair_sum_kernel(a_ref, b_ref, out_ref):
    out_ref[...] = a_ref[...].astype(F32) + b_ref[...].astype(F32)


def sums_kernel(part, rows, da0, da1, dm0, dm1, out_ref):
    lines = block_sums(part, rows, (da0, da1), True) + block_sums(part, rows, (dm0, dm1), False)
    out_ref[...] = jnp.concatenate(lines + [jnp.zeros((4, da0.shape[-1]), F32)], axis=0)


def block_sums(part, rows, refs, extra):
    place = token_place(rows)
    sums = [0.0, 0.0, 0.0]
    for ref in refs:
        for item in range(2):
            v = ref[item].astype(F32)
            sums[0] = sums[0] + jnp.sum(jnp.where(place < part, v, 0.0), axis=0, keepdims=True)
            if extra:
                for i in range(2):
                    at = (place == part + 2 * i) | (place == part + 2 * i + 1)
                    sums[1 + i] = sums[1 + i] + jnp.sum(jnp.where(at, v, 0.0), axis=0, keepdims=True)
    return sums if extra else sums[:1]


def vector_kernel(far, deep, part, rows, xt_ref, dh0, dh1, sums_ref, s0, s1, out_ref):
    lo = lax.axis_index("near") * 2 + lax.axis_index("core")
    width = dh0.shape[-1]
    total = 0.0
    for side, ref in enumerate((dh0, dh1)):
        for item in range(2):
            d = ref[item]
            for i in range(2):
                total = total + nn(xt_ref[4 * side + 2 * item + i], d[i * rows : (i + 1) * rows])
    k = total.shape[0] // far
    lines = block_sums(part, rows, (dh0, dh1), True)
    stacked = jnp.concatenate(lines + [sums_ref[i : i + 1, :] for i in range(5)], axis=0)
    up = s0[...] + s1[...]
    f = up.shape[1] // far
    spare = jnp.zeros((8, width - 2 * f), F32)
    row = lax.broadcasted_iota(jnp.int32, (8, 1), 0)
    for z in range(far):
        cut = 0.0
        for j in range(4):
            at = (z * 4 + j) * deep
            cut = cut + jnp.where(lo == j, stacked[:, at : at + deep], 0.0)
        low = jnp.concatenate((cut, jnp.zeros((8, 2 * f - deep), F32)), axis=1)
        tall = jnp.concatenate((up[:, z * f : (z + 1) * f], jnp.zeros((1, f), F32)), axis=1)
        low = jnp.where(row == 7, tall, low)
        low = jnp.concatenate((low, spare), axis=1)
        out_ref[z] = jnp.concatenate((total[z * k : (z + 1) * k], low), axis=0).astype(BF16)


def two_halves_kernel(mine_ref, other_ref, out_ref):
    seq = lax.axis_index("seq")
    k = mine_ref.shape[1]
    for i in range(2):
        mine, other = mine_ref[i].astype(F32), other_ref[i].astype(F32)
        out_ref[i * k : (i + 1) * k, :] = jnp.where(seq == 0, mine, other)
        out_ref[(2 + i) * k : (3 + i) * k, :] = jnp.where(seq == 0, other, mine)


def last_kernel(k, deep, f, mine_ref, other_ref, out_ref, vec_ref, up_ref):
    seq = lax.axis_index("seq")
    mine, other = mine_ref[...].astype(F32), other_ref[...].astype(F32)
    zero = jnp.where(seq == 0, mine, other)
    one = jnp.where(seq == 0, other, mine)
    out_ref[0:k, :] = zero[:k]
    out_ref[k : 2 * k, :] = one[:k]
    vec_ref[...] = mine[k : k + 8, :deep]
    up_ref[...] = jnp.concatenate((zero[k + 7 : k + 8, :f], one[k + 7 : k + 8, :f]), axis=1)


def columns_kernel(order, got_ref, out_ref):
    got = [got_ref[i].astype(F32) for i in range(8)]
    out_ref[...] = jnp.concatenate([got[2 * lo + s][:, at : at + n] for s, lo, at, n in order], axis=1)


def columns_call(run, order, got, name):
    wide = sum(n for *_, n in order)
    return run(functools.partial(columns_kernel, order), shape((got.shape[1], wide), F32), got, name=name)


def swap(v, *axes):
    return lax.ppermute(v, axes if len(axes) > 1 else axes[0], FLIP4 if len(axes) > 1 else FLIP2)


def send_own(own):
    return own, swap(own, "seq"), swap(own, "near"), swap(own, "near", "seq")


def spread_blocks(run, parts):
    rows, width = parts[0].shape
    quad = run(stack_kernel, shape((4, rows, width), BF16), *parts, name="stack")
    other = swap(quad, "core")
    return quad.reshape(2, 2 * rows, width), other.reshape(2, 2 * rows, width)


def collect_blocks(run, mine, got):
    dims = mine.shape[1:]
    outs = (shape(dims, F32),) + (shape(dims, BF16),) * 3
    own, b, c, d = run(merge_kernel, outs, mine, got, name="merge")
    return own, swap(b, "seq"), swap(c, "near"), swap(d, "near", "seq")


def from_far(v, far):
    return [v] + [lax.ppermute(v, "far", [(i, (i + j) % far) for i in range(far)]) for j in range(1, far)]


def to_far(blocks, far):
    return [blocks[0]] + [
        lax.ppermute(blocks[j], "far", [(i, (i + j) % far) for i in range(far)]) for j in range(1, far)
    ]


def gather_far(v):
    return lax.all_gather(v, "far", axis=0, tiled=False)


def pick(v, at, axis):
    return lax.dynamic_index_in_dim(v, at, axis, keepdims=False)


def body(
    inputs,
    skips,
    cotangent,
    bins,
    bin_weights,
    skip_w,
    skip_b,
    ln1_g,
    ln1_b,
    qkv_w,
    proj_w,
    proj_b,
    ln2_g,
    ln2_b,
    fc1_w,
    fc1_b,
    fc2_w,
    fc2_b,
    *,
    far,
):
    _, part, width = inputs.shape
    rows = -(-part // 8) * 8
    dp = far * 4
    seq = lax.axis_index("seq")
    lo = lax.axis_index("near") * 2 + lax.axis_index("core")
    per = HEADS // 8
    inner = per * HEAD_DIM
    joint = -(-3 * inner // 128) * 128
    deep = width // dp
    k = skip_w.shape[0] // 2
    f = fc2_w.shape[0] // 2
    half, quarter = far // 2, far // 4
    spread = far * k
    one_head = dp == HEADS

    run = Line()

    sent = pack_call(run, inputs[0], skips[0], rows, half, quarter, k)
    got = lax.all_to_all(sent, TEAM, split_axis=0, concat_axis=0, tiled=True)
    small = tuple(v.reshape(1, -1) for v in (fc1_b, skip_b, ln1_g, ln1_b, proj_b, ln2_g, ln2_b, fc2_b))
    skip_half = run(
        skip_half_kernel, shape((k + 8, width), BF16), skip_w, *small, name="skip_half"
    )
    skip_blocks = from_far(skip_half, far)
    columns = run(
        functools.partial(pack_columns_kernel, far, per, joint, f),
        (shape((deep, joint + far * f), BF16),) * 4,
        qkv_w,
        fc1_w,
        name="pack_columns",
    )
    columns = (columns[0], swap(columns[1], "core"), swap(columns[2], "near"), swap(columns[3], "near", "core"))
    qkv_part, rest = run(
        functools.partial(order_columns_kernel, joint),
        (shape((4, deep, joint + width // 3), BF16), shape((4, deep, width), BF16)),
        *columns,
        fc2_w,
        proj_w,
        name="order_columns",
    )
    first = gather_far(qkv_part).reshape(dp, deep, joint + width // 3)
    rest = gather_far(rest).reshape(4 * far, deep, width)
    w_skip, vec, b_up = run(
        functools.partial(order_skip_kernel, deep, f),
        (shape((far, k, width), BF16), shape((8, width), F32), shape((1, far * f), F32)),
        *skip_blocks,
        name="order_skip",
    )
    w_skip = w_skip.reshape(spread, width)

    x1, theirs = skip_call(run, 1, part, half * k, quarter * k, got, w_skip, vec, BF16)
    pair = swap(theirs, "core")
    x0, mine = skip_call(run, 0, part, half * k, quarter * k, got, w_skip, vec, F32)
    come = collect_blocks(run, mine, pair)
    x_turned = run(turn_kernel, shape((8, spread, rows), BF16), x0, x1, name="turn")
    d_wide, d_own = run(
        cot_kernel,
        (shape((rows, width), F32), shape((rows, width), BF16)),
        cotangent[0],
        name="cot",
        scalars=(bins, bin_weights),
    )
    hidden, normed, vec = run(
        norm_first_kernel,
        (shape((rows, width), F32), shape((rows, width), BF16), shape((8, width), F32)),
        *come,
        name="norm",
    )

    parts = send_own(normed)
    n1 = spread_blocks(run, parts)
    w_qkv, w_proj = run(
        split_first_kernel,
        (shape((dp, deep, joint), BF16), shape((far, deep, width), BF16)),
        first,
        name="split_first",
    )
    w_qkv = w_qkv.reshape(width, joint)
    if one_head:
        w_proj = w_proj.reshape(2, inner, width)
    else:
        w_proj = lax.all_gather(proj_w, ("far", "near", "core"), axis=0, tiled=True)
        w_proj = pick(w_proj.reshape(2, per, 4, HEAD_DIM, width), seq, 0)
        w_proj = pick(w_proj, lo, 1).reshape(1, inner, width)
    joined1, mixed1, theirs = attend_call(run, part, n1[1], w_qkv, w_proj, BF16)
    pair = swap(theirs, "core")
    d_parts = send_own(d_own)
    joined0, mixed0, mine = attend_call(run, part, n1[0], w_qkv, w_proj, F32)
    come = collect_blocks(run, mine, pair)
    d_mlp = spread_blocks(run, d_parts)
    middle, second = run(
        norm_second_kernel,
        (shape((rows, width), F32), shape((rows, width), BF16)),
        hidden,
        *come,
        vec,
        name="norm",
    )

    parts = send_own(second)
    w_up, w_down = run(
        functools.partial(split_kernel, far),
        (shape((4 * far, deep, far * f), BF16), shape((2 * far, deep, width), BF16)),
        rest,
        name="split",
    )
    w_up, w_down = w_up.reshape(width, far * f), w_down.reshape(far * f, width)
    n2 = spread_blocks(run, parts)
    act1, du1, s1, theirs = mlp_call(run, n2[1], d_mlp[1], w_up, b_up, w_down, BF16)
    pair = swap(theirs, "core")
    act0, du0, s0, mine = mlp_call(run, n2[0], d_mlp[0], w_up, b_up, w_down, F32)
    come = collect_blocks(run, mine, pair)

    def scatter(v):
        return lax.psum_scatter(v, "far", scatter_dimension=0, tiled=True)

    def to_team(v):
        return lax.all_to_all(v, TEAM, split_axis=0, concat_axis=0, tiled=True)

    g_rest = run(
        functools.partial(product_two_kernel, far),
        shape((far, 4, deep, width), BF16),
        *n2,
        du0,
        du1,
        act0,
        act1,
        *d_mlp,
        name="grad_mlp",
    )
    g_rest = scatter(g_rest.reshape(4 * far, deep, width))
    d_middle, d_branch = norm_back_call(run, 5, part, come, middle, vec, d_wide, True)

    parts = send_own(d_branch)
    out_pair = swap(down_call(run, act1, w_down, BF16), "core")
    out_mine = down_call(run, act0, w_down, F32)
    da = spread_blocks(run, parts)
    out_come = collect_blocks(run, out_mine, out_pair)
    dj1, theirs = attend_back_call(run, part, da[1], joined1, w_qkv, w_proj, BF16)
    pair = swap(theirs, "core")
    dj0, mine = attend_back_call(run, part, da[0], joined0, w_qkv, w_proj, F32)
    come = collect_blocks(run, mine, pair)
    output = run(
        functools.partial(output_kernel, 7), shape((part, width), BF16), middle, *out_come, vec, name="output"
    )
    if one_head:
        g_first = run(
            functools.partial(product_attend_kernel, far),
            shape((far, 4, deep, joint + width // 3), BF16),
            *n1,
            dj0,
            dj1,
            mixed0,
            mixed1,
            *da,
            name="grad_attend",
        )
        g_first = scatter(g_first.reshape(4 * far, deep, -1))
    else:
        g_qkv = scatter(product_call(run, n1, (dj0, dj1), "grad_qkv")).reshape(4, deep, joint)
        g_first = jnp.pad(g_qkv, ((0, 0), (0, 0), (0, width // 3)))
        g_proj = product_call(run, (mixed0, mixed1), da, "grad_proj")
        spot = jnp.zeros((2, per, 4, HEAD_DIM, width), BF16)
        spot = lax.dynamic_update_slice(
            spot, g_proj.reshape(1, per, 1, HEAD_DIM, width), (seq, 0, lo, 0, 0)
        )
        low_own = lax.psum_scatter(
            spot.reshape(width, width), ("far", "near", "core"), scatter_dimension=0, tiled=True
        )
    g_up, g_down = run(
        double_up_kernel,
        (shape((8, deep, far * f), BF16), shape((2, deep, width), BF16)),
        g_rest,
        name="double_up",
    )
    g_up = to_team(g_up)
    down_other = swap(g_down, "seq")
    d_hidden = norm_back_call(run, 2, part, come, hidden, vec, d_middle, False)

    parts = send_own(d_hidden)
    early = run(
        functools.partial(sums_kernel, part, rows), shape((8, width), F32), *da, *d_mlp, name="sums"
    )
    dh = spread_blocks(run, parts)
    g_skip = run(
        functools.partial(vector_kernel, far, deep, part, rows),
        shape((far, k + 8, width), BF16),
        x_turned,
        *dh,
        early,
        s0,
        s1,
        name="grad_skip",
    )
    g_skip = scatter(g_skip.reshape(far * (k + 8), width))
    blocks = tuple(v.reshape(4, rows, width) for v in dh)
    sent = skip_back_call(run, half * k, quarter * k, blocks, w_skip)
    got = lax.all_to_all(sent, TEAM, split_axis=0, concat_axis=0, tiled=True)
    g_qkv, low = run(
        double_qkv_kernel,
        (shape((8, deep, joint), BF16), shape((deep, width), BF16)),
        g_first,
        name="double_qkv",
    )
    g_qkv = to_team(g_qkv)
    if not one_head:
        low = low_own
    low_other = swap(low, "seq")

    order = [(s, j, z * f, f) for z in range(far) for j in range(4) for s in range(2)]
    d_fc1_w = columns_call(run, order, g_up, "whole_up")
    d_inputs, d_skips = unpack_call(run, got, part, half, quarter, k)
    order = [
        (s, j, (b * per + i) * HEAD_DIM, HEAD_DIM)
        for b in range(3)
        for s in range(2)
        for i in range(per)
        for j in range(4)
    ]
    d_qkv_w = columns_call(run, order, g_qkv, "whole_qkv")
    d_fc2_w = run(two_halves_kernel, shape((2 * f, width), F32), g_down, down_other, name="whole_down")
    d_proj_w = run(pair_sum_kernel, shape(low.shape, F32), low, low_other, name="whole_proj")
    d_skip_w, vectors, d_up_b = run(
        functools.partial(last_kernel, k, deep, f),
        (shape((2 * k, width), F32), shape((8, deep), F32), shape((1, 2 * f), F32)),
        g_skip,
        swap(g_skip, "seq"),
        name="whole_skip",
    )
    return (
        output.reshape(1, part, width),
        d_inputs.reshape(1, part, width),
        d_skips.reshape(1, 2 * part, width // 2),
        d_skip_w,
        vectors[0],
        vectors[1],
        vectors[2],
        d_qkv_w,
        d_proj_w,
        vectors[3],
        vectors[4],
        vectors[5],
        d_fc1_w,
        d_up_b.reshape(2 * f),
        d_fc2_w,
        vectors[6],
    )


def solution(mesh):
    dp, seq = mesh.shape["dp"], mesh.shape["seq"]
    far = dp // 4
    fine = Mesh(mesh.devices.reshape(far, 2, 2, seq), ("far", "near", "core", "seq"))
    items = ("far", "near", "core")
    tokens = P(items, "seq", None)
    features = P(items, None, "seq")
    matrix = P(items, None)
    vector = P(items)
    in_specs = (
        tokens,
        features,
        tokens,
        vector,
        P(),
        matrix,
        vector,
        vector,
        vector,
        matrix,
        matrix,
        vector,
        vector,
        vector,
        matrix,
        vector,
        matrix,
        vector,
    )
    out_specs = (
        tokens,
        tokens,
        features,
        matrix,
        vector,
        vector,
        vector,
        matrix,
        matrix,
        vector,
        vector,
        vector,
        matrix,
        vector,
        matrix,
        vector,
    )
    return jax.shard_map(
        functools.partial(body, far=far),
        mesh=fine,
        in_specs=in_specs,
        out_specs=out_specs,
        check_vma=False,
    )
```

```python
import functools

import jax
import jax.numpy as jnp
from jax import lax
from jax.experimental import pallas as pl
from jax.experimental.pallas import tpu as pltpu
from jax.sharding import Mesh, PartitionSpec as P

HEADS = 16
HEAD_DIM = 72
EPS = 1e-05
F32 = jnp.float32
BF16 = jnp.bfloat16
TEAM = ("near", "core", "seq")
WEIGHTS = {"turn": 12, "attend": 12, "grad_mlp": 12, "grad_attend": 12, "down": 20, "sums": 12, "double_up": 20, "skip_half": 8, "pack": 4, "pack_columns": 50, "whole_down": 6, "attend_back1": 3, "norm_back2": 2, "output": 2, "order_skip": 0.5, "merge3": 3, "grad_skip": 0.1, "unpack": 20, "stack4": 0.1, "stack5": 4, "mlp2": 3, "order_columns": 12, "norm_back1": 12, "merge5": 8, "mlp1": 1, "down_part": 0.1}
FLIP2 = [(0, 1), (1, 0)]
FLIP4 = [(0, 3), (1, 2), (2, 1), (3, 0)]


def nn(a, b):
    return lax.dot_general(a, b, (((1,), (0,)), ((), ())), preferred_element_type=F32)


def nt(a, b):
    return lax.dot_general(a, b, (((1,), (1,)), ((), ())), preferred_element_type=F32)


def tn(a, b):
    return lax.dot_general(a, b, (((0,), (0,)), ((), ())), preferred_element_type=F32)


def shape(dims, kind):
    return jax.ShapeDtypeStruct(tuple(dims), kind)


class Line:
    def __init__(self):
        self.word = None
        self.calls = {}

    def __call__(self, kernel, outs, *ops, scratch=(), limit=12, name=None, scalars=()):
        single = not isinstance(outs, tuple)
        outs = (outs,) if single else outs
        spec = pl.BlockSpec(memory_space=pltpu.VMEM)
        n, m = len(ops) + len(scalars), len(outs)
        late = () if self.word is None else (self.word,)
        count = self.calls[name] = self.calls.get(name, 0) + 1
        weight = WEIGHTS.get(f"{name}{count}", WEIGHTS.get(name, 0.1))

        def call(*refs):
            ins, rest = refs[:n], refs[n + len(late) :]
            rest[m][...] = jnp.zeros_like(rest[m])
            kernel(*ins, *rest[:m], *rest[m + 1 :])

        *results, self.word = pl.pallas_call(
            call,
            out_shape=outs + (jax.ShapeDtypeStruct((8, 128), F32),),
            in_specs=[spec] * len(ops)
            + [pl.BlockSpec(memory_space=pltpu.SMEM)] * len(scalars)
            + [pl.BlockSpec(memory_space=pl.ANY)] * len(late),
            out_specs=(spec,) * (m + 1),
            scratch_shapes=list(scratch),
            cost_estimate=pl.CostEstimate(flops=int(weight * 1e9), bytes_accessed=1000, transcendentals=0),
            compiler_params=pltpu.CompilerParams(vmem_limit_bytes=limit * 1024 * 1024),
            name=name,
        )(*ops, *scalars, *late)
        return results[0] if single else tuple(results)


def pack_kernel(half, quarter, k, x_ref, s_ref, out_ref, wide, tall):
    part = x_ref.shape[0]
    x = x_ref[...].astype(F32)
    wide[0 : 2 * part, :] = s_ref[...].astype(F32)
    first, second = wide[0:part, :], wide[part : 2 * part, :]
    tall[part:, :] = jnp.zeros((tall.shape[0] - part, tall.shape[1]), F32)
    for r in range(8):
        pieces = [
            src[:, (j * 8 + r) * k : (j * 8 + r + 1) * k]
            for src, n in ((x, half), (first, quarter), (second, quarter))
            for j in range(n)
        ]
        tall[0:part, :] = jnp.concatenate(pieces, axis=1)
        out_ref[r] = tall[...].astype(BF16)


def pack_call(run, x, s, rows, half, quarter, k):
    deep = 2 * half * k
    return run(
        functools.partial(pack_kernel, half, quarter, k),
        shape((8, rows, deep), BF16),
        x,
        s,
        scratch=[pltpu.VMEM((s.shape[0], s.shape[1]), F32), pltpu.VMEM((rows, deep), F32)],
        name="pack",
    )


def skip_half_kernel(w_ref, *refs):
    *small, out_ref = refs
    k = w_ref.shape[0] // 2
    w = w_ref[...].astype(F32)
    w = jnp.where(lax.axis_index("seq") == 0, w[:k], w[k:])
    line = [ref[...].astype(F32) for ref in small]
    line.append(jnp.zeros((1, w.shape[1] - sum(v.shape[1] for v in line)), F32))
    line = jnp.concatenate(line, axis=1)
    line = jnp.where(lax.broadcasted_iota(jnp.int32, (8, 1), 0) == 0, line, 0.0)
    out_ref[...] = jnp.concatenate((w, line), axis=0).astype(BF16)


def lo_index():
    return lax.axis_index("near") * 2 + lax.axis_index("core")


def choose(at, values):
    out = values[0]
    for i in range(1, len(values)):
        out = jnp.where(at == i, values[i], out)
    return out


def pack_columns_kernel(far, per, joint, f, qkv_ref, up_ref, *outs):
    seq = lax.axis_index("seq")
    lo = lo_index()
    w, up = qkv_ref[...].astype(F32), up_ref[...].astype(F32)
    deep, width = w.shape[0], w.shape[1] // 3
    spare = jnp.zeros((deep, joint - 3 * per * HEAD_DIM), F32)
    blocks = []
    for j in range(4):
        both = []
        for s in range(2):
            heads = [
                w[:, at : at + HEAD_DIM]
                for b in range(3)
                for i in range(per)
                for at in (b * width + ((s * per + i) * 4 + j) * HEAD_DIM,)
            ]
            hidden = [up[:, at : at + f] for z in range(far) for at in (((z * 4 + j) * 2 + s) * f,)]
            both.append(jnp.concatenate(heads + [spare] + hidden, axis=1))
        blocks.append(jnp.where(seq == 0, both[0], both[1]))
    for j, out in enumerate(outs):
        out[...] = choose(lax.bitwise_xor(lo, j), blocks).astype(BF16)


def order_columns_kernel(joint, own, a, b, c, down_ref, proj_ref, qkv_ref, rest_ref):
    lo = lo_index()
    got = [ref[...].astype(F32) for ref in (own, a, b, c)]
    deep = got[0].shape[0]
    blocks = [choose(lax.bitwise_xor(lo, j), got) for j in range(4)]
    third = proj_ref.shape[1] // 3
    for j in range(4):
        qkv_ref[j, :, :joint] = blocks[j][:, :joint].astype(BF16)
        if j < 3:
            qkv_ref[j, :, joint:] = proj_ref[:, j * third : (j + 1) * third]
        else:
            qkv_ref[j, :, joint:] = jnp.zeros((deep, third), BF16)
    down = down_ref[...].astype(F32)
    down = jnp.where(lax.axis_index("seq") == 0, down[: 2 * deep], down[2 * deep :])
    for i in range(2):
        up = jnp.concatenate((blocks[i][:, joint:], blocks[2 + i][:, joint:]), axis=1)
        rest_ref[i] = up.astype(BF16)
        rest_ref[2 + i] = down[i * deep : (i + 1) * deep].astype(BF16)


def split_first_kernel(got_ref, qkv_ref, proj_ref):
    joint = qkv_ref.shape[2]
    third = got_ref.shape[2] - joint
    for g in range(got_ref.shape[0]):
        qkv_ref[g] = got_ref[g, :, :joint]
        if g % 4 < 3:
            proj_ref[g // 4, :, (g % 4) * third : (g % 4 + 1) * third] = got_ref[g, :, joint:]


def split_kernel(far, got_ref, up_ref, down_ref):
    for z in range(far):
        for i in range(2):
            pair = got_ref[4 * z + i].astype(F32)
            n = pair.shape[1] // 2
            up_ref[4 * z + i] = pair[:, :n].astype(BF16)
            up_ref[4 * z + 2 + i] = pair[:, n:].astype(BF16)
            down_ref[2 * z + i] = got_ref[4 * z + 2 + i]


def order_skip_kernel(deep, lo_f, *refs):
    *blocks, w_ref, vec_ref, up_ref = refs
    n = len(blocks)
    k = w_ref.shape[1]
    far, lo, seq = lax.axis_index("far"), lo_index(), lax.axis_index("seq")
    got = [ref[...].astype(F32) for ref in blocks]
    for j, v in enumerate(got):
        w_ref[lax.rem(far - j + n, n)] = v[:k].astype(BF16)
    lines = [choose(lax.rem(far - z + n, n), [v[k : k + 1] for v in got]) for z in range(n)]
    up_ref[...] = jnp.concatenate(
        [jnp.where(seq == 0, v[:, :lo_f], v[:, lo_f : 2 * lo_f]) for v in lines], axis=1
    )
    pieces = []
    for v in lines:
        tall = [v[:, 2 * lo_f + i * deep : 2 * lo_f + (i + 1) * deep] for i in range(7)]
        tall = jnp.concatenate([jnp.zeros_like(tall[0])] + tall, axis=0)
        pieces += [jnp.where((lo == j) & (seq == 0), tall, 0.0) for j in range(4)]
    vec_ref[...] = jnp.concatenate(pieces, axis=1)


def unpack_kernel(half, quarter, k, got_ref, x_ref, s_ref, wide):
    part = x_ref.shape[0]
    got = [got_ref[r, 0:part, :].astype(F32) for r in range(8)]
    x_ref[...] = jnp.concatenate(
        [got[r][:, j * k : (j + 1) * k] for j in range(half) for r in range(8)], axis=1
    ).astype(BF16)
    for t in range(2):
        base = half + t * quarter
        wide[t * part : (t + 1) * part, :] = jnp.concatenate(
            [got[r][:, (base + j) * k : (base + j + 1) * k] for j in range(quarter) for r in range(8)],
            axis=1,
        )
    s_ref[...] = wide[...].astype(BF16)


def unpack_call(run, got, part, half, quarter, k):
    width = 8 * half * k
    return run(
        functools.partial(unpack_kernel, half, quarter, k),
        (shape((part, width), BF16), shape((2 * part, width // 2), BF16)),
        got,
        scratch=[pltpu.VMEM((2 * part, width // 2), F32)],
        name="unpack",
    )


def halves(h, q, a, b):
    zero = jnp.concatenate((a[:, :h], a[:, h : h + q], b[:, h : h + q]), axis=1)
    one = jnp.concatenate((b[:, :h], a[:, h + q :], b[:, h + q :]), axis=1)
    return zero, one


def skip_kernel(side, part, h, q, got_ref, w_ref, vec_ref, x_ref, out_ref):
    near, core, seq = (lax.axis_index(name) for name in TEAM)
    real = lax.broadcasted_iota(jnp.int32, (got_ref.shape[1], 1), 0) < part
    for fn in range(2):
        base = lax.bitwise_xor(near, fn) * 4 + lax.bitwise_xor(core, side) * 2
        zero, one = halves(h, q, got_ref[base].astype(F32), got_ref[base + 1].astype(F32))
        mine = jnp.where(seq == 0, zero, one)
        other = jnp.where(seq == 0, one, zero)
        for i, x in enumerate((mine, other)):
            x = jnp.where(real, x, 0.0).astype(BF16)
            x_ref[2 * fn + i] = x
            out = nn(x, w_ref[...])
            base = out.shape[0] - 8
            out = jnp.concatenate((out[:base], out[base:] + vec_ref[...]), axis=0)
            out_ref[2 * fn + i] = out.astype(out_ref.dtype)


def skip_call(run, side, part, h, q, got, w, vec, kind):
    _, rows, deep = got.shape
    return run(
        functools.partial(skip_kernel, side, part, h, q),
        (shape((4, rows, deep), BF16), shape((4, rows, w.shape[1]), kind)),
        got,
        w,
        vec,
        name="skip",
    )


def turn_kernel(x0_ref, x1_ref, out_ref):
    for i, ref in enumerate((x0_ref, x1_ref)):
        for j in range(4):
            out_ref[4 * i + j] = ref[j].astype(F32).T.astype(BF16)


def skip_back_kernel(h, q, d0_ref, d1_ref, w_ref, out_ref):
    near, core, seq = (lax.axis_index(name) for name in TEAM)
    for side, d_ref in enumerate((d0_ref, d1_ref)):
        for fn in range(2):
            base = lax.bitwise_xor(near, fn) * 4 + lax.bitwise_xor(core, side) * 2
            mine = nt(d_ref[2 * fn], w_ref[...])
            other = nt(d_ref[2 * fn + 1], w_ref[...])
            zero = jnp.where(seq == 0, mine, other)
            one = jnp.where(seq == 0, other, mine)
            out_ref[base] = jnp.concatenate(
                (zero[:, :h], zero[:, h : h + q], one[:, h : h + q]), axis=1
            ).astype(BF16)
            out_ref[base + 1] = jnp.concatenate(
                (one[:, :h], zero[:, h + q :], one[:, h + q :]), axis=1
            ).astype(BF16)


def skip_back_call(run, h, q, dh, w):
    rows = dh[0].shape[1]
    return run(
        functools.partial(skip_back_kernel, h, q),
        shape((8, rows, w.shape[0]), BF16),
        dh[0],
        dh[1],
        w,
        name="skip_back",
    )


def merge_kernel(mine_ref, got_ref, own_ref, *outs):
    own_ref[...] = mine_ref[0] + got_ref[0].astype(F32)
    for i, out in enumerate(outs):
        out[...] = (mine_ref[i + 1] + got_ref[i + 1].astype(F32)).astype(BF16)


def stack_kernel(a, b, c, d, out_ref):
    for i, ref in enumerate((a, b, c, d)):
        out_ref[i] = ref[...]


def arrived(own_ref, others):
    total = own_ref[...]
    for ref in others:
        total = total + ref[...].astype(F32)
    return total


def normalized(total, gain, shift):
    center = total - jnp.mean(total, axis=-1, keepdims=True)
    spread = jnp.mean(center * center, axis=-1, keepdims=True)
    return (center * lax.rsqrt(spread + EPS) * gain + shift).astype(BF16)


def norm_first_kernel(own, b, c, d, total_ref, normed_ref, vec_ref):
    total = arrived(own, (b, c, d))
    vec_ref[...] = total[total.shape[0] - 8 :]
    bias, gain, shift = (vec_ref[i : i + 1, :] for i in (1, 2, 3))
    total = total + bias
    total_ref[...] = total
    normed_ref[...] = normalized(total, gain, shift)


def norm_second_kernel(base, own, b, c, d, vec_ref, total_ref, normed_ref):
    bias, gain, shift = (vec_ref[i : i + 1, :] for i in (4, 5, 6))
    total = arrived(own, (b, c, d)) + bias + base[...]
    total_ref[...] = total
    normed_ref[...] = normalized(total, gain, shift)


def norm_back_kernel(place, part, own, b, c, d, total_ref, vec_ref, resid, wide_ref, low_ref):
    grad = arrived(own, (b, c, d))
    gain = vec_ref[place : place + 1, :]
    center = total_ref[...] - jnp.mean(total_ref[...], axis=-1, keepdims=True)
    spread = jnp.mean(center * center, axis=-1, keepdims=True)
    scale = lax.rsqrt(spread + EPS)
    unit = center * scale
    inner = grad * gain
    back = inner - jnp.mean(inner, axis=-1, keepdims=True)
    back = (back - unit * jnp.mean(inner * unit, axis=-1, keepdims=True)) * scale
    wide = resid[...] + back
    if wide_ref is not None:
        wide_ref[...] = wide
    d_gain = jnp.sum(grad * unit, axis=0, keepdims=True)
    d_shift = jnp.sum(grad, axis=0, keepdims=True)
    row = lax.broadcasted_iota(jnp.int32, (wide.shape[0], 1), 0)
    wide = jnp.where(row < part, wide, 0.0)
    for i, v in enumerate((d_gain, d_shift)):
        high = v.astype(BF16).astype(F32)
        wide = jnp.where(row == part + 2 * i, high, wide)
        wide = jnp.where(row == part + 2 * i + 1, v - high, wide)
    low_ref[...] = wide.astype(BF16)


def norm_back_last(place, part, own, b, c, d, total, vec, resid, low_ref):
    norm_back_kernel(place, part, own, b, c, d, total, vec, resid, None, low_ref)


def norm_back_call(run, place, part, parts, total, vec, resid, both):
    low = shape(total.shape, BF16)
    body = functools.partial(norm_back_kernel if both else norm_back_last, place, part)
    outs = (shape(total.shape, F32), low) if both else low
    return run(body, outs, *parts, total, vec, resid, name="norm_back")


def cot_kernel(cot_ref, bins_ref, weights_ref, wide_ref, low_ref):
    part = cot_ref.shape[0]
    wide_ref[...] = jnp.zeros_like(wide_ref)
    wide_ref[0:part, :] = cot_ref[...].astype(F32) * weights_ref[bins_ref[0]]
    low_ref[...] = wide_ref[...].astype(BF16)


def token_place(rows):
    place = lax.broadcasted_iota(jnp.int32, (2 * rows, 1), 0)
    return jnp.where(place >= rows, place - rows, place)


def head_masks(width):
    lane = lax.broadcasted_iota(jnp.int32, (1, width), 1)
    return [
        jnp.where((lane >= i * HEAD_DIM) & (lane < (i + 1) * HEAD_DIM), 1.0, 0.0).astype(BF16)
        for i in range(width // HEAD_DIM)
    ]


def probs_of(k, q, bias):
    scores = nt(k, q) * (HEAD_DIM**-0.5) + bias
    expo = jnp.exp(scores - jnp.max(scores, axis=0, keepdims=True))
    return expo * (1.0 / jnp.sum(expo, axis=0, keepdims=True))


def split3(v, width):
    return (v[:, i * width : (i + 1) * width] for i in range(3))


def attend_kernel(part, x_ref, qkv_ref, proj_ref, joined_ref, mixed_ref, out_ref):
    rows = out_ref.shape[1]
    seq = lax.axis_index("seq") if proj_ref.shape[0] > 1 else 0
    real = token_place(rows) < part
    bias = jnp.where(real, 0.0, -1e30).astype(F32)

    @pl.loop(0, x_ref.shape[0])
    def _(item):
        joined = nn(x_ref[item], qkv_ref[...]).astype(BF16)
        joined_ref[item] = joined
        q, k, v = split3(joined, mixed_ref.shape[2])
        mixed = None
        for mask in head_masks(q.shape[1]):
            probs = probs_of(k, q * mask, bias).astype(BF16)
            term = tn(probs, v * mask)
            mixed = term if mixed is None else mixed + term
        mixed = jnp.where(real, mixed, 0.0).astype(BF16)
        mixed_ref[item] = mixed
        out = nn(mixed, proj_ref[seq])
        out_ref[2 * item] = out[:rows].astype(out_ref.dtype)
        out_ref[2 * item + 1] = out[rows:].astype(out_ref.dtype)


def attend_call(run, part, x, w_qkv, w_proj, kind):
    items, rows, width = x.shape
    inner = w_proj.shape[1]
    return run(
        functools.partial(attend_kernel, part),
        (
            shape((items, rows, w_qkv.shape[1]), BF16),
            shape((items, rows, inner), BF16),
            shape((2 * items, rows // 2, width), kind),
        ),
        x,
        w_qkv,
        w_proj,
        name="attend",
    )


def attend_back_kernel(part, d_ref, joined_ref, qkv_ref, proj_ref, grads_ref, out_ref):
    rows = out_ref.shape[1]
    real = token_place(rows) < part
    bias = jnp.where(real, 0.0, -1e30).astype(F32)
    factor = HEAD_DIM**-0.5
    seq = lax.axis_index("seq") if proj_ref.shape[0] > 1 else 0

    @pl.loop(0, d_ref.shape[0])
    def _(item):
        d_mixed = nt(d_ref[item], proj_ref[seq])
        d_mixed = jnp.where(real, d_mixed, 0.0).astype(BF16)
        q, k, v = split3(joined_ref[item], proj_ref.shape[1])
        d_q = d_k = d_v = 0.0
        for mask in head_masks(q.shape[1]):
            probs = probs_of(k, q * mask, bias)
            d_one = d_mixed * mask
            d_v = d_v + nn(probs.astype(BF16), d_one)
            d_probs = nt(v, d_one)
            inner = jnp.sum(d_probs * probs, axis=0, keepdims=True)
            d_scores = (probs * (d_probs - inner)).astype(BF16)
            d_k = d_k + nn(d_scores, q * mask)
            d_q = d_q + tn(d_scores, k * mask)
        spare = jnp.zeros((2 * rows, grads_ref.shape[2] - 3 * d_v.shape[1]), F32)
        grads = jnp.concatenate((d_q * factor, d_k * factor, d_v, spare), axis=1).astype(BF16)
        grads_ref[item] = grads
        out = nt(grads, qkv_ref[...])
        out_ref[2 * item] = out[:rows].astype(out_ref.dtype)
        out_ref[2 * item + 1] = out[rows:].astype(out_ref.dtype)


def attend_back_call(run, part, d, joined, w_qkv, w_proj, kind):
    items, rows, width = d.shape
    return run(
        functools.partial(attend_back_kernel, part),
        (shape(joined.shape, BF16), shape((2 * items, rows // 2, width), kind)),
        d,
        joined,
        w_qkv,
        w_proj,
        name="attend_back",
    )


def mlp_kernel(x_ref, d_ref, up_ref, bias_ref, down_ref, act_ref, grad_ref, sum_ref, out_ref):
    rows = out_ref.shape[1]
    sum_ref[...] = jnp.zeros_like(sum_ref)

    @pl.loop(0, x_ref.shape[0])
    def _(item):
        upper = nn(x_ref[item], up_ref[...]) + bias_ref[...]
        bell = 0.5 * (1.0 + lax.erf(upper * (0.5**0.5)))
        act_ref[item] = (upper * bell).astype(BF16)
        slope = bell + upper * jnp.exp(-0.5 * upper * upper) * 0.3989422804014327
        d_upper = (slope * nt(d_ref[item], down_ref[...])).astype(BF16)
        grad_ref[item] = d_upper
        sum_ref[...] += jnp.sum(d_upper.astype(F32), axis=0, keepdims=True)
        out = nt(d_upper, up_ref[...])
        out_ref[2 * item] = out[:rows].astype(out_ref.dtype)
        out_ref[2 * item + 1] = out[rows:].astype(out_ref.dtype)


def mlp_call(run, x, d, w_up, b_up, w_down, kind):
    items, rows, width = x.shape
    inner = w_up.shape[1]
    return run(
        mlp_kernel,
        (
            shape((items, rows, inner), BF16),
            shape((items, rows, inner), BF16),
            shape((1, inner), F32),
            shape((2 * items, rows // 2, width), kind),
        ),
        x,
        d,
        w_up,
        b_up,
        w_down,
        name="mlp",
    )


def down_kernel(act_ref, w_ref, out_ref):
    rows = out_ref.shape[1]

    @pl.loop(0, act_ref.shape[0])
    def _(item):
        out = nn(act_ref[item], w_ref[...])
        out_ref[2 * item] = out[:rows].astype(out_ref.dtype)
        out_ref[2 * item + 1] = out[rows:].astype(out_ref.dtype)


def down_call(run, act, w, kind):
    items, rows, _ = act.shape
    dims = (2 * items, rows // 2, w.shape[1])
    return run(down_kernel, shape(dims, kind), act, w, name="down")


def output_kernel(place, base, own, b, c, d, vec_ref, out_ref):
    total = base[...] + arrived(own, (b, c, d)) + vec_ref[place : place + 1, :]
    out_ref[...] = total[: out_ref.shape[0]].astype(BF16)


def product_kernel(*refs):
    *sides, out_ref = refs
    total = 0.0
    n = len(sides) // 2
    for left, right in zip(sides[:n], sides[n:]):
        for item in range(left.shape[0]):
            total = total + tn(left[item], right[item])
    out_ref[...] = total.astype(BF16)


def product_call(run, left, right, name):
    dims = (left[0].shape[-1], right[0].shape[-1])
    return run(product_kernel, shape(dims, BF16), *left, *right, name=name)


def product_two_kernel(far, n20, n21, du0, du1, act0, act1, dm0, dm1, out_ref):
    def product(pairs):
        total = 0.0
        for left, right in pairs:
            for item in range(2):
                total = total + tn(left[item], right[item])
        return total

    deep = out_ref.shape[2]
    down = product(((act0, dm0), (act1, dm1)))
    for z in range(far):
        for i in range(2):
            at = (2 * z + i) * deep
            out_ref[z, 2 + i] = down[at : at + deep].astype(BF16)
    up = product(((n20, du0), (n21, du1)))
    for z in range(far):
        for i in range(2):
            at = (4 * z + i) * deep
            pair = (up[at : at + deep], up[at + 2 * deep : at + 3 * deep])
            out_ref[z, i] = jnp.concatenate(pair, axis=1).astype(BF16)


def product_attend_kernel(far, n10, n11, dj0, dj1, a0, a1, d0, d1, out_ref):
    def product(pairs):
        total = 0.0
        for left, right in pairs:
            for item in range(2):
                total = total + tn(left[item], right[item])
        return total

    deep, joint = out_ref.shape[2], dj0.shape[2]
    third = out_ref.shape[3] - joint
    qkv = product(((n10, dj0), (n11, dj1)))
    for z in range(far):
        for j in range(4):
            at = (4 * z + j) * deep
            out_ref[z, j, :, :joint] = qkv[at : at + deep].astype(BF16)
    proj = product(((a0, d0), (a1, d1)))
    seq = lax.axis_index("seq")
    for z in range(far):
        at = z % 2 * deep
        rows = jnp.where(seq == z // 2, proj[at : at + deep], 0.0).astype(BF16)
        for j in range(4):
            cut = rows[:, j * third : (j + 1) * third] if j < 3 else jnp.zeros((deep, third), BF16)
            out_ref[z, j, :, joint:] = cut


def double_up_kernel(got_ref, up_ref, down_ref):
    n = up_ref.shape[2]
    for j in range(4):
        v = got_ref[j % 2].astype(F32)[:, (j // 2) * n : (j // 2 + 1) * n].astype(BF16)
        up_ref[2 * j] = v
        up_ref[2 * j + 1] = v
    for i in range(2):
        down_ref[i] = got_ref[2 + i]


def double_qkv_kernel(got_ref, qkv_ref, proj_ref):
    joint = qkv_ref.shape[2]
    third = got_ref.shape[2] - joint
    for j in range(4):
        v = got_ref[j, :, :joint]
        qkv_ref[2 * j] = v
        qkv_ref[2 * j + 1] = v
        if j < 3:
            proj_ref[:, j * third : (j + 1) * third] = got_ref[j, :, joint:]


def pair_sum_kernel(a_ref, b_ref, out_ref):
    out_ref[...] = a_ref[...].astype(F32) + b_ref[...].astype(F32)


def sums_kernel(part, rows, da0, da1, dm0, dm1, out_ref):
    lines = block_sums(part, rows, (da0, da1), True) + block_sums(part, rows, (dm0, dm1), False)
    out_ref[...] = jnp.concatenate(lines + [jnp.zeros((4, da0.shape[-1]), F32)], axis=0)


def block_sums(part, rows, refs, extra):
    place = token_place(rows)
    sums = [0.0, 0.0, 0.0]
    for ref in refs:
        for item in range(2):
            v = ref[item].astype(F32)
            sums[0] = sums[0] + jnp.sum(jnp.where(place < part, v, 0.0), axis=0, keepdims=True)
            if extra:
                for i in range(2):
                    at = (place == part + 2 * i) | (place == part + 2 * i + 1)
                    sums[1 + i] = sums[1 + i] + jnp.sum(jnp.where(at, v, 0.0), axis=0, keepdims=True)
    return sums if extra else sums[:1]


def vector_kernel(far, deep, part, rows, xt_ref, dh0, dh1, sums_ref, s0, s1, out_ref):
    lo = lax.axis_index("near") * 2 + lax.axis_index("core")
    width = dh0.shape[-1]
    total = 0.0
    for side, ref in enumerate((dh0, dh1)):
        for item in range(2):
            d = ref[item]
            for i in range(2):
                total = total + nn(xt_ref[4 * side + 2 * item + i], d[i * rows : (i + 1) * rows])
    k = total.shape[0] // far
    lines = block_sums(part, rows, (dh0, dh1), True)
    stacked = jnp.concatenate(lines + [sums_ref[i : i + 1, :] for i in range(5)], axis=0)
    up = s0[...] + s1[...]
    f = up.shape[1] // far
    spare = jnp.zeros((8, width - 2 * f), F32)
    row = lax.broadcasted_iota(jnp.int32, (8, 1), 0)
    for z in range(far):
        cut = 0.0
        for j in range(4):
            at = (z * 4 + j) * deep
            cut = cut + jnp.where(lo == j, stacked[:, at : at + deep], 0.0)
        low = jnp.concatenate((cut, jnp.zeros((8, 2 * f - deep), F32)), axis=1)
        tall = jnp.concatenate((up[:, z * f : (z + 1) * f], jnp.zeros((1, f), F32)), axis=1)
        low = jnp.where(row == 7, tall, low)
        low = jnp.concatenate((low, spare), axis=1)
        out_ref[z] = jnp.concatenate((total[z * k : (z + 1) * k], low), axis=0).astype(BF16)


def two_halves_kernel(mine_ref, other_ref, out_ref):
    seq = lax.axis_index("seq")
    k = mine_ref.shape[1]
    for i in range(2):
        mine, other = mine_ref[i].astype(F32), other_ref[i].astype(F32)
        out_ref[i * k : (i + 1) * k, :] = jnp.where(seq == 0, mine, other)
        out_ref[(2 + i) * k : (3 + i) * k, :] = jnp.where(seq == 0, other, mine)


def last_kernel(k, deep, f, mine_ref, other_ref, out_ref, up_ref, *vec_refs):
    seq = lax.axis_index("seq")
    mine, other = mine_ref[...].astype(F32), other_ref[...].astype(F32)
    zero = jnp.where(seq == 0, mine, other)
    one = jnp.where(seq == 0, other, mine)
    out_ref[0:k, :] = zero[:k]
    out_ref[k : 2 * k, :] = one[:k]
    for i, ref in enumerate(vec_refs):
        ref[...] = mine[k + i, :deep]
    up_ref[...] = jnp.concatenate((zero[k + 7 : k + 8, :f], one[k + 7 : k + 8, :f]), axis=1)[0]


def columns_kernel(order, got_ref, out_ref):
    got = [got_ref[i].astype(F32) for i in range(8)]
    out_ref[...] = jnp.concatenate([got[2 * lo + s][:, at : at + n] for s, lo, at, n in order], axis=1)


def columns_call(run, order, got, name):
    wide = sum(n for *_, n in order)
    return run(functools.partial(columns_kernel, order), shape((got.shape[1], wide), F32), got, name=name)


def swap(v, *axes):
    return lax.ppermute(v, axes if len(axes) > 1 else axes[0], FLIP4 if len(axes) > 1 else FLIP2)


def send_own(own):
    return own, swap(own, "seq"), swap(own, "near"), swap(own, "near", "seq")


def spread_blocks(run, parts):
    rows, width = parts[0].shape
    quad = run(stack_kernel, shape((4, rows, width), BF16), *parts, name="stack")
    other = swap(quad, "core")
    return quad.reshape(2, 2 * rows, width), other.reshape(2, 2 * rows, width)


def collect_blocks(run, mine, got):
    dims = mine.shape[1:]
    outs = (shape(dims, F32),) + (shape(dims, BF16),) * 3
    own, b, c, d = run(merge_kernel, outs, mine, got, name="merge")
    return own, swap(b, "seq"), swap(c, "near"), swap(d, "near", "seq")


def from_far(v, far):
    return [v] + [lax.ppermute(v, "far", [(i, (i + j) % far) for i in range(far)]) for j in range(1, far)]


def to_far(blocks, far):
    return [blocks[0]] + [
        lax.ppermute(blocks[j], "far", [(i, (i + j) % far) for i in range(far)]) for j in range(1, far)
    ]


def gather_far(v):
    return lax.all_gather(v, "far", axis=0, tiled=False)


def pick(v, at, axis):
    return lax.dynamic_index_in_dim(v, at, axis, keepdims=False)


def body(
    inputs,
    skips,
    cotangent,
    bins,
    bin_weights,
    skip_w,
    skip_b,
    ln1_g,
    ln1_b,
    qkv_w,
    proj_w,
    proj_b,
    ln2_g,
    ln2_b,
    fc1_w,
    fc1_b,
    fc2_w,
    fc2_b,
    *,
    far,
):
    _, part, width = inputs.shape
    rows = -(-part // 8) * 8
    dp = far * 4
    seq = lax.axis_index("seq")
    lo = lax.axis_index("near") * 2 + lax.axis_index("core")
    per = HEADS // 8
    inner = per * HEAD_DIM
    joint = -(-3 * inner // 128) * 128
    deep = width // dp
    k = skip_w.shape[0] // 2
    f = fc2_w.shape[0] // 2
    half, quarter = far // 2, far // 4
    spread = far * k
    one_head = dp == HEADS

    run = Line()

    sent = pack_call(run, inputs[0], skips[0], rows, half, quarter, k)
    got = lax.all_to_all(sent, TEAM, split_axis=0, concat_axis=0, tiled=True)
    small = tuple(v.reshape(1, -1) for v in (fc1_b, skip_b, ln1_g, ln1_b, proj_b, ln2_g, ln2_b, fc2_b))
    skip_half = run(
        skip_half_kernel, shape((k + 8, width), BF16), skip_w, *small, name="skip_half"
    )
    skip_blocks = from_far(skip_half, far)
    columns = run(
        functools.partial(pack_columns_kernel, far, per, joint, f),
        (shape((deep, joint + far * f), BF16),) * 4,
        qkv_w,
        fc1_w,
        name="pack_columns",
    )
    columns = (columns[0], swap(columns[1], "core"), swap(columns[2], "near"), swap(columns[3], "near", "core"))
    qkv_part, rest = run(
        functools.partial(order_columns_kernel, joint),
        (shape((4, deep, joint + width // 3), BF16), shape((4, deep, width), BF16)),
        *columns,
        fc2_w,
        proj_w,
        name="order_columns",
    )
    first = gather_far(qkv_part).reshape(dp, deep, joint + width // 3)
    rest = gather_far(rest).reshape(4 * far, deep, width)
    w_skip, vec, b_up = run(
        functools.partial(order_skip_kernel, deep, f),
        (shape((far, k, width), BF16), shape((8, width), F32), shape((1, far * f), F32)),
        *skip_blocks,
        name="order_skip",
    )
    w_skip = w_skip.reshape(spread, width)

    x1, theirs = skip_call(run, 1, part, half * k, quarter * k, got, w_skip, vec, BF16)
    pair = swap(theirs, "core")
    x0, mine = skip_call(run, 0, part, half * k, quarter * k, got, w_skip, vec, F32)
    come = collect_blocks(run, mine, pair)
    x_turned = run(turn_kernel, shape((8, spread, rows), BF16), x0, x1, name="turn")
    d_wide, d_own = run(
        cot_kernel,
        (shape((rows, width), F32), shape((rows, width), BF16)),
        cotangent[0],
        name="cot",
        scalars=(bins, bin_weights),
    )
    hidden, normed, vec = run(
        norm_first_kernel,
        (shape((rows, width), F32), shape((rows, width), BF16), shape((8, width), F32)),
        *come,
        name="norm",
    )

    parts = send_own(normed)
    n1 = spread_blocks(run, parts)
    w_qkv, w_proj = run(
        split_first_kernel,
        (shape((dp, deep, joint), BF16), shape((far, deep, width), BF16)),
        first,
        name="split_first",
    )
    w_qkv = w_qkv.reshape(width, joint)
    if one_head:
        w_proj = w_proj.reshape(2, inner, width)
    else:
        w_proj = lax.all_gather(proj_w, ("far", "near", "core"), axis=0, tiled=True)
        w_proj = pick(w_proj.reshape(2, per, 4, HEAD_DIM, width), seq, 0)
        w_proj = pick(w_proj, lo, 1).reshape(1, inner, width)
    joined1, mixed1, theirs = attend_call(run, part, n1[1], w_qkv, w_proj, BF16)
    pair = swap(theirs, "core")
    d_parts = send_own(d_own)
    joined0, mixed0, mine = attend_call(run, part, n1[0], w_qkv, w_proj, F32)
    come = collect_blocks(run, mine, pair)
    d_mlp = spread_blocks(run, d_parts)
    middle, second = run(
        norm_second_kernel,
        (shape((rows, width), F32), shape((rows, width), BF16)),
        hidden,
        *come,
        vec,
        name="norm",
    )

    parts = send_own(second)
    w_up, w_down = run(
        functools.partial(split_kernel, far),
        (shape((4 * far, deep, far * f), BF16), shape((2 * far, deep, width), BF16)),
        rest,
        name="split",
    )
    w_up, w_down = w_up.reshape(width, far * f), w_down.reshape(far * f, width)
    n2 = spread_blocks(run, parts)
    act1, du1, s1, theirs = mlp_call(run, n2[1], d_mlp[1], w_up, b_up, w_down, BF16)
    pair = swap(theirs, "core")
    act0, du0, s0, mine = mlp_call(run, n2[0], d_mlp[0], w_up, b_up, w_down, F32)
    come = collect_blocks(run, mine, pair)

    def scatter(v):
        return lax.psum_scatter(v, "far", scatter_dimension=0, tiled=True)

    def to_team(v):
        return lax.all_to_all(v, TEAM, split_axis=0, concat_axis=0, tiled=True)

    g_rest = run(
        functools.partial(product_two_kernel, far),
        shape((far, 4, deep, width), BF16),
        *n2,
        du0,
        du1,
        act0,
        act1,
        *d_mlp,
        name="grad_mlp",
    )
    g_rest = scatter(g_rest.reshape(4 * far, deep, width))
    d_middle, d_branch = norm_back_call(run, 5, part, come, middle, vec, d_wide, True)

    parts = send_own(d_branch)
    out_pair = swap(down_call(run, act1, w_down, BF16), "core")
    out_mine = down_call(run, act0, w_down, F32)
    da = spread_blocks(run, parts)
    out_come = collect_blocks(run, out_mine, out_pair)
    dj1, theirs = attend_back_call(run, part, da[1], joined1, w_qkv, w_proj, BF16)
    pair = swap(theirs, "core")
    dj0, mine = attend_back_call(run, part, da[0], joined0, w_qkv, w_proj, F32)
    come = collect_blocks(run, mine, pair)
    output = run(
        functools.partial(output_kernel, 7), shape((part, width), BF16), middle, *out_come, vec, name="output"
    )
    if one_head:
        g_first = run(
            functools.partial(product_attend_kernel, far),
            shape((far, 4, deep, joint + width // 3), BF16),
            *n1,
            dj0,
            dj1,
            mixed0,
            mixed1,
            *da,
            name="grad_attend",
        )
        g_first = scatter(g_first.reshape(4 * far, deep, -1))
    else:
        g_qkv = scatter(product_call(run, n1, (dj0, dj1), "grad_qkv")).reshape(4, deep, joint)
        g_first = jnp.pad(g_qkv, ((0, 0), (0, 0), (0, width // 3)))
        g_proj = product_call(run, (mixed0, mixed1), da, "grad_proj")
        spot = jnp.zeros((2, per, 4, HEAD_DIM, width), BF16)
        spot = lax.dynamic_update_slice(
            spot, g_proj.reshape(1, per, 1, HEAD_DIM, width), (seq, 0, lo, 0, 0)
        )
        low_own = lax.psum_scatter(
            spot.reshape(width, width), ("far", "near", "core"), scatter_dimension=0, tiled=True
        )
    g_up, g_down = run(
        double_up_kernel,
        (shape((8, deep, far * f), BF16), shape((2, deep, width), BF16)),
        g_rest,
        name="double_up",
    )
    g_up = to_team(g_up)
    down_other = swap(g_down, "seq")
    d_hidden = norm_back_call(run, 2, part, come, hidden, vec, d_middle, False)

    parts = send_own(d_hidden)
    early = run(
        functools.partial(sums_kernel, part, rows), shape((8, width), F32), *da, *d_mlp, name="sums"
    )
    dh = spread_blocks(run, parts)
    g_skip = run(
        functools.partial(vector_kernel, far, deep, part, rows),
        shape((far, k + 8, width), BF16),
        x_turned,
        *dh,
        early,
        s0,
        s1,
        name="grad_skip",
    )
    g_skip = scatter(g_skip.reshape(far * (k + 8), width))
    blocks = tuple(v.reshape(4, rows, width) for v in dh)
    sent = skip_back_call(run, half * k, quarter * k, blocks, w_skip)
    got = lax.all_to_all(sent, TEAM, split_axis=0, concat_axis=0, tiled=True)
    g_qkv, low = run(
        double_qkv_kernel,
        (shape((8, deep, joint), BF16), shape((deep, width), BF16)),
        g_first,
        name="double_qkv",
    )
    g_qkv = to_team(g_qkv)
    if not one_head:
        low = low_own
    low_other = swap(low, "seq")

    order = [(s, j, z * f, f) for z in range(far) for j in range(4) for s in range(2)]
    d_fc1_w = columns_call(run, order, g_up, "whole_up")
    d_inputs, d_skips = unpack_call(run, got, part, half, quarter, k)
    order = [
        (s, j, (b * per + i) * HEAD_DIM, HEAD_DIM)
        for b in range(3)
        for s in range(2)
        for i in range(per)
        for j in range(4)
    ]
    d_qkv_w = columns_call(run, order, g_qkv, "whole_qkv")
    d_fc2_w = run(two_halves_kernel, shape((2 * f, width), F32), g_down, down_other, name="whole_down")
    d_proj_w = run(pair_sum_kernel, shape(low.shape, F32), low, low_other, name="whole_proj")
    d_skip_w, d_up_b, *vectors = run(
        functools.partial(last_kernel, k, deep, f),
        (shape((2 * k, width), F32), shape((2 * f,), F32)) + (shape((deep,), F32),) * 7,
        g_skip,
        swap(g_skip, "seq"),
        name="whole_skip",
    )
    return (
        output.reshape(1, part, width),
        d_inputs.reshape(1, part, width),
        d_skips.reshape(1, 2 * part, width // 2),
        d_skip_w,
        vectors[0],
        vectors[1],
        vectors[2],
        d_qkv_w,
        d_proj_w,
        vectors[3],
        vectors[4],
        vectors[5],
        d_fc1_w,
        d_up_b,
        d_fc2_w,
        vectors[6],
    )


def solution(mesh):
    dp, seq = mesh.shape["dp"], mesh.shape["seq"]
    far = dp // 4
    fine = Mesh(mesh.devices.reshape(far, 2, 2, seq), ("far", "near", "core", "seq"))
    items = ("far", "near", "core")
    tokens = P(items, "seq", None)
    features = P(items, None, "seq")
    matrix = P(items, None)
    vector = P(items)
    in_specs = (
        tokens,
        features,
        tokens,
        vector,
        P(),
        matrix,
        vector,
        vector,
        vector,
        matrix,
        matrix,
        vector,
        vector,
        vector,
        matrix,
        vector,
        matrix,
        vector,
    )
    out_specs = (
        tokens,
        tokens,
        features,
        matrix,
        vector,
        vector,
        vector,
        matrix,
        matrix,
        vector,
        vector,
        vector,
        matrix,
        vector,
        matrix,
        vector,
    )
    return jax.shard_map(
        functools.partial(body, far=far),
        mesh=fine,
        in_specs=in_specs,
        out_specs=out_specs,
        check_vma=False,
    )
```
